32 devices in a mesh: section: 2 (over x), seq: 16 (over z, y, core).
Axes of the slice: x: 2, y: 2, z: 4, core: 2. Of those that a mesh axis runs over, the one named last changes fastest.
Arguments:
- cotangent: bfloat16 [2048, 4096], P('seq'), may hold values from -6 to 6
- in_gate: bfloat16 [2, 2048, 4096], P('section', 'seq'), may hold values from -4 to 4
- mid_gate: bfloat16 [2, 2048, 4096], P('section', 'seq'), may hold values from -4 to 4
- layer_inputs: bfloat16 [2, 2048, 4096], P('section', 'seq'), may hold values from -6 to 6
- filters: bfloat16 [2, 128, 256], P('section'), may hold values from -0.5 to 0.5
- steer_second: float32 [2, 4096], P('section', 'seq'), may hold values from 2048 to 32768
- filter_second: float32 [2, 128, 256], P('section', None, 'seq'), may hold values from 8192 to 131072
Outputs:
- steer_step: float32 [2, 4096], P('section', 'seq')
- filter_step: float32 [2, 128, 256], P('section', None, 'seq')
The draws below stay inside these ranges and needn't reach their ends.
All inputs are finite; a program needn't handle non-finite values.
Results may differ from the reference program's by a relative error of at most 0.0095.
Values may be sent and summed in bfloat16 or wider, within the bound.
No kernel may reach another device: no remote copies, remote signals or barrier semaphores. Data moves between devices by JAX's collectives and lax.ppermute only.
A program may use at most 192 MiB of HBM per device.

```python
import math
import jax
import jax.numpy as jnp
from jax import lax

CHANNELS = 4096
GROUPS = 256
FILTER_LEN = 128
TOKENS = 2048
SECTIONS = 2


def block_scale(key, extent, cuts, least, largest):
    factor_of = 1.0
    for axis_at, shards_of in cuts:
        draws = jax.random.uniform(jax.random.fold_in(jax.random.fold_in(key, 6), axis_at), (shards_of,), jnp.float32, least / len(cuts), largest / len(cuts))
        factor_of = factor_of * jnp.repeat(jnp.exp(draws), extent[axis_at] // shards_of).reshape((-1,) + (1,) * (len(extent) - 1 - axis_at))
    return factor_of


def gaussian(own_key, extent, spread, reach, cuts=(), kind=jnp.bfloat16):
    level = block_scale(own_key, extent, cuts, -0.22, 0.18) if cuts else 1.0
    array = jax.random.normal(own_key, extent, jnp.float32) * spread * level
    return jnp.minimum(jnp.maximum(array, -reach), reach).astype(kind)


def setup_inputs(seed: int = 0) -> dict:
    key_of = jax.random.split(jax.random.key(seed), 8)
    return {
        "cotangent": gaussian(key_of[0], (TOKENS, CHANNELS), 1.0, 6.0, ((0, 16),)),
        "in_gate": gaussian(key_of[1], (SECTIONS, TOKENS, CHANNELS), 0.7, 4.0, ((0, 2), (1, 16))),
        "mid_gate": gaussian(key_of[2], (SECTIONS, TOKENS, CHANNELS), 0.7, 4.0, ((0, 2), (1, 16))),
        "layer_inputs": gaussian(key_of[3], (SECTIONS, TOKENS, CHANNELS), 1.0, 6.0, ((0, 2), (1, 16))),
        "filters": gaussian(key_of[4], (SECTIONS, FILTER_LEN, GROUPS), FILTER_LEN ** -0.5, 0.5, ((0, 2),)),
        "steer_second": jnp.clip(jnp.exp(math.log(32768.0) - 2.7725887 * jax.random.uniform(key_of[5], (SECTIONS, CHANNELS), jnp.float32) ** block_scale(key_of[5], (SECTIONS, CHANNELS), ((0, 2), (1, 16)), -0.2, 0.2)), 2048.0, 32768.0),
        "filter_second": jnp.clip(jnp.exp(math.log(131072.0) - 2.7725887 * jax.random.uniform(key_of[6], (SECTIONS, FILTER_LEN, GROUPS), jnp.float32) ** block_scale(key_of[6], (SECTIONS, FILTER_LEN, GROUPS), ((0, 2), (2, 16)), -0.2, 0.2)), 8192.0, 131072.0),
    }


def band_matrix(kernel, block_rows):
    filt_len, group_count = kernel.shape
    span_len = block_rows + filt_len
    padded = jnp.concatenate([kernel.T, jnp.zeros((group_count, block_rows + 1), kernel.dtype)], 1)
    tiled_rows = jnp.tile(padded, (1, block_rows))[:, :block_rows * span_len]
    return tiled_rows.reshape(group_count, block_rows, span_len)

def filter_rows(band_full, extended, row_count, filt_len, block_rows):
    group_count = band_full.shape[0]
    channel_count = extended.shape[1]
    group_size = channel_count // group_count
    block_count = row_count // block_rows
    summed = jnp.zeros((block_count, block_rows, group_count, group_size), jnp.float32)
    for part_index in range(filt_len // block_rows + 1):
        start = part_index * block_rows
        window_part = extended[start:start + row_count].astype(jnp.float32).reshape(block_count, block_rows, group_count, group_size)
        band_part = band_full[:, :, start:start + block_rows].astype(jnp.float32)
        summed = summed + jnp.einsum('grs,bsgc->brgc', band_part, window_part, precision=lax.Precision.HIGHEST)
    return summed.reshape(row_count, channel_count)

def filter_grad(extended, values, group_count, filt_len, block_rows):
    row_count, channel_count = values.shape
    group_size = channel_count // group_count
    block_count = row_count // block_rows
    span_len = block_rows + filt_len
    left_side = values.astype(jnp.float32).reshape(block_count, block_rows, group_count, group_size)
    pieces = []
    for part_index in range(filt_len // block_rows + 1):
        start = part_index * block_rows
        window_part = extended[start:start + row_count].astype(jnp.float32).reshape(block_count, block_rows, group_count, group_size)
        pieces.append(jnp.einsum('brgc,bsgc->grs', left_side, window_part, precision=lax.Precision.HIGHEST))
    pairwise = jnp.concatenate(pieces, 2)
    flat_rows = pairwise.reshape(group_count, block_rows * span_len)
    flat_rows = jnp.concatenate([flat_rows, jnp.zeros((group_count, block_rows), jnp.float32)], 1)
    skewed = flat_rows.reshape(group_count, block_rows, span_len + 1)
    return lax.optimization_barrier(jnp.sum(skewed[:, :, :filt_len], 1)).T

def reference(cotangent, in_gate, mid_gate, layer_inputs, filters, steer_second, filter_second):
    block_rows = math.gcd(32, FILTER_LEN)
    incoming = cotangent
    steer_steps = [None] * SECTIONS
    filter_steps = [None] * SECTIONS
    for layer_index in range(SECTIONS - 1, -1, -1):
        gate_now = in_gate[layer_index].astype(jnp.float32)
        mid_now = mid_gate[layer_index].astype(jnp.float32)
        values = (mid_now * layer_inputs[layer_index].astype(jnp.float32)).astype(jnp.bfloat16)
        weighted = (gate_now * incoming.astype(jnp.float32)).astype(jnp.bfloat16)
        extended = jnp.concatenate([weighted, jnp.zeros((FILTER_LEN, CHANNELS), jnp.bfloat16)], 0)
        band_full = band_matrix(filters[layer_index], block_rows)
        filtered = filter_rows(band_full, extended, TOKENS, FILTER_LEN, block_rows)
        outgoing = (incoming.astype(jnp.float32) + mid_now * filtered).astype(jnp.bfloat16)
        local_filter = filter_grad(extended, values, GROUPS, FILTER_LEN, block_rows)
        local_steer = lax.optimization_barrier(jnp.sum(outgoing.astype(jnp.float32), 0))
        steer_steps[layer_index] = local_steer / jnp.sqrt(steer_second[layer_index] + local_steer * local_steer)
        filter_steps[layer_index] = local_filter / jnp.sqrt(filter_second[layer_index] + local_filter * local_filter)
        incoming = outgoing
    return (jnp.stack(steer_steps, 0), jnp.stack(filter_steps, 0))
```

```python
import functools

import jax
import jax.numpy as jnp
from jax import lax
from jax.experimental import pallas as pl
from jax.experimental.pallas import tpu as pltpu
from jax.sharding import PartitionSpec as P

F32 = jnp.float32
BF16 = jnp.bfloat16
LANES = 128
SUB = 32
FLOPS_A_CYCLE = 4 * 2 * 256 * 256


def lane_of(shape):
    return lax.broadcasted_iota(jnp.int32, shape, 1)


def row_of(shape):
    return lax.broadcasted_iota(jnp.int32, shape, 0)


def times(a, b):
    return (a.astype(F32) * b.astype(F32)).astype(BF16)


def turned(x):
    return pltpu.roll(x, LANES // 2, 1)


def spread(x, x_turned, parity, count):
    low = lane_of((count, LANES)) < LANES // 2
    natural, other = (x, x_turned) if parity == 0 else (x_turned, x)
    tiles = []
    for first in (0, 2 * SUB):
        tiles.append(jnp.where(low, natural[first : first + count], other[first + SUB : first + SUB + count]))
    return jnp.concatenate(tiles, 1)


def gathered(even, odd):
    low = lane_of((SUB, LANES)) < LANES // 2
    out = []
    for tile in range(2):
        a = even[:, tile * LANES : (tile + 1) * LANES]
        b = odd[:, tile * LANES : (tile + 1) * LANES]
        out.append(jnp.where(low, a, turned(b)))
        out.append(jnp.where(low, turned(a), b))
    return jnp.concatenate(out, 0)


def in_order(reverse, own, halo):
    return jnp.concatenate([jnp.where(reverse, halo, own), jnp.where(reverse, own, halo)], 0)


def diagonal_sums(circ):
    total = circ[:8]
    for first in range(8, circ.shape[0], 8):
        total = total + pltpu.roll(circ[first : first + 8], LANES - first, 1)
    for fold in (4, 2, 1):
        total = total + pltpu.roll(pltpu.roll(total, LANES - fold, 1), 8 - fold, 0)
    return total[:1]


def near(reverse_int, shape):
    return lane_of(shape) - row_of(shape) >= reverse_int


def tap_matrix(reverse, taps_by_group):
    taps = taps_by_group.shape[0]
    source = row_of((taps, taps))
    target = lane_of((taps, taps))
    mirrored = jnp.where(source == 0, 0, taps - source)
    pick = jnp.where(target == jnp.where(reverse, mirrored, source), 1.0, 0.0)
    return pick, taps


def weigh_kernel(role, gate, incoming, mid, out):
    reverse = role[0] > 0

    @pl.when(reverse)
    def _():
        out[...] = mid[...]

    @pl.when(jnp.logical_not(reverse))
    def _():
        out[...] = times(gate[...], incoming[...])


def values_kernel(role, mid, inputs, values):
    values[...] = times(mid[...], inputs[...])


def taps_kernel(role, filters, taps_out):
    pick, _ = tap_matrix(role[0] > 0, filters[...])
    taps_out[...] = lax.dot_general(
        filters[...], pick.astype(BF16), (((0,), (0,)), ((), ())), preferred_element_type=F32
    )


def conv_kernel(group_size, role, own, halo, taps, mid, incoming, outgoing, filtered):
    reverse = role[0] > 0
    width = own.shape[1]
    half = LANES // 2
    per_half = half // group_size
    mask = near(role[0], (SUB, LANES))
    zero = jnp.zeros((SUB, LANES), F32)
    lane_group = (lane_of((SUB, 2 * LANES)) % half) // group_size
    for pair in range(width // LANES):
        cols = pl.ds(pair * LANES, LANES)
        ext = in_order(reverse, own[:, cols], halo[:, cols])
        ext_turned = turned(ext)
        results = []
        for parity in range(2):
            window = spread(ext, ext_turned, parity, own.shape[0] + SUB)
            bands = []
            for g in range(per_half):
                row = taps[pl.ds((2 * pair + parity) * per_half + g, 1), :]
                circ = pltpu.roll(jnp.broadcast_to(row, (SUB, LANES)), 0, 1, stride=1, stride_axis=0)
                band = jnp.concatenate(
                    [jnp.where(mask, circ, zero), jnp.where(mask, zero, circ)[:, :SUB]], 1
                )
                bands.append(band.astype(BF16))
            product = jnp.dot(jnp.concatenate(bands, 0), window, preferred_element_type=F32)
            total = product[:SUB]
            for g in range(1, per_half):
                total = jnp.where(lane_group == g, product[g * SUB : (g + 1) * SUB], total)
            results.append(total)
        conv = gathered(*results)
        filtered[:, cols] = conv
        outgoing[:, cols] = (
            incoming[:, cols].astype(F32) + mid[:, cols].astype(F32) * conv
        ).astype(BF16)


def grad_kernel(
    group_size, role, gate, mid, inputs, values_halo, own, halo, outgoing, received, filtered,
    tap_grad, steer_grad, left, right_own, right_halo,
):
    reverse = role[0] > 0
    width = own.shape[1]
    half = LANES // 2
    per_half = half // group_size

    @pl.when(reverse)
    def _():
        grad = received[...]
        weighted = times(gate[...], grad)
        left[...] = weighted
        right_own[...] = times(mid[...], inputs[...])
        right_halo[...] = values_halo[...]
        grad_in = grad.astype(F32) + weighted.astype(F32) * filtered[...]
        steer_grad[...] = jnp.sum(grad_in, 0, keepdims=True)

    @pl.when(jnp.logical_not(reverse))
    def _():
        left[...] = times(mid[...], inputs[...])
        right_own[...] = own[...]
        right_halo[...] = halo[...]
        steer_grad[...] = jnp.sum(outgoing[...].astype(F32), 0, keepdims=True)

    mask = near(role[0], (SUB, LANES))
    lane_group = (lane_of((SUB, 2 * LANES)) % half) // group_size
    nothing = jnp.zeros((SUB, 2 * LANES), BF16)
    for pair in range(width // LANES):
        cols = pl.ds(pair * LANES, LANES)
        ext = in_order(reverse, right_own[:, cols], right_halo[:, cols])
        ext_turned = turned(ext)
        rows = left[:, cols]
        rows_turned = turned(rows)
        for parity in range(2):
            window = spread(ext, ext_turned, parity, own.shape[0] + SUB)
            short = spread(rows, rows_turned, parity, SUB)
            lhs = jnp.concatenate(
                [jnp.where(lane_group == g, short, nothing) for g in range(per_half)], 0
            )
            product = lax.dot_general(lhs, window, (((1,), (1,)), ((), ())), preferred_element_type=F32)
            for g in range(per_half):
                block = product[g * SUB : (g + 1) * SUB]
                late = jnp.concatenate([block[:, LANES:], jnp.zeros((SUB, LANES - SUB), F32)], 1)
                circ = jnp.where(mask, block[:, :LANES], late)
                tap_grad[pl.ds((2 * pair + parity) * per_half + g, 1), :] = diagonal_sums(circ)


def step_kernel(role, parts, steer_second, filter_second, steer_out, filter_out):
    total = jnp.sum(parts[...], 0)
    groups = filter_second.shape[0]
    pick, _ = tap_matrix(role[0] > 0, filter_second[...].T)
    tap_grad = jnp.dot(total[:groups], pick, preferred_element_type=F32, precision=lax.Precision.HIGHEST)
    filter_out[...] = tap_grad / jnp.sqrt(filter_second[...] + tap_grad * tap_grad)
    channels = steer_out.shape[1]
    for row in range(pl.cdiv(channels, LANES)):
        cols = min(LANES, channels - row * LANES)
        at = pl.ds(row * LANES, cols)
        grad = total[groups + row : groups + row + 1, :cols]
        steer_out[:, at] = grad / jnp.sqrt(steer_second[:, at] + grad * grad)


def spec(rows, width, first=0):
    return pl.BlockSpec((rows, width), lambda i: (0, i + first))


SMEM = pl.BlockSpec(memory_space=pltpu.SMEM)
ANY = pl.BlockSpec(memory_space=pl.ANY)


def call(kernel, grid, in_specs, out_specs, out_shape, scratch=(), name=None, cycles=100, after=()):
    count = len(in_specs)

    def with_after(*refs):
        kernel(*refs[:count], *refs[count + len(after) :])

    return pl.pallas_call(
        with_after,
        grid=grid,
        in_specs=list(in_specs) + [ANY] * len(after),
        out_specs=out_specs,
        out_shape=out_shape,
        scratch_shapes=list(scratch),
        compiler_params=pltpu.CompilerParams(vmem_limit_bytes=32 * 1024 * 1024),
        cost_estimate=pl.CostEstimate(flops=cycles * FLOPS_A_CYCLE, bytes_accessed=0, transcendentals=0),
        name=name,
    )


def body(cotangent, in_gate, mid_gate, layer_inputs, filters, steer_second, filter_second):
    in_gate, mid_gate, layer_inputs = in_gate[0], mid_gate[0], layer_inputs[0]
    rows, channels = in_gate.shape
    filt_len, groups = filters.shape[1:]
    group_size = channels // groups
    sections, seqs = lax.axis_size("section"), lax.axis_size("seq")
    my_section = lax.axis_index("section")
    role = (my_section == 0).astype(jnp.int32).reshape(1)

    chunks = 4
    width = channels // chunks
    block = min(width, 512)
    steps = width // block
    block_groups = block // group_size
    both = [(seqs * s + i, seqs * s + i - 1) for s in range(1, sections) for i in range(1, seqs)]
    ahead = [(i, i + 1) for i in range(seqs - 1)]
    down = [(s, s - 1) for s in range(1, sections)]

    def bf16(width_of):
        return jax.ShapeDtypeStruct((rows, width_of), BF16)

    def weigh(incoming, first, last, offset, after=()):
        return call(
            weigh_kernel,
            ((last - first) // block,),
            [SMEM, spec(rows, block, first // block), spec(rows, block, (first - offset) // block),
             spec(rows, block, first // block)],
            spec(rows, block),
            bf16(last - first),
            name="weigh",
            after=after,
        )(role, in_gate, incoming, mid_gate, *after)

    def gradients(k):
        own, halo, at = sources[k]
        here = spec(rows, block, k * steps)
        values_at = spec(rows, block, k * width % half // block)
        after = tuple(outgoing[-1:])
        return call(
            functools.partial(grad_kernel, group_size),
            (steps,),
            [SMEM, here, here, here, values_at, spec(rows, block, at), spec(rows, block, at)]
            + [spec(rows, block)] * 3,
            [pl.BlockSpec((block_groups, filt_len), lambda i: (i, 0)), pl.BlockSpec((1, block), lambda i: (0, i))],
            [jax.ShapeDtypeStruct((width // group_size, filt_len), F32), jax.ShapeDtypeStruct((1, width), F32)],
            scratch=[pltpu.VMEM((rows, block), BF16)] * 3,
            name="grads",
            cycles=2000,
            after=after,
        )(role, in_gate, mid_gate, layer_inputs, values_halos[k * width // half], own, halo, outgoing[k],
          received[k], filtered[k], *after)

    taps = call(
        taps_kernel,
        (1,),
        [SMEM, pl.BlockSpec((filt_len, groups), lambda i: (0, 0))],
        pl.BlockSpec((groups, filt_len), lambda i: (0, 0)),
        jax.ShapeDtypeStruct((groups, filt_len), F32),
        name="taps",
    )(role, filters[0])

    def values_of(first, last, after):
        here = spec(rows, block, first // block)
        values = call(
            values_kernel, ((last - first) // block,), [SMEM, here, here], spec(rows, block), bf16(last - first),
            name="values", after=after,
        )(role, mid_gate, layer_inputs, *after)
        return lax.ppermute(values, ("section", "seq"), ahead)

    half = channels // 2
    incoming = [(cotangent, 0)] * chunks
    for hop in range(sections - 1):
        final = hop == sections - 2
        starts = [0, width, half] if hop == 0 else [k * width for k in range(chunks)]
        ends = starts[1:] + [channels]
        owns, halos, sources, outgoing, filtered, received = [], [], [], [], [], []

        def segment(after):
            first, last = starts[len(owns)], ends[len(owns)]
            array, offset = incoming[first // width]
            owns.append(weigh(array, first, last, offset, after))
            halos.append(lax.ppermute(owns[-1], ("section", "seq"), both + ahead))

        for k in range(chunks):
            if k == 0:
                segment(())
                segment(tuple(owns))
            if starts[len(owns) - 1] <= k * width and len(owns) < len(starts):
                segment(tuple(outgoing[-1:]))
            part = max(i for i, first in enumerate(starts) if first <= k * width)
            at = (k * width - starts[part]) // block
            array, offset = incoming[k]
            before = tuple(outgoing[-1:]) + tuple(received[-2:-1])
            out, conv = call(
                functools.partial(conv_kernel, group_size),
                (steps,),
                [SMEM, spec(rows, block, at), spec(rows, block, at),
                 pl.BlockSpec((block_groups, filt_len), lambda i, k=k: (i + k * steps, 0)),
                 spec(rows, block, k * steps), spec(rows, block, (k * width - offset) // block)],
                [spec(rows, block), spec(rows, block)],
                [bf16(width), jax.ShapeDtypeStruct((rows, width), F32)],
                name="filter",
                cycles=1000,
                after=before,
            )(role, owns[part], halos[part], taps, mid_gate, array, *before)
            sources.append((owns[part], halos[part], at))
            outgoing.append(out)
            filtered.append(conv)
            received.append(lax.ppermute(out, "section", down))
            if final and k == 1:
                values_halos = [values_of(0, half, (out,)), values_of(half, channels, (out,))]
        last = my_section == sections - 1
        incoming = [
            (jnp.where(last, cotangent[:, k * width : (k + 1) * width], received[k]), k * width)
            for k in range(chunks)
        ]
    grads = [gradients(k) for k in range(chunks)]
    tap_grads, steer_grads = zip(*grads)

    tap_all = jnp.concatenate(tap_grads, 0).reshape(seqs, groups // seqs, filt_len)
    own_channels = channels // seqs
    steer_rows = pl.cdiv(own_channels, LANES)
    steer_all = jnp.concatenate(steer_grads, 1).reshape(seqs, own_channels)
    steer_all = jnp.pad(steer_all, ((0, 0), (0, steer_rows * LANES - own_channels)))
    packed = jnp.concatenate([tap_all, steer_all.reshape(seqs, steer_rows, LANES)], 1)
    parts = lax.all_to_all(packed, "seq", 0, 0)
    steer_step, filter_step = pl.pallas_call(
        step_kernel,
        in_specs=[SMEM] + [pl.BlockSpec(memory_space=pltpu.VMEM)] * 3,
        out_shape=[
            jax.ShapeDtypeStruct((1, own_channels), F32),
            jax.ShapeDtypeStruct((groups // seqs, filt_len), F32),
        ],
        name="step",
    )(role, parts, steer_second, filter_second[0].T)
    return steer_step, filter_step.T[None]


def solution(mesh):
    in_specs = (
        P("seq", None),
        P("section", "seq", None),
        P("section", "seq", None),
        P("section", "seq", None),
        P("section", None, None),
        P("section", "seq"),
        P("section", None, "seq"),
    )
    out_specs = (P("section", "seq"), P("section", None, "seq"))
    return jax.shard_map(body, mesh=mesh, in_specs=in_specs, out_specs=out_specs, check_vma=False)
```

```python
import functools

import jax
import jax.numpy as jnp
from jax import lax
from jax.experimental import pallas as pl
from jax.experimental.pallas import tpu as pltpu
from jax.sharding import PartitionSpec as P

F32 = jnp.float32
BF16 = jnp.bfloat16
LANES = 128
SUB = 32
CHUNK_EDGES = (0, 2, 4, 6, 8)
HALO_EDGES = (0, 4, 8)
FIRST_VMEM = 61 * 1024 * 1024


def lane_of(shape):
    return lax.broadcasted_iota(jnp.int32, shape, 1)


def row_of(shape):
    return lax.broadcasted_iota(jnp.int32, shape, 0)


def times(a, b):
    return (a.astype(F32) * b.astype(F32)).astype(BF16)


def turned(x):
    return pltpu.roll(x, LANES // 2, 1)


def spread(x, x_turned, parity, count):
    low = lane_of((count, LANES)) < LANES // 2
    natural, other = (x, x_turned) if parity == 0 else (x_turned, x)
    tiles = []
    for first in (0, 2 * SUB):
        tiles.append(jnp.where(low, natural[first : first + count], other[first + SUB : first + SUB + count]))
    return jnp.concatenate(tiles, 1)


def gathered(even, odd):
    low = lane_of((SUB, LANES)) < LANES // 2
    out = []
    for tile in range(2):
        a = even[:, tile * LANES : (tile + 1) * LANES]
        b = odd[:, tile * LANES : (tile + 1) * LANES]
        out.append(jnp.where(low, a, turned(b)))
        out.append(jnp.where(low, turned(a), b))
    return jnp.concatenate(out, 0)


def in_order(reverse, own, halo):
    return jnp.concatenate([jnp.where(reverse, halo, own), jnp.where(reverse, own, halo)], 0)


def diagonal_sums(circ):
    total = circ[:8]
    for first in range(8, circ.shape[0], 8):
        total = total + pltpu.roll(circ[first : first + 8], LANES - first, 1)
    for fold in (4, 2, 1):
        total = total + pltpu.roll(pltpu.roll(total, LANES - fold, 1), 8 - fold, 0)
    return total[:1]


def near(reverse_int, shape):
    return lane_of(shape) - row_of(shape) >= reverse_int


def tap_matrix(reverse, taps_by_group):
    taps = taps_by_group.shape[0]
    source = row_of((taps, taps))
    target = lane_of((taps, taps))
    mirrored = jnp.where(source == 0, 0, taps - source)
    pick = jnp.where(target == jnp.where(reverse, mirrored, source), 1.0, 0.0)
    return pick, taps


def weigh_kernel(role, gate, incoming, out):
    @pl.when(role[0] == 0)
    def _():
        out[...] = times(gate[...], incoming[...])


def first_weigh_kernel(pieces, role, gate, incoming, *refs):
    outs, (gate_part, incoming_part, sems) = refs[:-3], refs[-3:]

    @pl.when(role[0] == 0)
    def _():
        copies = []
        for i, (first, last, _, _) in enumerate(pieces):
            cols = pl.ds(first, last - first)
            for which, (source, part) in enumerate(((gate, gate_part), (incoming, incoming_part))):
                copy = pltpu.make_async_copy(source.at[:, cols], part.at[:, cols], sems.at[which, i])
                copies.append(copy)
                copy.start()
        for i, (first, last, out, at) in enumerate(pieces):
            copies[2 * i].wait()
            copies[2 * i + 1].wait()
            cols = pl.ds(first, last - first)
            outs[out][:, pl.ds(at, last - first)] = times(gate_part[:, cols], incoming_part[:, cols])


def taps_kernel(role, filters, taps_out):
    pick, _ = tap_matrix(role[0] > 0, filters[...])
    taps_out[...] = lax.dot_general(
        filters[...], pick.astype(BF16), (((0,), (0,)), ((), ())), preferred_element_type=F32
    )


def convolved(reverse, group_size, own, halo, taps, first_group):
    half = LANES // 2
    per_half = half // group_size
    mask = near(int(reverse), (SUB, LANES))
    zero = jnp.zeros((SUB, LANES), F32)
    lane_group = (lane_of((SUB, 2 * LANES)) % half) // group_size
    ext = jnp.concatenate([halo, own] if reverse else [own, halo], 0)
    ext_turned = turned(ext)
    results = []
    for parity in range(2):
        window = spread(ext, ext_turned, parity, own.shape[0] + SUB)
        bands = []
        for g in range(per_half):
            row = taps[pl.ds(first_group + parity * per_half + g, 1), :]
            circ = pltpu.roll(jnp.broadcast_to(row, (SUB, LANES)), 0, 1, stride=1, stride_axis=0)
            band = jnp.concatenate([jnp.where(mask, circ, zero), jnp.where(mask, zero, circ)[:, :SUB]], 1)
            bands.append(band.astype(BF16))
        product = jnp.dot(jnp.concatenate(bands, 0), window, preferred_element_type=F32)
        total = product[:SUB]
        for g in range(1, per_half):
            total = jnp.where(lane_group == g, product[g * SUB : (g + 1) * SUB], total)
        results.append(total)
    return gathered(*results)


def filter_kernel(group_size, role, own, halo, taps, mid, incoming, outgoing):
    @pl.when(role[0] == 0)
    def _():
        for first in range(0, own.shape[1], LANES):
            cols = pl.ds(first, LANES)
            conv = convolved(False, group_size, own[:, cols], halo[:, cols], taps, first // group_size)
            outgoing[:, cols] = (
                incoming[:, cols].astype(F32) + mid[:, cols].astype(F32) * conv
            ).astype(BF16)


def turned_filter_kernel(group_size, role, mid, mid_halo, taps, filtered):
    @pl.when(role[0] > 0)
    def _():
        for first in range(0, mid.shape[1], LANES):
            cols = pl.ds(first, LANES)
            filtered[:, cols] = convolved(True, group_size, mid[:, cols], mid_halo[:, cols], taps, first // group_size)


def grad_kernel(
    group_size, role, gate, mid, inputs, mid_halo, inputs_halo, own, halo, outgoing, received, filtered,
    tap_grad, steer_grad, left, right_own, right_halo,
):
    reverse = role[0] > 0
    width = own.shape[1]
    half = LANES // 2
    per_half = half // group_size

    @pl.when(reverse)
    def _():
        grad = received[...]
        weighted = times(gate[...], grad)
        left[...] = weighted
        right_own[...] = times(mid[...], inputs[...])
        right_halo[...] = times(mid_halo[...], inputs_halo[...])
        grad_in = grad.astype(F32) + weighted.astype(F32) * filtered[...]
        steer_grad[...] = jnp.sum(grad_in, 0, keepdims=True)

    @pl.when(jnp.logical_not(reverse))
    def _():
        left[...] = times(mid[...], inputs[...])
        right_own[...] = own[...]
        right_halo[...] = halo[...]
        steer_grad[...] = jnp.sum(outgoing[...].astype(F32), 0, keepdims=True)

    mask = near(role[0], (SUB, LANES))
    lane_group = (lane_of((SUB, 2 * LANES)) % half) // group_size
    nothing = jnp.zeros((SUB, 2 * LANES), BF16)
    for pair in range(width // LANES):
        cols = pl.ds(pair * LANES, LANES)
        ext = in_order(reverse, right_own[:, cols], right_halo[:, cols])
        ext_turned = turned(ext)
        rows = left[:, cols]
        rows_turned = turned(rows)
        for parity in range(2):
            window = spread(ext, ext_turned, parity, own.shape[0] + SUB)
            short = spread(rows, rows_turned, parity, SUB)
            lhs = jnp.concatenate(
                [jnp.where(lane_group == g, short, nothing) for g in range(per_half)], 0
            )
            product = lax.dot_general(lhs, window, (((1,), (1,)), ((), ())), preferred_element_type=F32)
            for g in range(per_half):
                block = product[g * SUB : (g + 1) * SUB]
                late = jnp.concatenate([block[:, LANES:], jnp.zeros((SUB, LANES - SUB), F32)], 1)
                circ = jnp.where(mask, block[:, :LANES], late)
                tap_grad[pl.ds((2 * pair + parity) * per_half + g, 1), :] = diagonal_sums(circ)


def step_kernel(role, parts, steer_second, filter_second, steer_out, filter_out):
    total = jnp.sum(parts[...], 0)
    groups = filter_second.shape[0]
    tap_grad = total[:groups]
    lane = lane_of(tap_grad.shape)
    mirrored = jnp.where(lane == 0, 0, tap_grad.shape[1] - lane)
    tap_grad = jnp.take_along_axis(tap_grad, jnp.where(role[0] > 0, mirrored, lane), axis=1)
    filter_out[...] = tap_grad / jnp.sqrt(filter_second[...] + tap_grad * tap_grad)
    channels = steer_out.shape[1]
    for row in range(pl.cdiv(channels, LANES)):
        cols = min(LANES, channels - row * LANES)
        at = pl.ds(row * LANES, cols)
        grad = total[groups + row : groups + row + 1, :cols]
        steer_out[:, at] = grad / jnp.sqrt(steer_second[:, at] + grad * grad)


def spec(rows, width, first=0):
    return pl.BlockSpec((rows, width), lambda i: (0, i + first))


SMEM = pl.BlockSpec(memory_space=pltpu.SMEM)
ANY = pl.BlockSpec(memory_space=pl.ANY)


def call(kernel, grid, in_specs, out_specs, out_shape, scratch=(), name=None, cycles=100, after=()):
    count = len(in_specs)

    def with_after(*refs):
        kernel(*refs[:count], *refs[count + len(after) :])

    return pl.pallas_call(
        with_after,
        grid=grid,
        in_specs=list(in_specs) + [ANY] * len(after),
        out_specs=out_specs,
        out_shape=out_shape,
        scratch_shapes=list(scratch),
        compiler_params=pltpu.CompilerParams(vmem_limit_bytes=32 * 1024 * 1024),
        cost_estimate=pl.CostEstimate(flops=cycles, bytes_accessed=0, transcendentals=0),
        name=name,
    )


def body(cotangent, in_gate, mid_gate, layer_inputs, filters, steer_second, filter_second):
    in_gate, mid_gate, layer_inputs = in_gate[0], mid_gate[0], layer_inputs[0]
    rows, channels = in_gate.shape
    filt_len, groups = filters.shape[1:]
    group_size = channels // groups
    sections, seqs = lax.axis_size("section"), lax.axis_size("seq")
    my_section = lax.axis_index("section")
    role = (my_section == 0).astype(jnp.int32).reshape(1)

    edges = [channels * eighths // 8 for eighths in CHUNK_EDGES]
    bounds = list(zip(edges[:-1], edges[1:]))
    block = channels // 8
    block_groups = block // group_size
    behind = [(seqs * s + i, seqs * s + i - 1) for s in range(1, sections) for i in range(1, seqs)]
    ahead = [(i, i + 1) for i in range(seqs - 1)]
    down = [(s, s - 1) for s in range(1, sections)]

    def bf16(width_of):
        return jax.ShapeDtypeStruct((rows, width_of), BF16)

    def weigh(incoming, first, last):
        return call(
            weigh_kernel, ((last - first) // block,), [SMEM, spec(rows, block, first // block), spec(rows, block)],
            spec(rows, block), bf16(last - first), name="weigh",
        )(role, in_gate, incoming)

    def first_weigh(starts, ends):
        pieces = [
            (at, at + block, part, at - first)
            for part, (first, last) in enumerate(zip(starts, ends))
            for at in range(first, last, block)
        ]
        whole = pltpu.VMEM((rows, channels), BF16)
        return pl.pallas_call(
            functools.partial(first_weigh_kernel, pieces),
            in_specs=[SMEM] + [pl.BlockSpec(memory_space=pltpu.HBM)] * 2,
            out_specs=[pl.BlockSpec(memory_space=pltpu.VMEM)] * len(starts),
            out_shape=[bf16(last - first) for first, last in zip(starts, ends)],
            scratch_shapes=[whole, whole, pltpu.SemaphoreType.DMA((2, len(pieces)))],
            compiler_params=pltpu.CompilerParams(vmem_limit_bytes=FIRST_VMEM),
            name="first_weigh",
        )(role, in_gate, cotangent)

    mid_halo = lax.ppermute(mid_gate, ("section", "seq"), ahead)
    inputs_halo = lax.ppermute(layer_inputs, ("section", "seq"), ahead)
    taps = call(
        taps_kernel,
        (1,),
        [SMEM, pl.BlockSpec((filt_len, groups), lambda i: (0, 0))],
        pl.BlockSpec((groups, filt_len), lambda i: (0, 0)),
        jax.ShapeDtypeStruct((groups, filt_len), F32),
        name="taps",
    )(role, filters[0])
    group_spec = lambda first: pl.BlockSpec((block_groups, filt_len), lambda i: (i + first, 0))

    incoming = [(cotangent, 0)] * len(bounds)
    for hop in range(sections - 1):
        split = [channels * eighths // 8 for eighths in HALO_EDGES] if hop == 0 else edges
        starts, ends = split[:-1], split[1:]
        if hop == 0:
            owns = first_weigh(starts, ends)
        else:
            owns = [weigh(array, first, last) for (array, _), first, last in zip(incoming, starts, ends)]
        halos = [lax.ppermute(own, ("section", "seq"), behind) for own in owns]
        sources, outgoing, received = [], [], []
        for k, (first, last) in enumerate(bounds):
            part = max(i for i, start in enumerate(starts) if start <= first)
            at = (first - starts[part]) // block
            array, offset = incoming[k]
            before = tuple(outgoing[-1:])
            out = call(
                functools.partial(filter_kernel, group_size),
                ((last - first) // block,),
                [SMEM, spec(rows, block, at), spec(rows, block, at), group_spec(first // block),
                 spec(rows, block, first // block), spec(rows, block, (first - offset) // block)],
                spec(rows, block),
                bf16(last - first),
                name="filter",
                cycles=1000,
                after=before,
            )(role, owns[part], halos[part], taps, mid_gate, array, *before)
            sources.append((owns[part], halos[part], at))
            outgoing.append(out)
            received.append(lax.ppermute(out, "section", down))
        top = my_section == sections - 1
        incoming = [
            (jnp.where(top, cotangent[:, first:last], arrived), first)
            for (first, last), arrived in zip(bounds, received)
        ]

    filtered = call(
        functools.partial(turned_filter_kernel, group_size),
        (channels // block,),
        [SMEM, spec(rows, block), spec(rows, block), group_spec(0)],
        spec(rows, block),
        jax.ShapeDtypeStruct((rows, channels), F32),
        name="turned_filter",
        cycles=4000,
        after=tuple(outgoing[-1:]),
    )(role, mid_gate, mid_halo, taps, *outgoing[-1:])

    grads = []
    for k, (first, last) in enumerate(bounds):
        own, halo, at = sources[k]
        width = last - first
        here = spec(rows, block, first // block)
        after = tuple(grads[-1][:1] if grads else ())
        grads.append(call(
            functools.partial(grad_kernel, group_size),
            (width // block,),
            [SMEM, here, here, here, here, here, spec(rows, block, at), spec(rows, block, at)]
            + [spec(rows, block)] * 2 + [here],
            [group_spec(0), pl.BlockSpec((1, block), lambda i: (0, i))],
            [jax.ShapeDtypeStruct((width // group_size, filt_len), F32), jax.ShapeDtypeStruct((1, width), F32)],
            scratch=[pltpu.VMEM((rows, block), BF16)] * 3,
            name="grads",
            cycles=2000,
            after=after,
        )(role, in_gate, mid_gate, layer_inputs, mid_halo, inputs_halo, own, halo, outgoing[k],
          received[k], filtered, *after))
    tap_grads, steer_grads = zip(*grads)

    inner = max(d for d in range(1, seqs + 1) if seqs % d == 0 and d * d <= seqs)
    outer = seqs // inner
    own_channels = channels // seqs
    steer_rows = pl.cdiv(own_channels, LANES)
    tap_all = jnp.concatenate(tap_grads, 0).reshape(seqs, groups // seqs, filt_len)
    steer_all = jnp.concatenate(steer_grads, 1).reshape(seqs, own_channels)
    steer_all = jnp.pad(steer_all, ((0, 0), (0, steer_rows * LANES - own_channels)))
    packed = jnp.concatenate([tap_all, steer_all.reshape(seqs, steer_rows, LANES)], 1)
    packed = packed.reshape((outer, inner) + packed.shape[1:]).swapaxes(0, 1)
    near_by = [[o * inner + i for i in range(inner)] for o in range(outer)]
    far_off = [[o * inner + i for o in range(outer)] for i in range(inner)]
    parts = jnp.sum(lax.all_to_all(packed, "seq", 0, 0, axis_index_groups=near_by), 0)
    parts = lax.all_to_all(parts, "seq", 0, 0, axis_index_groups=far_off)
    steer_step, filter_step = pl.pallas_call(
        step_kernel,
        in_specs=[SMEM] + [pl.BlockSpec(memory_space=pltpu.VMEM)] * 3,
        out_shape=[
            jax.ShapeDtypeStruct((1, own_channels), F32),
            jax.ShapeDtypeStruct((groups // seqs, filt_len), F32),
        ],
        name="step",
    )(role, parts, steer_second, filter_second[0].T)
    return steer_step, filter_step.T[None]


def solution(mesh):
    in_specs = (
        P("seq", None),
        P("section", "seq", None),
        P("section", "seq", None),
        P("section", "seq", None),
        P("section", None, None),
        P("section", "seq"),
        P("section", None, "seq"),
    )
    out_specs = (P("section", "seq"), P("section", None, "seq"))
    return jax.shard_map(body, mesh=mesh, in_specs=in_specs, out_specs=out_specs, check_vma=False)
```

```python
import functools

import jax
import jax.numpy as jnp
from jax import lax
from jax.experimental import pallas as pl
from jax.experimental.pallas import tpu as pltpu
from jax.sharding import PartitionSpec as P

F32 = jnp.float32
BF16 = jnp.bfloat16
LANES = 128
SUB = 32
CHUNK_EDGES = (0, 3, 6, 7, 8)
HALO_EDGES = (0, 3, 6, 8)


def lane_of(shape):
    return lax.broadcasted_iota(jnp.int32, shape, 1)


def row_of(shape):
    return lax.broadcasted_iota(jnp.int32, shape, 0)


def times(a, b):
    return (a.astype(F32) * b.astype(F32)).astype(BF16)


def turned(x):
    return pltpu.roll(x, LANES // 2, 1)


def spread(x, x_turned, parity, count):
    low = lane_of((count, LANES)) < LANES // 2
    natural, other = (x, x_turned) if parity == 0 else (x_turned, x)
    tiles = []
    for first in (0, 2 * SUB):
        tiles.append(jnp.where(low, natural[first : first + count], other[first + SUB : first + SUB + count]))
    return jnp.concatenate(tiles, 1)


def gathered(even, odd):
    low = lane_of((SUB, LANES)) < LANES // 2
    out = []
    for tile in range(2):
        a = even[:, tile * LANES : (tile + 1) * LANES]
        b = odd[:, tile * LANES : (tile + 1) * LANES]
        out.append(jnp.where(low, a, turned(b)))
        out.append(jnp.where(low, turned(a), b))
    return jnp.concatenate(out, 0)


def in_order(reverse, own, halo):
    return jnp.concatenate([jnp.where(reverse, halo, own), jnp.where(reverse, own, halo)], 0)


def diagonal_sums(blocks):
    tiles = []
    for block in blocks:
        tile = block[:8]
        for first in range(8, SUB, 8):
            tile = tile + pltpu.roll(block[first : first + 8], LANES - first, 1)
        tiles.append(tile)
    row = row_of((8, LANES))
    for fold in (4, 2, 1):
        upper = row % (2 * fold) < fold
        tiles = [
            jnp.where(upper, a, pltpu.roll(b, fold, 0))
            + pltpu.roll(jnp.where(upper, pltpu.roll(a, 8 - fold, 0), b), LANES - fold, 1)
            for a, b in zip(tiles[:fold], tiles[fold:])
        ]
    return tiles[0]


def near(reverse_int, shape):
    return lane_of(shape) - row_of(shape) >= reverse_int


def tap_matrix(reverse, taps_by_group):
    taps = taps_by_group.shape[0]
    source = row_of((taps, taps))
    target = lane_of((taps, taps))
    mirrored = jnp.where(source == 0, 0, taps - source)
    pick = jnp.where(target == jnp.where(reverse, mirrored, source), 1.0, 0.0)
    return pick, taps


def weigh_kernel(role, gate, incoming, mid, out, incoming_out, mid_out):
    @pl.when(role[0] == 0)
    def _():
        out[...] = times(gate[...], incoming[...])
        incoming_out[...] = incoming[...]
        mid_out[...] = mid[...]


def taps_kernel(role, filters, taps_out):
    pick, _ = tap_matrix(role[0] > 0, filters[...])
    taps_out[...] = lax.dot_general(
        filters[...], pick.astype(BF16), (((0,), (0,)), ((), ())), preferred_element_type=F32
    )


def convolved(reverse, group_size, own, halo, taps, first_group):
    half = LANES // 2
    per_half = half // group_size
    mask = near(int(reverse), (SUB, LANES))
    zero = jnp.zeros((SUB, LANES), F32)
    lane_group = (lane_of((SUB, 2 * LANES)) % half) // group_size
    ext = jnp.concatenate([halo, own] if reverse else [own, halo], 0)
    ext_turned = turned(ext)
    results = []
    for parity in range(2):
        window = spread(ext, ext_turned, parity, own.shape[0] + SUB)
        bands = []
        for g in range(per_half):
            row = taps[pl.ds(first_group + parity * per_half + g, 1), :]
            circ = pltpu.roll(jnp.broadcast_to(row, (SUB, LANES)), 0, 1, stride=1, stride_axis=0)
            band = jnp.concatenate([jnp.where(mask, circ, zero), jnp.where(mask, zero, circ)[:, :SUB]], 1)
            bands.append(band.astype(BF16))
        product = jnp.dot(jnp.concatenate(bands, 0), window, preferred_element_type=F32)
        total = product[:SUB]
        for g in range(1, per_half):
            total = jnp.where(lane_group == g, product[g * SUB : (g + 1) * SUB], total)
        results.append(total)
    return gathered(*results)


def filter_kernel(group_size, role, own, halo, taps, mid, incoming, outgoing):
    @pl.when(role[0] == 0)
    def _():
        for first in range(0, own.shape[1], LANES):
            cols = pl.ds(first, LANES)
            conv = convolved(False, group_size, own[:, cols], halo[:, cols], taps, first // group_size)
            outgoing[:, cols] = (
                incoming[:, cols].astype(F32) + mid[:, cols].astype(F32) * conv
            ).astype(BF16)


def turned_filter_kernel(group_size, role, mid, mid_halo, taps, filtered):
    @pl.when(role[0] > 0)
    def _():
        for first in range(0, mid.shape[1], LANES):
            cols = pl.ds(first, LANES)
            filtered[:, cols] = convolved(True, group_size, mid[:, cols], mid_halo[:, cols], taps, first // group_size)


def grad_kernel(
    group_size, role, gate, mid, inputs, mid_halo, inputs_halo, own, halo, outgoing, received, filtered,
    tap_grad, steer_grad, left, right_own, right_halo,
):
    reverse = role[0] > 0
    width = own.shape[1]
    half = LANES // 2
    per_half = half // group_size

    @pl.when(reverse)
    def _():
        grad = received[...]
        weighted = times(gate[...], grad)
        left[...] = weighted
        right_own[...] = times(mid[...], inputs[...])
        right_halo[...] = times(mid_halo[...], inputs_halo[...])
        grad_in = grad.astype(F32) + weighted.astype(F32) * filtered[...]
        steer_grad[...] = jnp.sum(grad_in, 0, keepdims=True)

    @pl.when(jnp.logical_not(reverse))
    def _():
        left[...] = times(mid[...], inputs[...])
        right_own[...] = own[...]
        right_halo[...] = halo[...]
        steer_grad[...] = jnp.sum(outgoing[...].astype(F32), 0, keepdims=True)

    mask = near(role[0], (SUB, LANES))
    lane_group = (lane_of((SUB, 2 * LANES)) % half) // group_size
    nothing = jnp.zeros((SUB, 2 * LANES), BF16)
    for pair in range(width // LANES):
        cols = pl.ds(pair * LANES, LANES)
        ext = in_order(reverse, right_own[:, cols], right_halo[:, cols])
        ext_turned = turned(ext)
        rows = left[:, cols]
        rows_turned = turned(rows)
        blocks = []
        for parity in range(2):
            window = spread(ext, ext_turned, parity, own.shape[0] + SUB)
            short = spread(rows, rows_turned, parity, SUB)
            lhs = jnp.concatenate(
                [jnp.where(lane_group == g, short, nothing) for g in range(per_half)], 0
            )
            product = lax.dot_general(lhs, window, (((1,), (1,)), ((), ())), preferred_element_type=F32)
            for g in range(per_half):
                block = product[g * SUB : (g + 1) * SUB]
                late = jnp.concatenate([block[:, LANES:], jnp.zeros((SUB, LANES - SUB), F32)], 1)
                blocks.append(jnp.where(mask, block[:, :LANES], late))
        tap_grad[pl.ds(8 * pair, 8), :] = diagonal_sums(blocks)


def halves_of(bit, zero, one):
    mine = bit > 0
    return jnp.where(mine, zero, one), jnp.where(mine, one, zero)


def pack_kernel(owners, bits, *refs):
    count = (len(refs) - 2) // 2
    taps, steers, (give, keep) = refs[:count], refs[count : 2 * count], refs[2 * count :]
    groups = sum(ref.shape[0] for ref in taps) // owners
    channels = sum(ref.shape[1] for ref in steers) // owners

    def part(parts, axis, owner, size):
        at = owner * size
        for ref in parts:
            if at < ref.shape[axis]:
                return ref[at : at + size, :] if axis == 0 else ref[:, at : at + size]
            at -= ref.shape[axis]

    def packed(owner):
        steer = part(steers, 1, owner, channels)
        lines = [steer[:, at : at + LANES] for at in range(0, channels, LANES)]
        short = LANES - lines[-1].shape[1]
        if short > 0:
            lines[-1] = jnp.concatenate([lines[-1], jnp.zeros((1, short), F32)], 1)
        return [part(taps, 0, owner, groups)] + lines

    order = reversed_bits(owners)
    for i, (low, high) in enumerate(zip(order[: owners // 2], order[owners // 2 :])):
        at = 0
        for zero, one in zip(packed(low), packed(high)):
            lines = zero.shape[0]
            give[i, pl.ds(at, lines), :], keep[i, pl.ds(at, lines), :] = halves_of(bits[0], zero, one)
            at += lines


def reversed_bits(count):
    order = [0]
    while len(order) < count:
        order = [2 * i for i in order] + [2 * i + 1 for i in order]
    return order


def fold_kernel(step, bits, kept, arrived, give, keep):
    count = give.shape[0]
    for i in range(count):
        zero = kept[i] + arrived[i]
        one = kept[count + i] + arrived[count + i]
        give[i], keep[i] = halves_of(bits[step], zero, one)


def step_kernel(role, kept, arrived, steer_second, filter_second, steer_out, filter_out):
    total = kept[0] + arrived[0]
    groups = filter_second.shape[0]
    tap_grad = total[:groups]
    lane = lane_of(tap_grad.shape)
    mirrored = jnp.where(lane == 0, 0, tap_grad.shape[1] - lane)
    tap_grad = jnp.take_along_axis(tap_grad, jnp.where(role[0] > 0, mirrored, lane), axis=1)
    filter_out[...] = tap_grad / jnp.sqrt(filter_second[...] + tap_grad * tap_grad)
    channels = steer_out.shape[1]
    for row in range(pl.cdiv(channels, LANES)):
        cols = min(LANES, channels - row * LANES)
        at = pl.ds(row * LANES, cols)
        grad = total[groups + row : groups + row + 1, :cols]
        steer_out[:, at] = grad / jnp.sqrt(steer_second[:, at] + grad * grad)


def spec(rows, width, first=0):
    return pl.BlockSpec((rows, width), lambda i: (0, i + first))


SMEM = pl.BlockSpec(memory_space=pltpu.SMEM)
ANY = pl.BlockSpec(memory_space=pl.ANY)


def call(kernel, grid, in_specs, out_specs, out_shape, scratch=(), name=None, cycles=100, after=()):
    count = len(in_specs)

    def with_after(*refs):
        kernel(*refs[:count], *refs[count + len(after) :])

    return pl.pallas_call(
        with_after,
        grid=grid,
        in_specs=list(in_specs) + [ANY] * len(after),
        out_specs=out_specs,
        out_shape=out_shape,
        scratch_shapes=list(scratch),
        compiler_params=pltpu.CompilerParams(vmem_limit_bytes=32 * 1024 * 1024),
        cost_estimate=pl.CostEstimate(flops=cycles, bytes_accessed=0, transcendentals=0),
        name=name,
    )


def body(cotangent, in_gate, mid_gate, layer_inputs, filters, steer_second, filter_second):
    in_gate, mid_gate, layer_inputs = in_gate[0], mid_gate[0], layer_inputs[0]
    rows, channels = in_gate.shape
    filt_len, groups = filters.shape[1:]
    group_size = channels // groups
    sections, seqs = lax.axis_size("section"), lax.axis_size("seq")
    my_section = lax.axis_index("section")
    role = (my_section == 0).astype(jnp.int32).reshape(1)

    edges = [channels * eighths // 8 for eighths in CHUNK_EDGES]
    bounds = list(zip(edges[:-1], edges[1:]))
    block = channels // 8
    block_groups = block // group_size
    behind = [(seqs * s + i, seqs * s + i - 1) for s in range(1, sections) for i in range(1, seqs)]
    ahead = [(i, i + 1) for i in range(seqs - 1)]
    down = [(s, s - 1) for s in range(1, sections)]

    def bf16(width_of):
        return jax.ShapeDtypeStruct((rows, width_of), BF16)

    def weigh(incoming, first, last, offset, after):
        return call(
            weigh_kernel,
            ((last - first) // block,),
            [SMEM, spec(rows, block, first // block), spec(rows, block, (first - offset) // block),
             spec(rows, block, first // block)],
            [spec(rows, block)] * 3,
            [bf16(last - first)] * 3,
            name="weigh",
            after=after,
        )(role, *[pltpu.with_memory_space_constraint(array, pltpu.HBM) for array in (in_gate, incoming, mid_gate)],
          *after)

    taps = call(
        taps_kernel,
        (1,),
        [SMEM, pl.BlockSpec((filt_len, groups), lambda i: (0, 0))],
        pl.BlockSpec((groups, filt_len), lambda i: (0, 0)),
        jax.ShapeDtypeStruct((groups, filt_len), F32),
        name="taps",
    )(role, filters[0])
    group_spec = lambda first: pl.BlockSpec((block_groups, filt_len), lambda i: (i + first, 0))

    incoming = [(cotangent, 0)] * len(bounds)
    for hop in range(sections - 1):
        split = [channels * eighths // 8 for eighths in HALO_EDGES] if hop == 0 else edges
        starts, ends = split[:-1], split[1:]
        weighed = []
        for first, last in zip(starts, ends):
            array, offset = next(entry for entry, edge in zip(incoming, edges) if edge == first)
            weighed.append(weigh(array, first, last, offset, tuple(weighed[-1][:1] if weighed else ())))
        owns, incomings, mids = zip(*weighed)
        if hop == 0:
            mid_late, inputs_late, _ = lax.optimization_barrier((mid_gate, layer_inputs, owns[0]))
            mid_halo = lax.ppermute(mid_late, ("section", "seq"), ahead)
            inputs_halo = lax.ppermute(inputs_late, ("section", "seq"), ahead)
        halos = [lax.ppermute(own, ("section", "seq"), behind) for own in owns]
        sources, outgoing, received = [], [], []
        for k, (first, last) in enumerate(bounds):
            part = max(i for i, start in enumerate(starts) if start <= first)
            at = (first - starts[part]) // block
            before = tuple(outgoing[-1:])
            out = call(
                functools.partial(filter_kernel, group_size),
                ((last - first) // block,),
                [SMEM, spec(rows, block, at), spec(rows, block, at), group_spec(first // block),
                 spec(rows, block, at), spec(rows, block, at)],
                spec(rows, block),
                bf16(last - first),
                name="filter",
                cycles=1000,
                after=before,
            )(role, owns[part], halos[part], taps, mids[part], incomings[part], *before)
            sources.append((owns[part], halos[part], at))
            outgoing.append(out)
            received.append(lax.ppermute(out, "section", down))
        top = my_section == sections - 1
        incoming = [
            (jnp.where(top, cotangent[:, first:last], arrived), first)
            for (first, last), arrived in zip(bounds, received)
        ]

    filtered = call(
        functools.partial(turned_filter_kernel, group_size),
        (channels // block,),
        [SMEM, spec(rows, block), spec(rows, block), group_spec(0)],
        spec(rows, block),
        jax.ShapeDtypeStruct((rows, channels), F32),
        name="turned_filter",
        cycles=4000,
        after=tuple(outgoing[-1:]),
    )(role, mid_gate, mid_halo, taps, *outgoing[-1:])

    grads = []
    for k, (first, last) in enumerate(bounds):
        own, halo, at = sources[k]
        width = last - first
        here = spec(rows, block, first // block)
        after = tuple(grads[-1][:1] if grads else ())
        grads.append(call(
            functools.partial(grad_kernel, group_size),
            (width // block,),
            [SMEM, here, here, here, here, here, spec(rows, block, at), spec(rows, block, at)]
            + [spec(rows, block)] * 2 + [here],
            [group_spec(0), pl.BlockSpec((1, block), lambda i: (0, i))],
            [jax.ShapeDtypeStruct((width // group_size, filt_len), F32), jax.ShapeDtypeStruct((1, width), F32)],
            scratch=[pltpu.VMEM((rows, block), BF16)] * 3,
            name="grads",
            cycles=2000,
            after=after,
        )(role, in_gate, mid_gate, layer_inputs, mid_halo, inputs_halo, own, halo, outgoing[k],
          received[k], filtered, *after))
    tap_grads, steer_grads = zip(*grads)

    own_channels = channels // seqs
    lines = groups // seqs + pl.cdiv(own_channels, LANES)
    place = lax.axis_index("seq")
    steps = seqs.bit_length() - 1
    bits = jnp.stack([(place >> step) & 1 for step in range(steps)]).astype(jnp.int32)

    def halves(count):
        return [jax.ShapeDtypeStruct((count, lines, LANES), F32)] * 2

    vmem = pl.BlockSpec(memory_space=pltpu.VMEM)
    give, keep = pl.pallas_call(
        functools.partial(pack_kernel, seqs),
        in_specs=[SMEM] + [vmem] * (2 * len(grads)),
        out_specs=[vmem] * 2,
        out_shape=halves(seqs // 2),
        name="pack",
    )(bits, *tap_grads, *steer_grads)
    for step in range(steps):
        route = [(i, i ^ (1 << step)) for i in range(seqs)]
        arrived = lax.ppermute(give, "seq", route)
        if step < steps - 1:
            give, keep = pl.pallas_call(
                functools.partial(fold_kernel, step + 1),
                in_specs=[SMEM, vmem, vmem],
                out_specs=[vmem] * 2,
                out_shape=halves(keep.shape[0] // 2),
                name="fold",
            )(bits, keep, arrived)
    steer_step, filter_step = pl.pallas_call(
        step_kernel,
        in_specs=[SMEM] + [vmem] * 4,
        out_shape=[
            jax.ShapeDtypeStruct((1, own_channels), F32),
            jax.ShapeDtypeStruct((groups // seqs, filt_len), F32),
        ],
        name="step",
    )(role, keep, arrived, steer_second, filter_second[0].T)
    return steer_step, filter_step.T[None]


def solution(mesh):
    in_specs = (
        P("seq", None),
        P("section", "seq", None),
        P("section", "seq", None),
        P("section", "seq", None),
        P("section", None, None),
        P("section", "seq"),
        P("section", None, "seq"),
    )
    out_specs = (P("section", "seq"), P("section", None, "seq"))
    return jax.shard_map(body, mesh=mesh, in_specs=in_specs, out_specs=out_specs, check_vma=False)
```

```python
import functools

import jax
import jax.numpy as jnp
from jax import lax
from jax.experimental import pallas as pl
from jax.experimental.pallas import tpu as pltpu
from jax.sharding import PartitionSpec as P

F32 = jnp.float32
BF16 = jnp.bfloat16
LANES = 128
SUB = 32
CHUNK_EDGES = (0, 3, 6, 7, 8)
HALO_EDGES = (0, 3, 6, 8)


def lane_of(shape):
    return lax.broadcasted_iota(jnp.int32, shape, 1)


def row_of(shape):
    return lax.broadcasted_iota(jnp.int32, shape, 0)


def times(a, b):
    return (a.astype(F32) * b.astype(F32)).astype(BF16)


def turned(x):
    return pltpu.roll(x, LANES // 2, 1)


def spread(x, x_turned, parity, count):
    low = lane_of((count, LANES)) < LANES // 2
    natural, other = (x, x_turned) if parity == 0 else (x_turned, x)
    tiles = []
    for first in (0, 2 * SUB):
        tiles.append(jnp.where(low, natural[first : first + count], other[first + SUB : first + SUB + count]))
    return jnp.concatenate(tiles, 1)


def gathered(even, odd):
    low = lane_of((SUB, LANES)) < LANES // 2
    out = []
    for tile in range(2):
        a = even[:, tile * LANES : (tile + 1) * LANES]
        b = odd[:, tile * LANES : (tile + 1) * LANES]
        out.append(jnp.where(low, a, turned(b)))
        out.append(jnp.where(low, turned(a), b))
    return jnp.concatenate(out, 0)


def in_order(reverse, own, halo):
    return jnp.concatenate([jnp.where(reverse, halo, own), jnp.where(reverse, own, halo)], 0)


def diagonal_sums(blocks):
    tiles = []
    for block in blocks:
        tile = block[:8]
        for first in range(8, SUB, 8):
            tile = tile + pltpu.roll(block[first : first + 8], LANES - first, 1)
        tiles.append(tile)
    row = row_of((8, LANES))
    for fold in (4, 2, 1):
        upper = row % (2 * fold) < fold
        tiles = [
            jnp.where(upper, a, pltpu.roll(b, fold, 0))
            + pltpu.roll(jnp.where(upper, pltpu.roll(a, 8 - fold, 0), b), LANES - fold, 1)
            for a, b in zip(tiles[:fold], tiles[fold:])
        ]
    return tiles[0]


def near(reverse_int, shape):
    return lane_of(shape) - row_of(shape) >= reverse_int


def tap_matrix(reverse, taps_by_group):
    taps = taps_by_group.shape[0]
    source = row_of((taps, taps))
    target = lane_of((taps, taps))
    mirrored = jnp.where(source == 0, 0, taps - source)
    pick = jnp.where(target == jnp.where(reverse, mirrored, source), 1.0, 0.0)
    return pick, taps


def weigh_kernel(role, gate, incoming, out):
    @pl.when(role[0] == 0)
    def _():
        out[...] = times(gate[...], incoming[...])


def first_weigh_kernel(block, role, gate, incoming, out, gate_part, incoming_part, sems):
    @pl.when(role[0] == 0)
    def _():
        tiles = [pl.ds(at, block) for at in range(0, out.shape[1], block)]
        copies = [
            [
                pltpu.make_async_copy(source.at[:, t], part.at[:, t], sems.at[which, i])
                for which, (source, part) in enumerate(((gate, gate_part), (incoming, incoming_part)))
            ]
            for i, t in enumerate(tiles)
        ]
        for pair in copies:
            for copy in pair:
                copy.start()
        for t, pair in zip(tiles, copies):
            for copy in pair:
                copy.wait()
            out[:, t] = times(gate_part[:, t], incoming_part[:, t])


def taps_kernel(role, filters, taps_out):
    pick, _ = tap_matrix(role[0] > 0, filters[...])
    taps_out[...] = lax.dot_general(
        filters[...], pick.astype(BF16), (((0,), (0,)), ((), ())), preferred_element_type=F32
    )


def convolved(reverse, group_size, own, halo, taps, first_group):
    half = LANES // 2
    per_half = half // group_size
    mask = near(int(reverse), (SUB, LANES))
    zero = jnp.zeros((SUB, LANES), F32)
    lane_group = (lane_of((SUB, 2 * LANES)) % half) // group_size
    ext = jnp.concatenate([halo, own] if reverse else [own, halo], 0)
    ext_turned = turned(ext)
    results = []
    for parity in range(2):
        window = spread(ext, ext_turned, parity, own.shape[0] + SUB)
        bands = []
        for g in range(per_half):
            row = taps[pl.ds(first_group + parity * per_half + g, 1), :]
            circ = pltpu.roll(jnp.broadcast_to(row, (SUB, LANES)), 0, 1, stride=1, stride_axis=0)
            band = jnp.concatenate([jnp.where(mask, circ, zero), jnp.where(mask, zero, circ)[:, :SUB]], 1)
            bands.append(band.astype(BF16))
        product = jnp.dot(jnp.concatenate(bands, 0), window, preferred_element_type=F32)
        total = product[:SUB]
        for g in range(1, per_half):
            total = jnp.where(lane_group == g, product[g * SUB : (g + 1) * SUB], total)
        results.append(total)
    return gathered(*results)


def filter_kernel(group_size, role, own, halo, taps, mid, incoming, outgoing):
    @pl.when(role[0] == 0)
    def _():
        for first in range(0, own.shape[1], LANES):
            cols = pl.ds(first, LANES)
            conv = convolved(False, group_size, own[:, cols], halo[:, cols], taps, first // group_size)
            outgoing[:, cols] = (
                incoming[:, cols].astype(F32) + mid[:, cols].astype(F32) * conv
            ).astype(BF16)


def turned_filter_kernel(group_size, role, mid, mid_halo, taps, filtered):
    @pl.when(role[0] > 0)
    def _():
        for first in range(0, mid.shape[1], LANES):
            cols = pl.ds(first, LANES)
            filtered[:, cols] = convolved(True, group_size, mid[:, cols], mid_halo[:, cols], taps, first // group_size)


def grad_kernel(
    group_size, role, gate, mid, inputs, mid_halo, inputs_halo, own, halo, outgoing, received, filtered,
    tap_grad, steer_grad, left, right_own, right_halo,
):
    reverse = role[0] > 0
    width = own.shape[1]
    half = LANES // 2
    per_half = half // group_size

    @pl.when(reverse)
    def _():
        grad = received[...]
        weighted = times(gate[...], grad)
        left[...] = weighted
        right_own[...] = times(mid[...], inputs[...])
        right_halo[...] = times(mid_halo[...], inputs_halo[...])
        grad_in = grad.astype(F32) + weighted.astype(F32) * filtered[...]
        steer_grad[...] = jnp.sum(grad_in, 0, keepdims=True)

    @pl.when(jnp.logical_not(reverse))
    def _():
        left[...] = times(mid[...], inputs[...])
        right_own[...] = own[...]
        right_halo[...] = halo[...]
        steer_grad[...] = jnp.sum(outgoing[...].astype(F32), 0, keepdims=True)

    mask = near(role[0], (SUB, LANES))
    lane_group = (lane_of((SUB, 2 * LANES)) % half) // group_size
    nothing = jnp.zeros((SUB, 2 * LANES), BF16)
    for pair in range(width // LANES):
        cols = pl.ds(pair * LANES, LANES)
        ext = in_order(reverse, right_own[:, cols], right_halo[:, cols])
        ext_turned = turned(ext)
        rows = left[:, cols]
        rows_turned = turned(rows)
        blocks = []
        for parity in range(2):
            window = spread(ext, ext_turned, parity, own.shape[0] + SUB)
            short = spread(rows, rows_turned, parity, SUB)
            lhs = jnp.concatenate(
                [jnp.where(lane_group == g, short, nothing) for g in range(per_half)], 0
            )
            product = lax.dot_general(lhs, window, (((1,), (1,)), ((), ())), preferred_element_type=F32)
            for g in range(per_half):
                block = product[g * SUB : (g + 1) * SUB]
                late = jnp.concatenate([block[:, LANES:], jnp.zeros((SUB, LANES - SUB), F32)], 1)
                blocks.append(jnp.where(mask, block[:, :LANES], late))
        tap_grad[pl.ds(8 * pair, 8), :] = diagonal_sums(blocks)


def halves_of(place, step, zero, one):
    mine = (place[0] >> step) & 1 > 0
    return jnp.where(mine, zero, one), jnp.where(mine, one, zero)


def pack_kernel(owners, place, *refs):
    count = (len(refs) - 2) // 2
    taps, steers, (give, keep) = refs[:count], refs[count : 2 * count], refs[2 * count :]
    groups = sum(ref.shape[0] for ref in taps) // owners
    channels = sum(ref.shape[1] for ref in steers) // owners

    def part(parts, axis, owner, size):
        at = owner * size
        for ref in parts:
            if at < ref.shape[axis]:
                return ref[at : at + size, :] if axis == 0 else ref[:, at : at + size]
            at -= ref.shape[axis]

    def packed(owner):
        steer = part(steers, 1, owner, channels)
        lines = [steer[:, at : at + LANES] for at in range(0, channels, LANES)]
        short = LANES - lines[-1].shape[1]
        if short > 0:
            lines[-1] = jnp.concatenate([lines[-1], jnp.zeros((1, short), F32)], 1)
        return [part(taps, 0, owner, groups)] + lines

    order = reversed_bits(owners)
    for i, (low, high) in enumerate(zip(order[: owners // 2], order[owners // 2 :])):
        at = 0
        for zero, one in zip(packed(low), packed(high)):
            lines = zero.shape[0]
            give[i, pl.ds(at, lines), :], keep[i, pl.ds(at, lines), :] = halves_of(place, 0, zero, one)
            at += lines


def reversed_bits(count):
    order = [0]
    while len(order) < count:
        order = [2 * i for i in order] + [2 * i + 1 for i in order]
    return order


def fold_kernel(step, place, kept, arrived, give, keep):
    count = give.shape[0]
    for i in range(count):
        zero = kept[i] + arrived[i]
        one = kept[count + i] + arrived[count + i]
        give[i], keep[i] = halves_of(place, step, zero, one)


def step_kernel(role, kept, arrived, steer_second, filter_second, steer_out, filter_out):
    total = kept[0] + arrived[0]
    groups = filter_second.shape[0]
    tap_grad = total[:groups]
    lane = lane_of(tap_grad.shape)
    mirrored = jnp.where(lane == 0, 0, tap_grad.shape[1] - lane)
    tap_grad = jnp.take_along_axis(tap_grad, jnp.where(role[0] > 0, mirrored, lane), axis=1)
    filter_out[...] = tap_grad / jnp.sqrt(filter_second[...] + tap_grad * tap_grad)
    channels = steer_out.shape[1]
    for row in range(pl.cdiv(channels, LANES)):
        cols = min(LANES, channels - row * LANES)
        at = pl.ds(row * LANES, cols)
        grad = total[groups + row : groups + row + 1, :cols]
        steer_out[:, at] = grad / jnp.sqrt(steer_second[:, at] + grad * grad)


def spec(rows, width, first=0):
    return pl.BlockSpec((rows, width), lambda i: (0, i + first))


SMEM = pl.BlockSpec(memory_space=pltpu.SMEM)
ANY = pl.BlockSpec(memory_space=pl.ANY)
SMALL = pltpu.CompilerParams(vmem_limit_bytes=4 * 1024 * 1024)


def call(kernel, grid, in_specs, out_specs, out_shape, scratch=(), name=None, cycles=100, after=()):
    count = len(in_specs)

    def with_after(*refs):
        kernel(*refs[:count], *refs[count + len(after) :])

    return pl.pallas_call(
        with_after,
        grid=grid,
        in_specs=list(in_specs) + [ANY] * len(after),
        out_specs=out_specs,
        out_shape=out_shape,
        scratch_shapes=list(scratch),
        compiler_params=pltpu.CompilerParams(vmem_limit_bytes=16 * 1024 * 1024),
        cost_estimate=pl.CostEstimate(flops=cycles, bytes_accessed=0, transcendentals=0),
        name=name,
    )


def body(cotangent, in_gate, mid_gate, layer_inputs, filters, steer_second, filter_second):
    in_gate, mid_gate, layer_inputs = in_gate[0], mid_gate[0], layer_inputs[0]
    rows, channels = in_gate.shape
    filt_len, groups = filters.shape[1:]
    group_size = channels // groups
    sections, seqs = lax.axis_size("section"), lax.axis_size("seq")
    my_section = lax.axis_index("section")
    role = (my_section == 0).astype(jnp.int32).reshape(1)

    edges = [channels * eighths // 8 for eighths in CHUNK_EDGES]
    bounds = list(zip(edges[:-1], edges[1:]))
    block = channels // 8
    block_groups = block // group_size
    behind = [(seqs * s + i, seqs * s + i - 1) for s in range(1, sections) for i in range(1, seqs)]
    ahead = [(i, i + 1) for i in range(seqs - 1)]
    down = [(s, s - 1) for s in range(1, sections)]

    def bf16(width_of):
        return jax.ShapeDtypeStruct((rows, width_of), BF16)

    def weigh(incoming, first, last, offset, after):
        return call(
            weigh_kernel,
            ((last - first) // block,),
            [SMEM, spec(rows, block, first // block), spec(rows, block, (first - offset) // block)],
            spec(rows, block),
            bf16(last - first),
            name="weigh",
            after=after,
        )(role, in_gate, incoming, *after)

    def first_weigh(last):
        part = pltpu.VMEM((rows, last), BF16)
        return pl.pallas_call(
            functools.partial(first_weigh_kernel, block),
            in_specs=[SMEM] + [pl.BlockSpec(memory_space=pl.ANY)] * 2,
            out_specs=pl.BlockSpec(memory_space=pltpu.VMEM),
            out_shape=bf16(last),
            scratch_shapes=[part, part, pltpu.SemaphoreType.DMA((2, last // block))],
            compiler_params=SMALL,
            name="first_weigh",
        )(role, *[pltpu.with_memory_space_constraint(a, pltpu.HBM) for a in (in_gate, cotangent)])

    taps = call(
        taps_kernel,
        (1,),
        [SMEM, pl.BlockSpec((filt_len, groups), lambda i: (0, 0))],
        pl.BlockSpec((groups, filt_len), lambda i: (0, 0)),
        jax.ShapeDtypeStruct((groups, filt_len), F32),
        name="taps",
    )(role, filters[0])
    group_spec = lambda first: pl.BlockSpec((block_groups, filt_len), lambda i: (i + first, 0))

    incoming = [(cotangent, 0)] * len(bounds)
    for hop in range(sections - 1):
        split = [channels * eighths // 8 for eighths in HALO_EDGES] if hop == 0 else edges
        starts, ends = split[:-1], split[1:]
        owns = []
        for first, last in zip(starts, ends):
            array, offset = next(entry for entry, edge in zip(incoming, edges) if edge == first)
            if hop == 0 and first == 0:
                owns.append(first_weigh(last))
            else:
                owns.append(weigh(array, first, last, offset, tuple(owns[-1:])))
        if hop == 0:
            mid_sent, inputs_sent, _ = lax.optimization_barrier((mid_gate, layer_inputs, owns[0]))
            mid_halo = lax.ppermute(mid_sent, ("section", "seq"), ahead)
            inputs_halo = lax.ppermute(inputs_sent, ("section", "seq"), ahead)
        halos = [lax.ppermute(own, ("section", "seq"), behind) for own in owns]
        sources, outgoing, received = [], [], []
        for k, (first, last) in enumerate(bounds):
            part = max(i for i, start in enumerate(starts) if start <= first)
            at = (first - starts[part]) // block
            array, offset = incoming[k]
            before = tuple(outgoing[-1:])
            out = call(
                functools.partial(filter_kernel, group_size),
                ((last - first) // block,),
                [SMEM, spec(rows, block, at), spec(rows, block, at), group_spec(first // block),
                 spec(rows, block, first // block), spec(rows, block, (first - offset) // block)],
                spec(rows, block),
                bf16(last - first),
                name="filter",
                cycles=1000,
                after=before,
            )(role, owns[part], halos[part], taps, mid_gate, array, *before)
            sources.append((owns[part], halos[part], at))
            outgoing.append(out)
            received.append(lax.ppermute(out, "section", down))
        top = my_section == sections - 1
        incoming = [
            (jnp.where(top, cotangent[:, first:last], arrived), first)
            for (first, last), arrived in zip(bounds, received)
        ]

    filtered = []
    for first, last in bounds:
        after = tuple(outgoing[-1:]) + tuple(filtered[-1:])
        filtered.append(call(
            functools.partial(turned_filter_kernel, group_size),
            ((last - first) // block,),
            [SMEM, spec(rows, block, first // block), spec(rows, block, first // block), group_spec(first // block)],
            spec(rows, block),
            jax.ShapeDtypeStruct((rows, last - first), F32),
            name="turned_filter",
            cycles=1000,
            after=after,
        )(role, mid_gate, mid_halo, taps, *after))

    grads = []
    for k, (first, last) in enumerate(bounds):
        own, halo, at = sources[k]
        width = last - first
        here = spec(rows, block, first // block)
        after = tuple(grads[-1][:1] if grads else ())
        grads.append(call(
            functools.partial(grad_kernel, group_size),
            (width // block,),
            [SMEM, here, here, here, here, here, spec(rows, block, at), spec(rows, block, at)]
            + [spec(rows, block)] * 3,
            [group_spec(0), pl.BlockSpec((1, block), lambda i: (0, i))],
            [jax.ShapeDtypeStruct((width // group_size, filt_len), F32), jax.ShapeDtypeStruct((1, width), F32)],
            scratch=[pltpu.VMEM((rows, block), BF16)] * 3,
            name="grads",
            cycles=2000,
            after=after,
        )(role, in_gate, mid_gate, layer_inputs, mid_halo, inputs_halo, own, halo, outgoing[k],
          received[k], filtered[k], *after))
    tap_grads, steer_grads = zip(*grads)

    own_channels = channels // seqs
    lines = groups // seqs + pl.cdiv(own_channels, LANES)
    place = lax.axis_index("seq").reshape(1)
    steps = seqs.bit_length() - 1

    def halves(count):
        return [jax.ShapeDtypeStruct((count, lines, LANES), F32)] * 2

    vmem = pl.BlockSpec(memory_space=pltpu.VMEM)
    give, keep = pl.pallas_call(
        functools.partial(pack_kernel, seqs),
        in_specs=[SMEM] + [vmem] * (2 * len(grads)),
        out_specs=[vmem] * 2,
        out_shape=halves(seqs // 2),
        compiler_params=SMALL,
        name="pack",
    )(place, *tap_grads, *steer_grads)
    for step in range(steps):
        route = [(i, i ^ (1 << step)) for i in range(seqs)]
        arrived = lax.ppermute(give, "seq", route)
        if step < steps - 1:
            give, keep = pl.pallas_call(
                functools.partial(fold_kernel, step + 1),
                in_specs=[SMEM, vmem, vmem],
                out_specs=[vmem] * 2,
                out_shape=halves(keep.shape[0] // 2),
                compiler_params=SMALL,
                name="fold",
            )(place, keep, arrived)
    steer_step, filter_step = pl.pallas_call(
        step_kernel,
        in_specs=[SMEM] + [vmem] * 4,
        out_shape=[
            jax.ShapeDtypeStruct((1, own_channels), F32),
            jax.ShapeDtypeStruct((groups // seqs, filt_len), F32),
        ],
        compiler_params=SMALL,
        name="step",
    )(role, keep, arrived, steer_second, filter_second[0].T)
    return steer_step, filter_step.T[None]


def solution(mesh):
    in_specs = (
        P("seq", None),
        P("section", "seq", None),
        P("section", "seq", None),
        P("section", "seq", None),
        P("section", None, None),
        P("section", "seq"),
        P("section", None, "seq"),
    )
    out_specs = (P("section", "seq"), P("section", None, "seq"))
    return jax.shard_map(body, mesh=mesh, in_specs=in_specs, out_specs=out_specs, check_vma=False)
```

```python
import functools

import jax
import jax.numpy as jnp
from jax import lax
from jax.experimental import pallas as pl
from jax.experimental.pallas import tpu as pltpu
from jax.sharding import PartitionSpec as P

F32 = jnp.float32
BF16 = jnp.bfloat16
LANES = 128
SUB = 32
CHUNK_EDGES = (0, 2, 4, 6, 7, 8)
HALO_EDGES = (0, 2, 4, 6, 8)


def lane_of(shape):
    return lax.broadcasted_iota(jnp.int32, shape, 1)


def row_of(shape):
    return lax.broadcasted_iota(jnp.int32, shape, 0)


def first_section(role):
    return (role[0] & 1) > 0


def times(a, b):
    return (a.astype(F32) * b.astype(F32)).astype(BF16)


def turned(x):
    return pltpu.roll(x, LANES // 2, 1)


def spread(x, x_turned, parity, count):
    low = lane_of((count, LANES)) < LANES // 2
    natural, other = (x, x_turned) if parity == 0 else (x_turned, x)
    tiles = []
    for first in (0, 2 * SUB):
        tiles.append(jnp.where(low, natural[first : first + count], other[first + SUB : first + SUB + count]))
    return jnp.concatenate(tiles, 1)


def gathered(even, odd):
    low = lane_of((SUB, LANES)) < LANES // 2
    out = []
    for tile in range(2):
        a = even[:, tile * LANES : (tile + 1) * LANES]
        b = odd[:, tile * LANES : (tile + 1) * LANES]
        out.append(jnp.where(low, a, turned(b)))
        out.append(jnp.where(low, turned(a), b))
    return jnp.concatenate(out, 0)


def in_order(reverse, own, halo):
    return jnp.concatenate([jnp.where(reverse, halo, own), jnp.where(reverse, own, halo)], 0)


def diagonal_sums(blocks):
    tiles = []
    for block in blocks:
        tile = block[:8]
        for first in range(8, SUB, 8):
            tile = tile + pltpu.roll(block[first : first + 8], LANES - first, 1)
        tiles.append(tile)
    row = row_of((8, LANES))
    for fold in (4, 2, 1):
        upper = row % (2 * fold) < fold
        tiles = [
            jnp.where(upper, a, pltpu.roll(b, fold, 0))
            + pltpu.roll(jnp.where(upper, pltpu.roll(a, 8 - fold, 0), b), LANES - fold, 1)
            for a, b in zip(tiles[:fold], tiles[fold:])
        ]
    return tiles[0]


def near(reverse_int, shape):
    return lane_of(shape) - row_of(shape) >= reverse_int


def tap_matrix(reverse, taps_by_group):
    taps = taps_by_group.shape[0]
    source = row_of((taps, taps))
    target = lane_of((taps, taps))
    mirrored = jnp.where(source == 0, 0, taps - source)
    pick = jnp.where(target == jnp.where(reverse, mirrored, source), 1.0, 0.0)
    return pick, taps


def weigh_kernel(role, gate, incoming, out):
    @pl.when(jnp.logical_not(first_section(role)))
    def _():
        out[...] = times(gate[...], incoming[...])


def first_weigh_kernel(block, role, gate, incoming, out, gate_part, incoming_part, sems):
    @pl.when(jnp.logical_not(first_section(role)))
    def _():
        tiles = [pl.ds(at, block) for at in range(0, out.shape[1], block)]
        copies = [
            [
                pltpu.make_async_copy(source.at[:, t], part.at[:, t], sems.at[which, i])
                for which, (source, part) in enumerate(((gate, gate_part), (incoming, incoming_part)))
            ]
            for i, t in enumerate(tiles)
        ]
        for pair in copies:
            for copy in pair:
                copy.start()
        for t, pair in zip(tiles, copies):
            for copy in pair:
                copy.wait()
            out[:, t] = times(gate_part[:, t], incoming_part[:, t])


def taps_kernel(role, filters, taps_out):
    pick, _ = tap_matrix(first_section(role), filters[...])
    taps_out[...] = lax.dot_general(
        filters[...], pick.astype(BF16), (((0,), (0,)), ((), ())), preferred_element_type=F32
    )


def convolved(reverse, group_size, own, halo, taps, first_group):
    half = LANES // 2
    per_half = half // group_size
    mask = near(int(reverse), (SUB, LANES))
    zero = jnp.zeros((SUB, LANES), F32)
    lane_group = (lane_of((SUB, 2 * LANES)) % half) // group_size
    ext = jnp.concatenate([halo, own] if reverse else [own, halo], 0)
    ext_turned = turned(ext)
    results = []
    for parity in range(2):
        window = spread(ext, ext_turned, parity, own.shape[0] + SUB)
        bands = []
        for g in range(per_half):
            row = taps[pl.ds(first_group + parity * per_half + g, 1), :]
            circ = pltpu.roll(jnp.broadcast_to(row, (SUB, LANES)), 0, 1, stride=1, stride_axis=0)
            band = jnp.concatenate([jnp.where(mask, circ, zero), jnp.where(mask, zero, circ)[:, :SUB]], 1)
            bands.append(band.astype(BF16))
        product = jnp.dot(jnp.concatenate(bands, 0), window, preferred_element_type=F32)
        total = product[:SUB]
        for g in range(1, per_half):
            total = jnp.where(lane_group == g, product[g * SUB : (g + 1) * SUB], total)
        results.append(total)
    return gathered(*results)


def filter_kernel(group_size, role, own, halo, taps, mid, incoming, outgoing):
    @pl.when(jnp.logical_not(first_section(role)))
    def _():
        for first in range(0, own.shape[1], LANES):
            cols = pl.ds(first, LANES)
            conv = convolved(False, group_size, own[:, cols], halo[:, cols], taps, first // group_size)
            outgoing[:, cols] = (
                incoming[:, cols].astype(F32) + mid[:, cols].astype(F32) * conv
            ).astype(BF16)


def turned_filter_kernel(group_size, role, mid, mid_halo, taps, filtered):
    @pl.when(first_section(role))
    def _():
        for first in range(0, mid.shape[1], LANES):
            cols = pl.ds(first, LANES)
            filtered[:, cols] = convolved(True, group_size, mid[:, cols], mid_halo[:, cols], taps, first // group_size)


def grad_kernel(
    group_size, role, gate, mid, inputs, mid_halo, inputs_halo, own, halo, outgoing, received, filtered,
    tap_grad, steer_grad, left, right_own, right_halo,
):
    reverse = first_section(role)
    width = own.shape[1]
    half = LANES // 2
    per_half = half // group_size

    @pl.when(reverse)
    def _():
        grad = received[...]
        weighted = times(gate[...], grad)
        left[...] = weighted
        right_own[...] = times(mid[...], inputs[...])
        right_halo[...] = times(mid_halo[...], inputs_halo[...])
        grad_in = grad.astype(F32) + weighted.astype(F32) * filtered[...]
        steer_grad[...] = jnp.sum(grad_in, 0, keepdims=True)

    @pl.when(jnp.logical_not(reverse))
    def _():
        left[...] = times(mid[...], inputs[...])
        right_own[...] = own[...]
        right_halo[...] = halo[...]
        steer_grad[...] = jnp.sum(outgoing[...].astype(F32), 0, keepdims=True)

    mask = near(role[0] & 1, (SUB, LANES))
    lane_group = (lane_of((SUB, 2 * LANES)) % half) // group_size
    nothing = jnp.zeros((SUB, 2 * LANES), BF16)
    for pair in range(width // LANES):
        cols = pl.ds(pair * LANES, LANES)
        ext = in_order(reverse, right_own[:, cols], right_halo[:, cols])
        ext_turned = turned(ext)
        rows = left[:, cols]
        rows_turned = turned(rows)
        blocks = []
        for parity in range(2):
            window = spread(ext, ext_turned, parity, own.shape[0] + SUB)
            short = spread(rows, rows_turned, parity, SUB)
            lhs = jnp.concatenate(
                [jnp.where(lane_group == g, short, nothing) for g in range(per_half)], 0
            )
            product = lax.dot_general(lhs, window, (((1,), (1,)), ((), ())), preferred_element_type=F32)
            for g in range(per_half):
                block = product[g * SUB : (g + 1) * SUB]
                late = jnp.concatenate([block[:, LANES:], jnp.zeros((SUB, LANES - SUB), F32)], 1)
                blocks.append(jnp.where(mask, block[:, :LANES], late))
        tap_grad[pl.ds(8 * pair, 8), :] = diagonal_sums(blocks)


def halves_of(role, step, zero, one):
    mine = (role[0] >> (step + 1)) & 1 > 0
    return jnp.where(mine, zero, one), jnp.where(mine, one, zero)


def pack_kernel(owners, role, *refs):
    count = (len(refs) - 2) // 2
    taps, steers, (give, keep) = refs[:count], refs[count : 2 * count], refs[2 * count :]
    groups = sum(ref.shape[0] for ref in taps) // owners
    channels = sum(ref.shape[1] for ref in steers) // owners

    def part(parts, axis, owner, size):
        at = owner * size
        for ref in parts:
            if at < ref.shape[axis]:
                return ref[at : at + size, :] if axis == 0 else ref[:, at : at + size]
            at -= ref.shape[axis]

    def packed(owner):
        steer = part(steers, 1, owner, channels)
        lines = [steer[:, at : at + LANES] for at in range(0, channels, LANES)]
        short = LANES - lines[-1].shape[1]
        if short > 0:
            lines[-1] = jnp.concatenate([lines[-1], jnp.zeros((1, short), F32)], 1)
        return [part(taps, 0, owner, groups)] + lines

    order = reversed_bits(owners)
    for i, (low, high) in enumerate(zip(order[: owners // 2], order[owners // 2 :])):
        at = 0
        for zero, one in zip(packed(low), packed(high)):
            lines = zero.shape[0]
            give[i, pl.ds(at, lines), :], keep[i, pl.ds(at, lines), :] = halves_of(role, 0, zero, one)
            at += lines


def reversed_bits(count):
    order = [0]
    while len(order) < count:
        order = [2 * i for i in order] + [2 * i + 1 for i in order]
    return order


def fold_kernel(step, role, kept, arrived, give, keep):
    count = give.shape[0]
    for i in range(count):
        zero = kept[i] + arrived[i]
        one = kept[count + i] + arrived[count + i]
        give[i], keep[i] = halves_of(role, step, zero, one)


def step_kernel(role, kept, arrived, steer_second, filter_second, steer_out, filter_out):
    total = kept[0] + arrived[0]
    groups = filter_second.shape[0]
    tap_grad = total[:groups]
    lane = lane_of(tap_grad.shape)
    mirrored = jnp.where(lane == 0, 0, tap_grad.shape[1] - lane)
    tap_grad = jnp.take_along_axis(tap_grad, jnp.where(first_section(role), mirrored, lane), axis=1)
    filter_out[...] = tap_grad / jnp.sqrt(filter_second[...] + tap_grad * tap_grad)
    channels = steer_out.shape[1]
    for row in range(pl.cdiv(channels, LANES)):
        cols = min(LANES, channels - row * LANES)
        at = pl.ds(row * LANES, cols)
        grad = total[groups + row : groups + row + 1, :cols]
        steer_out[:, at] = grad / jnp.sqrt(steer_second[:, at] + grad * grad)


def spec(rows, width, first=0):
    return pl.BlockSpec((rows, width), lambda i: (0, i + first))


SMEM = pl.BlockSpec(memory_space=pltpu.SMEM)
ANY = pl.BlockSpec(memory_space=pl.ANY)
SMALL = pltpu.CompilerParams(vmem_limit_bytes=4 * 1024 * 1024)


def call(kernel, grid, in_specs, out_specs, out_shape, scratch=(), name=None, cycles=100, after=()):
    count = len(in_specs)

    def with_after(*refs):
        kernel(*refs[:count], *refs[count + len(after) :])

    return pl.pallas_call(
        with_after,
        grid=grid,
        in_specs=list(in_specs) + [ANY] * len(after),
        out_specs=out_specs,
        out_shape=out_shape,
        scratch_shapes=list(scratch),
        compiler_params=pltpu.CompilerParams(vmem_limit_bytes=16 * 1024 * 1024),
        cost_estimate=pl.CostEstimate(flops=cycles, bytes_accessed=0, transcendentals=0),
        name=name,
    )


def body(cotangent, in_gate, mid_gate, layer_inputs, filters, steer_second, filter_second):
    in_gate, mid_gate, layer_inputs = in_gate[0], mid_gate[0], layer_inputs[0]
    rows, channels = in_gate.shape
    filt_len, groups = filters.shape[1:]
    group_size = channels // groups
    sections, seqs = lax.axis_size("section"), lax.axis_size("seq")
    my_section = lax.axis_index("section")
    role = (2 * lax.axis_index("seq") + (my_section == 0)).astype(jnp.int32).reshape(1)

    edges = [channels * eighths // 8 for eighths in CHUNK_EDGES]
    bounds = list(zip(edges[:-1], edges[1:]))
    block = channels // 8
    block_groups = block // group_size
    behind = [(seqs * s + i, seqs * s + i - 1) for s in range(1, sections) for i in range(1, seqs)]
    ahead = [(i, i + 1) for i in range(seqs - 1)]
    down = [(s, s - 1) for s in range(1, sections)]

    def bf16(width_of):
        return jax.ShapeDtypeStruct((rows, width_of), BF16)

    def weigh(incoming, first, last, offset, after):
        return call(
            weigh_kernel,
            ((last - first) // block,),
            [SMEM, spec(rows, block, first // block), spec(rows, block, (first - offset) // block)],
            spec(rows, block),
            bf16(last - first),
            name="weigh",
            after=after,
        )(role, in_gate, incoming, *after)

    def first_weigh(last):
        part = pltpu.VMEM((rows, last), BF16)
        return pl.pallas_call(
            functools.partial(first_weigh_kernel, block),
            in_specs=[SMEM] + [pl.BlockSpec(memory_space=pl.ANY)] * 2,
            out_specs=pl.BlockSpec(memory_space=pltpu.VMEM),
            out_shape=bf16(last),
            scratch_shapes=[part, part, pltpu.SemaphoreType.DMA((2, last // block))],
            compiler_params=SMALL,
            name="first_weigh",
        )(role, *[pltpu.with_memory_space_constraint(a, pltpu.HBM) for a in (in_gate, cotangent)])

    taps = call(
        taps_kernel,
        (1,),
        [SMEM, pl.BlockSpec((filt_len, groups), lambda i: (0, 0))],
        pl.BlockSpec((groups, filt_len), lambda i: (0, 0)),
        jax.ShapeDtypeStruct((groups, filt_len), F32),
        name="taps",
    )(role, filters[0])
    group_spec = lambda first: pl.BlockSpec((block_groups, filt_len), lambda i: (i + first, 0))

    incoming = [(cotangent, 0)] * len(bounds)
    for hop in range(sections - 1):
        split = [channels * eighths // 8 for eighths in HALO_EDGES] if hop == 0 else edges
        starts, ends = split[:-1], split[1:]
        owns = []
        for first, last in zip(starts, ends):
            array, offset = next(entry for entry, edge in zip(incoming, edges) if edge == first)
            if hop == 0 and first == 0:
                owns.append(first_weigh(last))
            else:
                owns.append(weigh(array, first, last, offset, tuple(owns[-1:])))
        if hop == 0:
            mid_sent, inputs_sent, _ = lax.optimization_barrier((mid_gate, layer_inputs, owns[0]))
            mid_halo = lax.ppermute(mid_sent, ("section", "seq"), ahead)
            inputs_halo = lax.ppermute(inputs_sent, ("section", "seq"), ahead)
        halos = [lax.ppermute(own, ("section", "seq"), behind) for own in owns]
        sources, outgoing, received = [], [], []
        for k, (first, last) in enumerate(bounds):
            part = max(i for i, start in enumerate(starts) if start <= first)
            at = (first - starts[part]) // block
            array, offset = incoming[k]
            before = tuple(outgoing[-1:])
            out = call(
                functools.partial(filter_kernel, group_size),
                ((last - first) // block,),
                [SMEM, spec(rows, block, at), spec(rows, block, at), group_spec(first // block),
                 spec(rows, block, first // block), spec(rows, block, (first - offset) // block)],
                spec(rows, block),
                bf16(last - first),
                name="filter",
                cycles=1000,
                after=before,
            )(role, owns[part], halos[part], taps, mid_gate, array, *before)
            sources.append((owns[part], halos[part], at))
            outgoing.append(out)
            received.append(lax.ppermute(out, "section", down))
        top = my_section == sections - 1
        incoming = [
            (jnp.where(top, cotangent[:, first:last], arrived), first)
            for (first, last), arrived in zip(bounds, received)
        ]

    filtered = []
    for first, last in bounds:
        after = tuple(outgoing[-1:]) + tuple(filtered[-1:])
        filtered.append(call(
            functools.partial(turned_filter_kernel, group_size),
            ((last - first) // block,),
            [SMEM, spec(rows, block, first // block), spec(rows, block, first // block), group_spec(first // block)],
            spec(rows, block),
            jax.ShapeDtypeStruct((rows, last - first), F32),
            name="turned_filter",
            cycles=1000,
            after=after,
        )(role, mid_gate, mid_halo, taps, *after))

    grads = []
    for k, (first, last) in enumerate(bounds):
        own, halo, at = sources[k]
        width = last - first
        here = spec(rows, block, first // block)
        after = tuple(grads[-1][:1] if grads else ())
        grads.append(call(
            functools.partial(grad_kernel, group_size),
            (width // block,),
            [SMEM, here, here, here, here, here, spec(rows, block, at), spec(rows, block, at)]
            + [spec(rows, block)] * 3,
            [group_spec(0), pl.BlockSpec((1, block), lambda i: (0, i))],
            [jax.ShapeDtypeStruct((width // group_size, filt_len), F32), jax.ShapeDtypeStruct((1, width), F32)],
            scratch=[pltpu.VMEM((rows, block), BF16)] * 3,
            name="grads",
            cycles=2000,
            after=after,
        )(role, in_gate, mid_gate, layer_inputs, mid_halo, inputs_halo, own, halo, outgoing[k],
          received[k], filtered[k], *after))
    tap_grads, steer_grads = zip(*grads)

    own_channels = channels // seqs
    lines = groups // seqs + pl.cdiv(own_channels, LANES)
    steps = seqs.bit_length() - 1

    def halves(count):
        return [jax.ShapeDtypeStruct((count, lines, LANES), F32)] * 2

    vmem = pl.BlockSpec(memory_space=pltpu.VMEM)
    give, keep = pl.pallas_call(
        functools.partial(pack_kernel, seqs),
        in_specs=[SMEM] + [vmem] * (2 * len(grads)),
        out_specs=[vmem] * 2,
        out_shape=halves(seqs // 2),
        compiler_params=SMALL,
        name="pack",
    )(role, *tap_grads, *steer_grads)
    for step in range(steps):
        route = [(i, i ^ (1 << step)) for i in range(seqs)]
        arrived = lax.ppermute(give, "seq", route)
        if step < steps - 1:
            give, keep = pl.pallas_call(
                functools.partial(fold_kernel, step + 1),
                in_specs=[SMEM, vmem, vmem],
                out_specs=[vmem] * 2,
                out_shape=halves(keep.shape[0] // 2),
                compiler_params=SMALL,
                name="fold",
            )(role, keep, arrived)
    steer_step, filter_step = pl.pallas_call(
        step_kernel,
        in_specs=[SMEM] + [vmem] * 4,
        out_shape=[
            jax.ShapeDtypeStruct((1, own_channels), F32),
            jax.ShapeDtypeStruct((groups // seqs, filt_len), F32),
        ],
        compiler_params=SMALL,
        name="step",
    )(role, keep, arrived, steer_second, filter_second[0].T)
    return steer_step, filter_step.T[None]


def solution(mesh):
    in_specs = (
        P("seq", None),
        P("section", "seq", None),
        P("section", "seq", None),
        P("section", "seq", None),
        P("section", None, None),
        P("section", "seq"),
        P("section", None, "seq"),
    )
    out_specs = (P("section", "seq"), P("section", None, "seq"))
    return jax.shard_map(body, mesh=mesh, in_specs=in_specs, out_specs=out_specs, check_vma=False)
```

```python
import functools

import jax
import jax.numpy as jnp
from jax import lax
from jax.experimental import pallas as pl
from jax.experimental.pallas import tpu as pltpu
from jax.sharding import PartitionSpec as P

F32 = jnp.float32
BF16 = jnp.bfloat16
LANES = 128
SUB = 32
CHUNK_EDGES = (0, 2, 4, 5, 6, 8)
HALO_EDGES = (0, 4, 8)


def lane_of(shape):
    return lax.broadcasted_iota(jnp.int32, shape, 1)


def row_of(shape):
    return lax.broadcasted_iota(jnp.int32, shape, 0)


def first_section(role):
    return (role[0] & 1) > 0


def second_section(role):
    return (role[0] & 2) > 0


def times(a, b):
    return (a.astype(F32) * b.astype(F32)).astype(BF16)


def turned(x):
    return pltpu.roll(x, LANES // 2, 1)


def spread(x, x_turned, parity, count):
    low = lane_of((count, LANES)) < LANES // 2
    natural, other = (x, x_turned) if parity == 0 else (x_turned, x)
    tiles = []
    for first in (0, 2 * SUB):
        tiles.append(jnp.where(low, natural[first : first + count], other[first + SUB : first + SUB + count]))
    return jnp.concatenate(tiles, 1)


def gathered(even, odd):
    low = lane_of((SUB, LANES)) < LANES // 2
    out = []
    for tile in range(2):
        a = even[:, tile * LANES : (tile + 1) * LANES]
        b = odd[:, tile * LANES : (tile + 1) * LANES]
        out.append(jnp.where(low, a, turned(b)))
        out.append(jnp.where(low, turned(a), b))
    return jnp.concatenate(out, 0)


def in_order(reverse, own, halo):
    return jnp.concatenate([jnp.where(reverse, halo, own), jnp.where(reverse, own, halo)], 0)


def diagonal_sums(blocks):
    tiles = []
    for block in blocks:
        tile = block[:8]
        for first in range(8, SUB, 8):
            tile = tile + pltpu.roll(block[first : first + 8], LANES - first, 1)
        tiles.append(tile)
    row = row_of((8, LANES))
    for fold in (4, 2, 1):
        upper = row % (2 * fold) < fold
        tiles = [
            jnp.where(upper, a, pltpu.roll(b, fold, 0))
            + pltpu.roll(jnp.where(upper, pltpu.roll(a, 8 - fold, 0), b), LANES - fold, 1)
            for a, b in zip(tiles[:fold], tiles[fold:])
        ]
    return tiles[0]


def near(reverse_int, shape):
    return lane_of(shape) - row_of(shape) >= reverse_int


def tap_matrix(reverse, taps_by_group):
    taps = taps_by_group.shape[0]
    source = row_of((taps, taps))
    target = lane_of((taps, taps))
    mirrored = jnp.where(source == 0, 0, taps - source)
    pick = jnp.where(target == jnp.where(reverse, mirrored, source), 1.0, 0.0)
    return pick, taps


def weigh_kernel(own_blocks, role, gate, incoming, raw, out):
    width = out.shape[1]
    step = pl.program_id(0)
    foreign = jnp.logical_and(second_section(role), step >= own_blocks)

    @pl.when(foreign)
    def _():
        at = pl.multiple_of(jnp.maximum(step - own_blocks, 0) * width, width)
        out[...] = times(raw[:, pl.ds(at, width)], incoming[...])

    @pl.when(jnp.logical_not(jnp.logical_or(foreign, first_section(role))))
    def _():
        out[...] = times(gate[...], incoming[...])


def first_weigh_kernel(block, first_raw, role, gate, incoming, mid, filters, out, raw, gate_part, incoming_part, sems):
    channels = gate.shape[1]
    foreign = channels - first_raw
    tap_lanes = raw.shape[1] - 2 * foreign
    groups = filters.shape[1]

    @pl.when(jnp.logical_not(first_section(role)))
    def _():
        tiles = [pl.ds(at, block) for at in range(0, out.shape[1], block)]
        copies = [
            [
                pltpu.make_async_copy(source.at[:, t], part.at[:, t], sems.at[which, i])
                for which, (source, part) in enumerate(((gate, gate_part), (incoming, incoming_part)))
            ]
            for i, t in enumerate(tiles)
        ]
        parts = (
            (gate.at[:, pl.ds(first_raw, foreign)], raw.at[:, pl.ds(0, foreign)]),
            (mid.at[:, pl.ds(first_raw, foreign)], raw.at[:, pl.ds(foreign, foreign)]),
            (filters.at[:, pl.ds(groups - tap_lanes, tap_lanes)], raw.at[:, pl.ds(2 * foreign, tap_lanes)]),
        )
        raws = [pltpu.make_async_copy(source, part, sems.at[2, i]) for i, (source, part) in enumerate(parts)]
        for pair in copies:
            for copy in pair:
                copy.start()
        for copy in raws:
            copy.start()
        for t, pair in zip(tiles, copies):
            for copy in pair:
                copy.wait()
            out[:, t] = times(gate_part[:, t], incoming_part[:, t])
        for copy in raws:
            copy.wait()


def taps_kernel(role, filters, taps_out):
    pick, _ = tap_matrix(first_section(role), filters[...])
    taps_out[...] = lax.dot_general(
        filters[...], pick.astype(BF16), (((0,), (0,)), ((), ())), preferred_element_type=F32
    )


def convolved(reverse, group_size, own, halo, taps, first_group):
    half = LANES // 2
    per_half = half // group_size
    mask = near(int(reverse), (SUB, LANES))
    zero = jnp.zeros((SUB, LANES), F32)
    lane_group = (lane_of((SUB, 2 * LANES)) % half) // group_size
    ext = jnp.concatenate([halo, own] if reverse else [own, halo], 0)
    ext_turned = turned(ext)
    results = []
    for parity in range(2):
        window = spread(ext, ext_turned, parity, own.shape[0] + SUB)
        bands = []
        for g in range(per_half):
            row = taps[pl.ds(first_group + parity * per_half + g, 1), :]
            circ = pltpu.roll(jnp.broadcast_to(row, (SUB, LANES)), 0, 1, stride=1, stride_axis=0)
            band = jnp.concatenate([jnp.where(mask, circ, zero), jnp.where(mask, zero, circ)[:, :SUB]], 1)
            bands.append(band.astype(BF16))
        product = jnp.dot(jnp.concatenate(bands, 0), window, preferred_element_type=F32)
        total = product[:SUB]
        for g in range(1, per_half):
            total = jnp.where(lane_group == g, product[g * SUB : (g + 1) * SUB], total)
        results.append(total)
    return gathered(*results)


def filter_kernel(group_size, role, own, halo, taps, mid, incoming, outgoing):
    @pl.when(jnp.logical_not(first_section(role)))
    def _():
        for first in range(0, own.shape[1], LANES):
            cols = pl.ds(first, LANES)
            conv = convolved(False, group_size, own[:, cols], halo[:, cols], taps, first // group_size)
            outgoing[:, cols] = (
                incoming[:, cols].astype(F32) + mid[:, cols].astype(F32) * conv
            ).astype(BF16)


def raw_filter_kernel(group_size, foreign, role, own, halo, taps, mid, incoming, raw, outgoing, raw_taps):
    width = own.shape[1]
    step = pl.program_id(0)
    tap_lanes = raw.shape[1] - 2 * foreign

    def run(own_taps, first_group, gate_of):
        for first in range(0, width, LANES):
            cols = pl.ds(first, LANES)
            conv = convolved(
                False, group_size, own[:, cols], halo[:, cols], own_taps, first_group + first // group_size
            )
            outgoing[:, cols] = (
                incoming[:, cols].astype(F32) + gate_of(first).astype(F32) * conv
            ).astype(BF16)

    @pl.when(second_section(role))
    def _():
        pick = jnp.where(row_of((taps.shape[1],) * 2) == lane_of((taps.shape[1],) * 2), 1.0, 0.0).astype(BF16)
        raw_taps[...] = lax.dot_general(
            raw[:, pl.ds(2 * foreign, tap_lanes)], pick, (((0,), (0,)), ((), ())), preferred_element_type=F32
        )
        skipped = tap_lanes - foreign // group_size
        run(
            raw_taps,
            skipped + step * (width // group_size),
            lambda first: raw[:, pl.ds(pl.multiple_of(foreign + step * width + first, LANES), LANES)],
        )

    @pl.when(jnp.logical_not(jnp.logical_or(first_section(role), second_section(role))))
    def _():
        run(taps, 0, lambda first: mid[:, pl.ds(first, LANES)])


def turned_filter_kernel(group_size, role, mid, mid_halo, taps, filtered):
    @pl.when(first_section(role))
    def _():
        for first in range(0, mid.shape[1], LANES):
            cols = pl.ds(first, LANES)
            filtered[:, cols] = convolved(True, group_size, mid[:, cols], mid_halo[:, cols], taps, first // group_size)


def grad_kernel(
    group_size, role, gate, mid, inputs, mid_halo, inputs_halo, own, halo, outgoing, received, filtered,
    tap_grad, steer_grad, left, right_own, right_halo,
):
    reverse = first_section(role)
    width = own.shape[1]
    half = LANES // 2
    per_half = half // group_size

    @pl.when(reverse)
    def _():
        grad = received[...]
        weighted = times(gate[...], grad)
        left[...] = weighted
        right_own[...] = times(mid[...], inputs[...])
        right_halo[...] = times(mid_halo[...], inputs_halo[...])
        grad_in = grad.astype(F32) + weighted.astype(F32) * filtered[...]
        steer_grad[...] = jnp.sum(grad_in, 0, keepdims=True)

    @pl.when(jnp.logical_not(reverse))
    def _():
        left[...] = times(mid[...], inputs[...])
        right_own[...] = own[...]
        right_halo[...] = halo[...]
        steer_grad[...] = jnp.sum(outgoing[...].astype(F32), 0, keepdims=True)

    mask = near(role[0] & 1, (SUB, LANES))
    lane_group = (lane_of((SUB, 2 * LANES)) % half) // group_size
    nothing = jnp.zeros((SUB, 2 * LANES), BF16)
    for pair in range(width // LANES):
        cols = pl.ds(pair * LANES, LANES)
        ext = in_order(reverse, right_own[:, cols], right_halo[:, cols])
        ext_turned = turned(ext)
        rows = left[:, cols]
        rows_turned = turned(rows)
        blocks = []
        for parity in range(2):
            window = spread(ext, ext_turned, parity, own.shape[0] + SUB)
            short = spread(rows, rows_turned, parity, SUB)
            lhs = jnp.concatenate(
                [jnp.where(lane_group == g, short, nothing) for g in range(per_half)], 0
            )
            product = lax.dot_general(lhs, window, (((1,), (1,)), ((), ())), preferred_element_type=F32)
            for g in range(per_half):
                block = product[g * SUB : (g + 1) * SUB]
                late = jnp.concatenate([block[:, LANES:], jnp.zeros((SUB, LANES - SUB), F32)], 1)
                blocks.append(jnp.where(mask, block[:, :LANES], late))
        tap_grad[pl.ds(8 * pair, 8), :] = diagonal_sums(blocks)


def pack_kernel(owners, *refs):
    count = (len(refs) - 1) // 2
    taps, steers, out = refs[:count], refs[count : 2 * count], refs[-1]
    groups = sum(ref.shape[0] for ref in taps) // owners
    channels = sum(ref.shape[1] for ref in steers) // owners

    def part(parts, axis, at, size):
        for ref in parts:
            if at < ref.shape[axis]:
                return ref[at : at + size, :] if axis == 0 else ref[:, at : at + size]
            at -= ref.shape[axis]

    for owner in range(owners):
        out[owner, pl.ds(0, groups), :] = part(taps, 0, owner * groups, groups)
        for line, at in enumerate(range(0, channels, LANES)):
            size = min(LANES, channels - at)
            steer = part(steers, 1, owner * channels + at, size)
            if size < LANES:
                steer = jnp.concatenate([steer, jnp.zeros((1, LANES - size), F32)], 1)
            out[owner, pl.ds(groups + line, 1), :] = steer


def step_kernel(role, parts, steer_second, filter_second, steer_out, filter_out):
    total = jnp.sum(parts[...], 0)
    groups = filter_second.shape[0]
    tap_grad = total[:groups]
    lane = lane_of(tap_grad.shape)
    mirrored = jnp.where(lane == 0, 0, tap_grad.shape[1] - lane)
    tap_grad = jnp.take_along_axis(tap_grad, jnp.where(first_section(role), mirrored, lane), axis=1)
    filter_out[...] = tap_grad / jnp.sqrt(filter_second[...] + tap_grad * tap_grad)
    channels = steer_out.shape[1]
    for row in range(pl.cdiv(channels, LANES)):
        cols = min(LANES, channels - row * LANES)
        at = pl.ds(row * LANES, cols)
        grad = total[groups + row : groups + row + 1, :cols]
        steer_out[:, at] = grad / jnp.sqrt(steer_second[:, at] + grad * grad)


def spec(rows, width, first=0):
    return pl.BlockSpec((rows, width), lambda i: (0, i + first))


SMEM = pl.BlockSpec(memory_space=pltpu.SMEM)
ANY = pl.BlockSpec(memory_space=pl.ANY)
SMALL = pltpu.CompilerParams(vmem_limit_bytes=4 * 1024 * 1024)


def call(kernel, grid, in_specs, out_specs, out_shape, scratch=(), name=None, cycles=100, after=()):
    count = len(in_specs)

    def with_after(*refs):
        kernel(*refs[:count], *refs[count + len(after) :])

    return pl.pallas_call(
        with_after,
        grid=grid,
        in_specs=list(in_specs) + [ANY] * len(after),
        out_specs=out_specs,
        out_shape=out_shape,
        scratch_shapes=list(scratch),
        compiler_params=pltpu.CompilerParams(vmem_limit_bytes=16 * 1024 * 1024),
        cost_estimate=pl.CostEstimate(flops=cycles, bytes_accessed=0, transcendentals=0),
        name=name,
    )


def body(cotangent, in_gate, mid_gate, layer_inputs, filters, steer_second, filter_second):
    in_gate, mid_gate, layer_inputs = in_gate[0], mid_gate[0], layer_inputs[0]
    rows, channels = in_gate.shape
    filt_len, groups = filters.shape[1:]
    group_size = channels // groups
    sections, seqs = lax.axis_size("section"), lax.axis_size("seq")
    my_section = lax.axis_index("section")
    role = ((my_section == 0) + 2 * (my_section == sections - 2)).astype(jnp.int32).reshape(1)

    edges = [channels * eighths // 8 for eighths in CHUNK_EDGES]
    bounds = list(zip(edges[:-1], edges[1:]))
    block = channels // 8
    block_groups = block // group_size
    behind = [(seqs * s + i, seqs * s + i - 1) for s in range(1, sections) for i in range(1, seqs)]
    below = [(i, i - 1) for i in range(1, seqs)] if sections == 2 else []
    ahead = [(i, i + 1) for i in range(seqs - 1)]
    down = [(s, s - 1) for s in range(1, sections)]

    def bf16(width_of):
        return jax.ShapeDtypeStruct((rows, width_of), BF16)

    def weigh(incoming, first, last, offset, raw, own_blocks, after):
        return call(
            functools.partial(weigh_kernel, own_blocks),
            ((last - first) // block,),
            [SMEM, spec(rows, block, first // block), spec(rows, block, (first - offset) // block),
             pl.BlockSpec(raw.shape, lambda i: (0, 0))],
            spec(rows, block),
            bf16(last - first),
            name="weigh",
            after=after,
        )(role, in_gate, incoming, raw, *after)

    def first_weigh(last):
        part = pltpu.VMEM((rows, last), BF16)
        return pl.pallas_call(
            functools.partial(first_weigh_kernel, block, first_raw),
            in_specs=[SMEM] + [pl.BlockSpec(memory_space=pl.ANY)] * 4,
            out_specs=[pl.BlockSpec(memory_space=pltpu.VMEM)] * 2,
            out_shape=[bf16(last), bf16(2 * foreign + min(groups, LANES))],
            scratch_shapes=[part, part, pltpu.SemaphoreType.DMA((3, max(3, last // block)))],
            compiler_params=SMALL,
            name="first_weigh",
        )(role, *[pltpu.with_memory_space_constraint(a, pltpu.HBM) for a in (in_gate, cotangent, mid_gate, filters[0])])

    taps = call(
        taps_kernel,
        (1,),
        [SMEM, pl.BlockSpec((filt_len, groups), lambda i: (0, 0))],
        pl.BlockSpec((groups, filt_len), lambda i: (0, 0)),
        jax.ShapeDtypeStruct((groups, filt_len), F32),
        name="taps",
    )(role, filters[0])
    first_raw = edges[-2]
    foreign = channels - first_raw
    group_spec = lambda first: pl.BlockSpec((block_groups, filt_len), lambda i: (i + first, 0))

    incoming = [(cotangent, 0)] * len(bounds)
    raws = []
    for hop in range(sections - 1):
        split = [channels * eighths // 8 for eighths in HALO_EDGES] if hop == 0 else edges
        starts, ends = split[:-1], split[1:]
        owns, halos = [], []

        def send_halo(after):
            first, last = starts[len(owns)], ends[len(owns)]
            array, offset = next(entry for entry, edge in zip(incoming, edges) if edge == first)
            if hop == 0 and first == 0:
                own, sent = first_weigh(last)
                owns.append(own)
                raws.append(lax.ppermute(sent, "section", [(sections - 1, sections - 2)]))
            else:
                own_blocks = (first_raw - first if hop == 0 else channels) // block
                owns.append(weigh(array, first, last, offset, raws[0], own_blocks, after))
            halos.append(lax.ppermute(owns[-1], ("section", "seq"), behind + (below if hop == 0 and last == channels else [])))

        send_halo(())
        if hop == 0:
            mid_sent, inputs_sent, _ = lax.optimization_barrier((mid_gate, layer_inputs, owns[0]))
            mid_halo = lax.ppermute(mid_sent, ("section", "seq"), ahead)
            inputs_halo = lax.ppermute(inputs_sent, ("section", "seq"), ahead)
        send_halo((owns[0],))
        sources, outgoing, received = [], [], []
        for k, (first, last) in enumerate(bounds):
            part = max(i for i, start in enumerate(starts) if start <= first)
            while part >= len(owns):
                send_halo(tuple(outgoing[-1:]))
            at = (first - starts[part]) // block
            array, offset = incoming[k]
            before = tuple(outgoing[-1:])
            shared = hop == 0 and first == first_raw
            out = call(
                functools.partial(raw_filter_kernel, group_size, foreign) if shared
                else functools.partial(filter_kernel, group_size),
                ((last - first) // block,),
                [SMEM, spec(rows, block, at), spec(rows, block, at), group_spec(first // block),
                 spec(rows, block, first // block), spec(rows, block, (first - offset) // block)]
                + [pl.BlockSpec(raw.shape, lambda i: (0, 0)) for raw in raws[:shared]],
                spec(rows, block),
                bf16(last - first),
                scratch=[pltpu.VMEM((min(groups, LANES), filt_len), F32)] * shared,
                name="filter",
                cycles=1000,
                after=before,
            )(role, owns[part], halos[part], taps, mid_gate, array, *raws[:shared], *before)
            sources.append((owns[part], halos[part], at))
            outgoing.append(out)
            received.append(out if shared else lax.ppermute(out, "section", down))
        top = my_section == sections - 1
        incoming = [
            (jnp.where(top, cotangent[:, first:last], arrived), first)
            for (first, last), arrived in zip(bounds, received)
        ]

    filtered = []
    for first, last in bounds:
        after = tuple(outgoing[-1:]) + tuple(filtered[-1:])
        filtered.append(call(
            functools.partial(turned_filter_kernel, group_size),
            ((last - first) // block,),
            [SMEM, spec(rows, block, first // block), spec(rows, block, first // block), group_spec(first // block)],
            spec(rows, block),
            jax.ShapeDtypeStruct((rows, last - first), F32),
            name="turned_filter",
            cycles=1000,
            after=after,
        )(role, mid_gate, mid_halo, taps, *after))

    grads, latest = {}, ()
    for k in [0, len(bounds) - 1] + list(range(1, len(bounds) - 1)):
        first, last = bounds[k]
        own, halo, at = sources[k]
        width = last - first
        here = spec(rows, block, first // block)
        after = tuple(latest[:1])
        latest = grads[k] = call(
            functools.partial(grad_kernel, group_size),
            (width // block,),
            [SMEM, here, here, here, here, here, spec(rows, block, at), spec(rows, block, at)]
            + [spec(rows, block)] * 3,
            [group_spec(0), pl.BlockSpec((1, block), lambda i: (0, i))],
            [jax.ShapeDtypeStruct((width // group_size, filt_len), F32), jax.ShapeDtypeStruct((1, width), F32)],
            scratch=[pltpu.VMEM((rows, block), BF16)] * 3,
            name="grads",
            cycles=2000,
            after=after,
        )(role, in_gate, mid_gate, layer_inputs, mid_halo, inputs_halo, own, halo, outgoing[k],
          received[k], filtered[k], *after)
    tap_grads, steer_grads = zip(*(grads[k] for k in range(len(bounds))))

    own_channels = channels // seqs
    lines = groups // seqs + pl.cdiv(own_channels, LANES)
    vmem = pl.BlockSpec(memory_space=pltpu.VMEM)
    packed = pl.pallas_call(
        functools.partial(pack_kernel, seqs),
        in_specs=[vmem] * (2 * len(grads)),
        out_specs=vmem,
        out_shape=jax.ShapeDtypeStruct((seqs, lines, LANES), F32),
        compiler_params=SMALL,
        name="pack",
    )(*tap_grads, *steer_grads)
    parts = lax.all_to_all(packed, "seq", 0, 0)
    steer_step, filter_step = pl.pallas_call(
        step_kernel,
        in_specs=[SMEM] + [vmem] * 3,
        out_shape=[
            jax.ShapeDtypeStruct((1, own_channels), F32),
            jax.ShapeDtypeStruct((groups // seqs, filt_len), F32),
        ],
        compiler_params=SMALL,
        name="step",
    )(role, parts, steer_second, filter_second[0].T)
    return steer_step, filter_step.T[None]


def solution(mesh):
    in_specs = (
        P("seq", None),
        P("section", "seq", None),
        P("section", "seq", None),
        P("section", "seq", None),
        P("section", None, None),
        P("section", "seq"),
        P("section", None, "seq"),
    )
    out_specs = (P("section", "seq"), P("section", None, "seq"))
    return jax.shard_map(body, mesh=mesh, in_specs=in_specs, out_specs=out_specs, check_vma=False)
```

```python
import functools

import jax
import jax.numpy as jnp
from jax import lax
from jax.experimental import pallas as pl
from jax.experimental.pallas import tpu as pltpu
from jax.sharding import PartitionSpec as P

F32 = jnp.float32
BF16 = jnp.bfloat16
LANES = 128
SUB = 32
CHUNK_EDGES = (0, 3, 6, 7, 8)
HALO_EDGES = (0, 3, 6, 8)


def lane_of(shape):
    return lax.broadcasted_iota(jnp.int32, shape, 1)


def row_of(shape):
    return lax.broadcasted_iota(jnp.int32, shape, 0)


def first_section(role):
    return (role[0] & 1) > 0


def times(a, b):
    return (a.astype(F32) * b.astype(F32)).astype(BF16)


def turned(x):
    return pltpu.roll(x, LANES // 2, 1)


def spread(x, x_turned, parity, count):
    low = lane_of((count, LANES)) < LANES // 2
    natural, other = (x, x_turned) if parity == 0 else (x_turned, x)
    tiles = []
    for first in (0, 2 * SUB):
        tiles.append(jnp.where(low, natural[first : first + count], other[first + SUB : first + SUB + count]))
    return jnp.concatenate(tiles, 1)


def gathered(even, odd):
    low = lane_of((SUB, LANES)) < LANES // 2
    out = []
    for tile in range(2):
        a = even[:, tile * LANES : (tile + 1) * LANES]
        b = odd[:, tile * LANES : (tile + 1) * LANES]
        out.append(jnp.where(low, a, turned(b)))
        out.append(jnp.where(low, turned(a), b))
    return jnp.concatenate(out, 0)


def in_order(reverse, own, halo):
    return jnp.concatenate([jnp.where(reverse, halo, own), jnp.where(reverse, own, halo)], 0)


def diagonal_sums(blocks):
    tiles = []
    for block in blocks:
        tile = block[:8]
        for first in range(8, SUB, 8):
            tile = tile + pltpu.roll(block[first : first + 8], LANES - first, 1)
        tiles.append(tile)
    row = row_of((8, LANES))
    for fold in (4, 2, 1):
        upper = row % (2 * fold) < fold
        tiles = [
            jnp.where(upper, a, pltpu.roll(b, fold, 0))
            + pltpu.roll(jnp.where(upper, pltpu.roll(a, 8 - fold, 0), b), LANES - fold, 1)
            for a, b in zip(tiles[:fold], tiles[fold:])
        ]
    return tiles[0]


def near(reverse_int, shape):
    return lane_of(shape) - row_of(shape) >= reverse_int


def tap_matrix(reverse, taps_by_group):
    taps = taps_by_group.shape[0]
    source = row_of((taps, taps))
    target = lane_of((taps, taps))
    mirrored = jnp.where(source == 0, 0, taps - source)
    pick = jnp.where(target == jnp.where(reverse, mirrored, source), 1.0, 0.0)
    return pick, taps


def weigh_kernel(role, gate, incoming, out):
    @pl.when(jnp.logical_not(first_section(role)))
    def _():
        out[...] = times(gate[...], incoming[...])


def first_weigh_kernel(block, role, gate, incoming, out, gate_part, incoming_part, sems):
    @pl.when(jnp.logical_not(first_section(role)))
    def _():
        tiles = [pl.ds(at, block) for at in range(0, out.shape[1], block)]
        copies = [
            [
                pltpu.make_async_copy(source.at[:, t], part.at[:, t], sems.at[which, i])
                for which, (source, part) in enumerate(((gate, gate_part), (incoming, incoming_part)))
            ]
            for i, t in enumerate(tiles)
        ]
        for pair in copies:
            for copy in pair:
                copy.start()
        for t, pair in zip(tiles, copies):
            for copy in pair:
                copy.wait()
            out[:, t] = times(gate_part[:, t], incoming_part[:, t])


def taps_kernel(role, filters, taps_out):
    pick, _ = tap_matrix(first_section(role), filters[...])
    taps_out[...] = lax.dot_general(
        filters[...], pick.astype(BF16), (((0,), (0,)), ((), ())), preferred_element_type=F32
    )


def convolved(reverse, group_size, own, halo, taps, first_group):
    half = LANES // 2
    per_half = half // group_size
    mask = near(int(reverse), (SUB, LANES))
    zero = jnp.zeros((SUB, LANES), F32)
    lane_group = (lane_of((SUB, 2 * LANES)) % half) // group_size
    ext = jnp.concatenate([halo, own] if reverse else [own, halo], 0)
    ext_turned = turned(ext)
    results = []
    for parity in range(2):
        window = spread(ext, ext_turned, parity, own.shape[0] + SUB)
        bands = []
        for g in range(per_half):
            row = taps[pl.ds(first_group + parity * per_half + g, 1), :]
            circ = pltpu.roll(jnp.broadcast_to(row, (SUB, LANES)), 0, 1, stride=1, stride_axis=0)
            band = jnp.concatenate([jnp.where(mask, circ, zero), jnp.where(mask, zero, circ)[:, :SUB]], 1)
            bands.append(band.astype(BF16))
        product = jnp.dot(jnp.concatenate(bands, 0), window, preferred_element_type=F32)
        total = product[:SUB]
        for g in range(1, per_half):
            total = jnp.where(lane_group == g, product[g * SUB : (g + 1) * SUB], total)
        results.append(total)
    return gathered(*results)


def filter_kernel(group_size, role, own, halo, taps, mid, incoming, outgoing):
    @pl.when(jnp.logical_not(first_section(role)))
    def _():
        for first in range(0, own.shape[1], LANES):
            cols = pl.ds(first, LANES)
            conv = convolved(False, group_size, own[:, cols], halo[:, cols], taps, first // group_size)
            outgoing[:, cols] = (
                incoming[:, cols].astype(F32) + mid[:, cols].astype(F32) * conv
            ).astype(BF16)


def turned_filter_kernel(group_size, role, mid, mid_halo, taps, filtered):
    @pl.when(first_section(role))
    def _():
        for first in range(0, mid.shape[1], LANES):
            cols = pl.ds(first, LANES)
            filtered[:, cols] = convolved(True, group_size, mid[:, cols], mid_halo[:, cols], taps, first // group_size)


def grad_kernel(
    group_size, role, gate, mid, inputs, mid_halo, inputs_halo, own, halo, outgoing, received, filtered,
    tap_grad, steer_grad, left, right_own, right_halo,
):
    reverse = first_section(role)
    width = own.shape[1]
    half = LANES // 2
    per_half = half // group_size

    @pl.when(reverse)
    def _():
        grad = received[...]
        weighted = times(gate[...], grad)
        left[...] = weighted
        right_own[...] = times(mid[...], inputs[...])
        right_halo[...] = times(mid_halo[...], inputs_halo[...])
        grad_in = grad.astype(F32) + weighted.astype(F32) * filtered[...]
        steer_grad[...] = jnp.sum(grad_in, 0, keepdims=True)

    @pl.when(jnp.logical_not(reverse))
    def _():
        left[...] = times(mid[...], inputs[...])
        right_own[...] = own[...]
        right_halo[...] = halo[...]
        steer_grad[...] = jnp.sum(outgoing[...].astype(F32), 0, keepdims=True)

    mask = near(role[0] & 1, (SUB, LANES))
    lane_group = (lane_of((SUB, 2 * LANES)) % half) // group_size
    nothing = jnp.zeros((SUB, 2 * LANES), BF16)
    for pair in range(width // LANES):
        cols = pl.ds(pair * LANES, LANES)
        ext = in_order(reverse, right_own[:, cols], right_halo[:, cols])
        ext_turned = turned(ext)
        rows = left[:, cols]
        rows_turned = turned(rows)
        blocks = []
        for parity in range(2):
            window = spread(ext, ext_turned, parity, own.shape[0] + SUB)
            short = spread(rows, rows_turned, parity, SUB)
            lhs = jnp.concatenate(
                [jnp.where(lane_group == g, short, nothing) for g in range(per_half)], 0
            )
            product = lax.dot_general(lhs, window, (((1,), (1,)), ((), ())), preferred_element_type=F32)
            for g in range(per_half):
                block = product[g * SUB : (g + 1) * SUB]
                late = jnp.concatenate([block[:, LANES:], jnp.zeros((SUB, LANES - SUB), F32)], 1)
                blocks.append(jnp.where(mask, block[:, :LANES], late))
        tap_grad[pl.ds(8 * pair, 8), :] = diagonal_sums(blocks)


def pack_kernel(owners, *refs):
    count = (len(refs) - 1) // 2
    taps, steers, out = refs[:count], refs[count : 2 * count], refs[-1]
    groups = sum(ref.shape[0] for ref in taps) // owners
    channels = sum(ref.shape[1] for ref in steers) // owners

    def part(parts, axis, at, size):
        for ref in parts:
            if at < ref.shape[axis]:
                return ref[at : at + size, :] if axis == 0 else ref[:, at : at + size]
            at -= ref.shape[axis]

    for owner in range(owners):
        lines = [part(taps, 0, owner * groups, groups)]
        for at in range(0, channels, LANES):
            size = min(LANES, channels - at)
            steer = part(steers, 1, owner * channels + at, size)
            if size < LANES:
                steer = jnp.concatenate([steer, jnp.zeros((1, LANES - size), F32)], 1)
            lines.append(steer)
        out[owner] = jnp.concatenate(lines, 0).astype(BF16)


def step_kernel(role, parts, steer_second, filter_second, steer_out, filter_out):
    total = jnp.sum(parts[...].astype(F32), 0)
    groups = filter_second.shape[0]
    tap_grad = total[:groups]
    lane = lane_of(tap_grad.shape)
    mirrored = jnp.where(lane == 0, 0, tap_grad.shape[1] - lane)
    tap_grad = jnp.take_along_axis(tap_grad, jnp.where(first_section(role), mirrored, lane), axis=1)
    filter_out[...] = tap_grad / jnp.sqrt(filter_second[...] + tap_grad * tap_grad)
    channels = steer_out.shape[1]
    for row in range(pl.cdiv(channels, LANES)):
        cols = min(LANES, channels - row * LANES)
        at = pl.ds(row * LANES, cols)
        grad = total[groups + row : groups + row + 1, :cols]
        steer_out[:, at] = grad / jnp.sqrt(steer_second[:, at] + grad * grad)


def spec(rows, width, first=0):
    return pl.BlockSpec((rows, width), lambda i: (0, i + first))


SMEM = pl.BlockSpec(memory_space=pltpu.SMEM)
ANY = pl.BlockSpec(memory_space=pl.ANY)
SMALL = pltpu.CompilerParams(vmem_limit_bytes=4 * 1024 * 1024)


def call(kernel, grid, in_specs, out_specs, out_shape, scratch=(), name=None, cycles=100, after=()):
    count = len(in_specs)

    def with_after(*refs):
        kernel(*refs[:count], *refs[count + len(after) :])

    return pl.pallas_call(
        with_after,
        grid=grid,
        in_specs=list(in_specs) + [ANY] * len(after),
        out_specs=out_specs,
        out_shape=out_shape,
        scratch_shapes=list(scratch),
        compiler_params=pltpu.CompilerParams(vmem_limit_bytes=16 * 1024 * 1024),
        cost_estimate=pl.CostEstimate(flops=cycles, bytes_accessed=0, transcendentals=0),
        name=name,
    )


def body(cotangent, in_gate, mid_gate, layer_inputs, filters, steer_second, filter_second):
    in_gate, mid_gate, layer_inputs = in_gate[0], mid_gate[0], layer_inputs[0]
    rows, channels = in_gate.shape
    filt_len, groups = filters.shape[1:]
    group_size = channels // groups
    sections, seqs = lax.axis_size("section"), lax.axis_size("seq")
    my_section = lax.axis_index("section")
    role = (my_section == 0).astype(jnp.int32).reshape(1)

    edges = [channels * eighths // 8 for eighths in CHUNK_EDGES]
    bounds = list(zip(edges[:-1], edges[1:]))
    block = channels // 8
    block_groups = block // group_size
    behind = [(seqs * s + i, seqs * s + i - 1) for s in range(1, sections) for i in range(1, seqs)]
    ahead = [(i, i + 1) for i in range(seqs - 1)]
    down = [(s, s - 1) for s in range(1, sections)]

    def bf16(width_of):
        return jax.ShapeDtypeStruct((rows, width_of), BF16)

    def weigh(incoming, first, last, offset, after):
        return call(
            weigh_kernel,
            ((last - first) // block,),
            [SMEM, spec(rows, block, first // block), spec(rows, block, (first - offset) // block)],
            spec(rows, block),
            bf16(last - first),
            name="weigh",
            after=after,
        )(role, in_gate, incoming, *after)

    def first_weigh(last):
        part = pltpu.VMEM((rows, last), BF16)
        return pl.pallas_call(
            functools.partial(first_weigh_kernel, block),
            in_specs=[SMEM] + [pl.BlockSpec(memory_space=pl.ANY)] * 2,
            out_specs=pl.BlockSpec(memory_space=pltpu.VMEM),
            out_shape=bf16(last),
            scratch_shapes=[part, part, pltpu.SemaphoreType.DMA((2, last // block))],
            compiler_params=SMALL,
            name="first_weigh",
        )(role, *[pltpu.with_memory_space_constraint(a, pltpu.HBM) for a in (in_gate, cotangent)])

    taps = call(
        taps_kernel,
        (1,),
        [SMEM, pl.BlockSpec((filt_len, groups), lambda i: (0, 0))],
        pl.BlockSpec((groups, filt_len), lambda i: (0, 0)),
        jax.ShapeDtypeStruct((groups, filt_len), F32),
        name="taps",
    )(role, filters[0])
    group_spec = lambda first: pl.BlockSpec((block_groups, filt_len), lambda i: (i + first, 0))

    incoming = [(cotangent, 0)] * len(bounds)
    for hop in range(sections - 1):
        split = [channels * eighths // 8 for eighths in HALO_EDGES] if hop == 0 else edges
        starts, ends = split[:-1], split[1:]
        owns, halos = [], []

        def send_halo(after):
            first, last = starts[len(owns)], ends[len(owns)]
            array, offset = next(entry for entry, edge in zip(incoming, edges) if edge == first)
            if hop == 0 and first == 0:
                owns.append(first_weigh(last))
            else:
                owns.append(weigh(array, first, last, offset, after))
            halos.append(lax.ppermute(owns[-1], ("section", "seq"), behind))

        send_halo(())
        if hop == 0:
            mid_sent, inputs_sent, _ = lax.optimization_barrier((mid_gate, layer_inputs, owns[0]))
            mid_halo = lax.ppermute(mid_sent, ("section", "seq"), ahead)
            inputs_halo = lax.ppermute(inputs_sent, ("section", "seq"), ahead)
        send_halo((owns[0],))
        sources, outgoing, received = [], [], []
        for k, (first, last) in enumerate(bounds):
            part = max(i for i, start in enumerate(starts) if start <= first)
            while part >= len(owns):
                send_halo(tuple(received[:1]))
            at = (first - starts[part]) // block
            array, offset = incoming[k]
            before = tuple(outgoing[-1:])
            out = call(
                functools.partial(filter_kernel, group_size),
                ((last - first) // block,),
                [SMEM, spec(rows, block, at), spec(rows, block, at), group_spec(first // block),
                 spec(rows, block, first // block), spec(rows, block, (first - offset) // block)],
                spec(rows, block),
                bf16(last - first),
                name="filter",
                cycles=1000,
                after=before,
            )(role, owns[part], halos[part], taps, mid_gate, array, *before)
            sources.append((owns[part], halos[part], at))
            outgoing.append(out)
            received.append(lax.ppermute(out, "section", down))
        top = my_section == sections - 1
        incoming = [
            (jnp.where(top, cotangent[:, first:last], arrived), first)
            for (first, last), arrived in zip(bounds, received)
        ]

    filtered = []
    for first, last in bounds:
        after = tuple(outgoing[-1:]) + tuple(filtered[-1:])
        filtered.append(call(
            functools.partial(turned_filter_kernel, group_size),
            ((last - first) // block,),
            [SMEM, spec(rows, block, first // block), spec(rows, block, first // block), group_spec(first // block)],
            spec(rows, block),
            jax.ShapeDtypeStruct((rows, last - first), F32),
            name="turned_filter",
            cycles=1000,
            after=after,
        )(role, mid_gate, mid_halo, taps, *after))

    grads = []
    for k, (first, last) in enumerate(bounds):
        own, halo, at = sources[k]
        width = last - first
        here = spec(rows, block, first // block)
        after = tuple(grads[-1][:1] if grads else ())
        grads.append(call(
            functools.partial(grad_kernel, group_size),
            (width // block,),
            [SMEM, here, here, here, here, here, spec(rows, block, at), spec(rows, block, at)]
            + [spec(rows, block)] * 3,
            [group_spec(0), pl.BlockSpec((1, block), lambda i: (0, i))],
            [jax.ShapeDtypeStruct((width // group_size, filt_len), F32), jax.ShapeDtypeStruct((1, width), F32)],
            scratch=[pltpu.VMEM((rows, block), BF16)] * 3,
            name="grads",
            cycles=2000,
            after=after,
        )(role, in_gate, mid_gate, layer_inputs, mid_halo, inputs_halo, own, halo, outgoing[k],
          received[k], filtered[k], *after))
    tap_grads, steer_grads = zip(*grads)

    own_channels = channels // seqs
    lines = groups // seqs + pl.cdiv(own_channels, LANES)
    vmem = pl.BlockSpec(memory_space=pltpu.VMEM)
    packed = pl.pallas_call(
        functools.partial(pack_kernel, seqs),
        in_specs=[vmem] * (2 * len(grads)),
        out_specs=vmem,
        out_shape=jax.ShapeDtypeStruct((seqs, lines, LANES), BF16),
        compiler_params=SMALL,
        name="pack",
    )(*tap_grads, *steer_grads)
    parts = lax.all_to_all(packed, "seq", 0, 0)
    steer_step, filter_step = pl.pallas_call(
        step_kernel,
        in_specs=[SMEM] + [vmem] * 3,
        out_shape=[
            jax.ShapeDtypeStruct((1, own_channels), F32),
            jax.ShapeDtypeStruct((groups // seqs, filt_len), F32),
        ],
        compiler_params=SMALL,
        name="step",
    )(role, parts, steer_second, filter_second[0].T)
    return steer_step, filter_step.T[None]


def solution(mesh):
    in_specs = (
        P("seq", None),
        P("section", "seq", None),
        P("section", "seq", None),
        P("section", "seq", None),
        P("section", None, None),
        P("section", "seq"),
        P("section", None, "seq"),
    )
    out_specs = (P("section", "seq"), P("section", None, "seq"))
    return jax.shard_map(body, mesh=mesh, in_specs=in_specs, out_specs=out_specs, check_vma=False)
```

```python
import functools

import jax
import jax.numpy as jnp
from jax import lax
from jax.experimental import pallas as pl
from jax.experimental.pallas import tpu as pltpu
from jax.sharding import PartitionSpec as P

F32 = jnp.float32
BF16 = jnp.bfloat16
LANES = 128
SUB = 32
CHUNK_EDGES = (0, 3, 6, 7, 8)
HALO_EDGES = (0, 3, 6, 8)


def lane_of(shape):
    return lax.broadcasted_iota(jnp.int32, shape, 1)


def row_of(shape):
    return lax.broadcasted_iota(jnp.int32, shape, 0)


def first_section(role):
    return (role[0] & 1) > 0


def times(a, b):
    return (a.astype(F32) * b.astype(F32)).astype(BF16)


def turned(x):
    return pltpu.roll(x, LANES // 2, 1)


def spread(x, x_turned, parity, count):
    low = lane_of((count, LANES)) < LANES // 2
    natural, other = (x, x_turned) if parity == 0 else (x_turned, x)
    tiles = []
    for first in (0, 2 * SUB):
        tiles.append(jnp.where(low, natural[first : first + count], other[first + SUB : first + SUB + count]))
    return jnp.concatenate(tiles, 1)


def gathered(even, odd):
    low = lane_of((SUB, LANES)) < LANES // 2
    out = []
    for tile in range(2):
        a = even[:, tile * LANES : (tile + 1) * LANES]
        b = odd[:, tile * LANES : (tile + 1) * LANES]
        out.append(jnp.where(low, a, turned(b)))
        out.append(jnp.where(low, turned(a), b))
    return jnp.concatenate(out, 0)


def in_order(reverse, own, halo):
    return jnp.concatenate([jnp.where(reverse, halo, own), jnp.where(reverse, own, halo)], 0)


def diagonal_sums(blocks):
    tiles = []
    for block in blocks:
        tile = block[:8]
        for first in range(8, SUB, 8):
            tile = tile + pltpu.roll(block[first : first + 8], LANES - first, 1)
        tiles.append(tile)
    row = row_of((8, LANES))
    for fold in (4, 2, 1):
        upper = row % (2 * fold) < fold
        tiles = [
            jnp.where(upper, a, pltpu.roll(b, fold, 0))
            + pltpu.roll(jnp.where(upper, pltpu.roll(a, 8 - fold, 0), b), LANES - fold, 1)
            for a, b in zip(tiles[:fold], tiles[fold:])
        ]
    return tiles[0]


def near(reverse_int, shape):
    return lane_of(shape) - row_of(shape) >= reverse_int


def tap_matrix(reverse, taps_by_group):
    taps = taps_by_group.shape[0]
    source = row_of((taps, taps))
    target = lane_of((taps, taps))
    mirrored = jnp.where(source == 0, 0, taps - source)
    pick = jnp.where(target == jnp.where(reverse, mirrored, source), 1.0, 0.0)
    return pick, taps


def weigh_kernel(role, gate, incoming, out):
    @pl.when(jnp.logical_not(first_section(role)))
    def _():
        out[...] = times(gate[...], incoming[...])


def first_weigh_kernel(block, role, gate, incoming, out, gate_part, incoming_part, sems):
    @pl.when(jnp.logical_not(first_section(role)))
    def _():
        tiles = [pl.ds(at, block) for at in range(0, out.shape[1], block)]
        copies = [
            [
                pltpu.make_async_copy(source.at[:, t], part.at[:, t], sems.at[which, i])
                for which, (source, part) in enumerate(((gate, gate_part), (incoming, incoming_part)))
            ]
            for i, t in enumerate(tiles)
        ]
        for pair in copies:
            for copy in pair:
                copy.start()
        for t, pair in zip(tiles, copies):
            for copy in pair:
                copy.wait()
            out[:, t] = times(gate_part[:, t], incoming_part[:, t])


def taps_kernel(role, filters, taps_out):
    pick, _ = tap_matrix(first_section(role), filters[...])
    taps_out[...] = lax.dot_general(
        filters[...], pick.astype(BF16), (((0,), (0,)), ((), ())), preferred_element_type=F32
    )


def convolved(reverse, group_size, own, halo, taps, first_group):
    half = LANES // 2
    per_half = half // group_size
    mask = near(int(reverse), (SUB, LANES))
    zero = jnp.zeros((SUB, LANES), F32)
    lane_group = (lane_of((SUB, 2 * LANES)) % half) // group_size
    ext = jnp.concatenate([halo, own] if reverse else [own, halo], 0)
    ext_turned = turned(ext)
    results = []
    for parity in range(2):
        window = spread(ext, ext_turned, parity, own.shape[0] + SUB)
        bands = []
        for g in range(per_half):
            row = taps[pl.ds(first_group + parity * per_half + g, 1), :]
            circ = pltpu.roll(jnp.broadcast_to(row, (SUB, LANES)), 0, 1, stride=1, stride_axis=0)
            band = jnp.concatenate([jnp.where(mask, circ, zero), jnp.where(mask, zero, circ)[:, :SUB]], 1)
            bands.append(band.astype(BF16))
        product = jnp.dot(jnp.concatenate(bands, 0), window, preferred_element_type=F32)
        total = product[:SUB]
        for g in range(1, per_half):
            total = jnp.where(lane_group == g, product[g * SUB : (g + 1) * SUB], total)
        results.append(total)
    return gathered(*results)


def filter_kernel(group_size, role, own, halo, taps, mid, incoming, outgoing):
    @pl.when(jnp.logical_not(first_section(role)))
    def _():
        for first in range(0, own.shape[1], LANES):
            cols = pl.ds(first, LANES)
            conv = convolved(False, group_size, own[:, cols], halo[:, cols], taps, first // group_size)
            outgoing[:, cols] = (
                incoming[:, cols].astype(F32) + mid[:, cols].astype(F32) * conv
            ).astype(BF16)


def turned_filter_kernel(group_size, role, mid, mid_halo, taps, filtered):
    @pl.when(first_section(role))
    def _():
        for first in range(0, mid.shape[1], LANES):
            cols = pl.ds(first, LANES)
            filtered[:, cols] = convolved(True, group_size, mid[:, cols], mid_halo[:, cols], taps, first // group_size)


def tap_sums(reverse, group_size, left, own, halo):
    half = LANES // 2
    per_half = half // group_size
    mask = near(int(reverse), (SUB, LANES))
    lane_group = (lane_of((SUB, 2 * LANES)) % half) // group_size
    nothing = jnp.zeros((SUB, 2 * LANES), BF16)
    ext = jnp.concatenate([halo, own] if reverse else [own, halo], 0)
    ext_turned, left_turned = turned(ext), turned(left)
    blocks = []
    for parity in range(2):
        window = spread(ext, ext_turned, parity, own.shape[0] + SUB)
        short = spread(left, left_turned, parity, SUB)
        lhs = jnp.concatenate([jnp.where(lane_group == g, short, nothing) for g in range(per_half)], 0)
        product = lax.dot_general(lhs, window, (((1,), (1,)), ((), ())), preferred_element_type=F32)
        for g in range(per_half):
            block = product[g * SUB : (g + 1) * SUB]
            late = jnp.concatenate([block[:, LANES:], jnp.zeros((SUB, LANES - SUB), F32)], 1)
            blocks.append(jnp.where(mask, block[:, :LANES], late))
    return diagonal_sums(blocks)


def upper_grad_kernel(group_size, role, mid, inputs, own, halo, outgoing, tap_grad, steer_grad):
    @pl.when(role[0] == 0)
    def _():
        steer_grad[...] = jnp.sum(outgoing[...].astype(F32), 0, keepdims=True)
        for pair in range(own.shape[1] // LANES):
            cols = pl.ds(pair * LANES, LANES)
            values = times(mid[:, cols], inputs[:, cols])
            tap_grad[pl.ds(8 * pair, 8), :] = tap_sums(False, group_size, values, own[:, cols], halo[:, cols])


def first_grad_kernel(
    group_size, role, gate, mid, inputs, mid_halo, inputs_halo, received, filtered, tap_grad, steer_grad
):
    @pl.when(role[0] > 0)
    def _():
        for pair in range(gate.shape[1] // LANES):
            cols = pl.ds(pair * LANES, LANES)
            grad = received[:, cols]
            weighted = times(gate[:, cols], grad)
            grad_in = grad.astype(F32) + weighted.astype(F32) * filtered[:, cols]
            steer_grad[:, cols] = jnp.sum(grad_in, 0, keepdims=True)
            own, halo = times(mid[:, cols], inputs[:, cols]), times(mid_halo[:, cols], inputs_halo[:, cols])
            tap_grad[pl.ds(8 * pair, 8), :] = tap_sums(True, group_size, weighted, own, halo)


def pack_kernel(owners, role, steer_second, filter_second, *refs):
    refs, (out, steer_out, filter_out) = refs[:-3], refs[-3:]
    count = len(refs) // 4
    steer_out[...] = steer_second[...]
    filter_out[...] = filter_second[...]

    def part(parts, axis, at, size):
        for ref in parts:
            if at < ref.shape[axis]:
                return ref[at : at + size, :] if axis == 0 else ref[:, at : at + size]
            at -= ref.shape[axis]

    def pack(taps, steers):
        groups = sum(ref.shape[0] for ref in taps) // owners
        channels = sum(ref.shape[1] for ref in steers) // owners
        for owner in range(owners):
            lines = [part(taps, 0, owner * groups, groups)]
            for at in range(0, channels, LANES):
                size = min(LANES, channels - at)
                steer = part(steers, 1, owner * channels + at, size)
                if size < LANES:
                    steer = jnp.concatenate([steer, jnp.zeros((1, LANES - size), F32)], 1)
                lines.append(steer)
            out[owner] = jnp.concatenate(lines, 0).astype(BF16)

    @pl.when(first_section(role))
    def _():
        pack(refs[:count], refs[count : 2 * count])

    @pl.when(jnp.logical_not(first_section(role)))
    def _():
        pack(refs[2 * count : 3 * count], refs[3 * count :])


def step_kernel(role, parts, steer_second, filter_second, steer_out, filter_out):
    total = jnp.sum(parts[...].astype(F32), 0)
    groups = filter_second.shape[0]
    tap_grad = total[:groups]
    lane = lane_of(tap_grad.shape)
    mirrored = jnp.where(lane == 0, 0, tap_grad.shape[1] - lane)
    tap_grad = jnp.take_along_axis(tap_grad, jnp.where(first_section(role), mirrored, lane), axis=1)
    filter_out[...] = tap_grad / jnp.sqrt(filter_second[...] + tap_grad * tap_grad)
    channels = steer_out.shape[1]
    for row in range(pl.cdiv(channels, LANES)):
        cols = min(LANES, channels - row * LANES)
        at = pl.ds(row * LANES, cols)
        grad = total[groups + row : groups + row + 1, :cols]
        steer_out[:, at] = grad / jnp.sqrt(steer_second[:, at] + grad * grad)


def spec(rows, width, first=0):
    return pl.BlockSpec((rows, width), lambda i: (0, i + first))


SMEM = pl.BlockSpec(memory_space=pltpu.SMEM)
ANY = pl.BlockSpec(memory_space=pl.ANY)
SMALL = pltpu.CompilerParams(vmem_limit_bytes=4 * 1024 * 1024)


def call(kernel, grid, in_specs, out_specs, out_shape, scratch=(), name=None, cycles=100, after=()):
    count = len(in_specs)

    def with_after(*refs):
        kernel(*refs[:count], *refs[count + len(after) :])

    return pl.pallas_call(
        with_after,
        grid=grid,
        in_specs=list(in_specs) + [ANY] * len(after),
        out_specs=out_specs,
        out_shape=out_shape,
        scratch_shapes=list(scratch),
        compiler_params=pltpu.CompilerParams(vmem_limit_bytes=16 * 1024 * 1024),
        cost_estimate=pl.CostEstimate(flops=cycles, bytes_accessed=0, transcendentals=0),
        name=name,
    )


def body(cotangent, in_gate, mid_gate, layer_inputs, filters, steer_second, filter_second):
    in_gate, mid_gate, layer_inputs = in_gate[0], mid_gate[0], layer_inputs[0]
    rows, channels = in_gate.shape
    filt_len, groups = filters.shape[1:]
    group_size = channels // groups
    sections, seqs = lax.axis_size("section"), lax.axis_size("seq")
    my_section = lax.axis_index("section")
    role = (my_section == 0).astype(jnp.int32).reshape(1)

    edges = [channels * eighths // 8 for eighths in CHUNK_EDGES]
    bounds = list(zip(edges[:-1], edges[1:]))
    block = channels // 8
    block_groups = block // group_size
    behind = [(seqs * s + i, seqs * s + i - 1) for s in range(1, sections) for i in range(1, seqs)]
    ahead = [(i, i + 1) for i in range(seqs - 1)]
    down = [(s, s - 1) for s in range(1, sections)]

    def bf16(width_of):
        return jax.ShapeDtypeStruct((rows, width_of), BF16)

    def weigh(incoming, first, last, offset, after):
        return call(
            weigh_kernel,
            ((last - first) // block,),
            [SMEM, spec(rows, block, first // block), spec(rows, block, (first - offset) // block)],
            spec(rows, block),
            bf16(last - first),
            name="weigh",
            after=after,
        )(role, in_gate, incoming, *after)

    def first_weigh(last):
        part = pltpu.VMEM((rows, last), BF16)
        return pl.pallas_call(
            functools.partial(first_weigh_kernel, block),
            in_specs=[SMEM] + [pl.BlockSpec(memory_space=pl.ANY)] * 2,
            out_specs=pl.BlockSpec(memory_space=pltpu.VMEM),
            out_shape=bf16(last),
            scratch_shapes=[part, part, pltpu.SemaphoreType.DMA((2, last // block))],
            compiler_params=SMALL,
            name="first_weigh",
        )(role, *[pltpu.with_memory_space_constraint(a, pltpu.HBM) for a in (in_gate, cotangent)])

    taps = call(
        taps_kernel,
        (1,),
        [SMEM, pl.BlockSpec((filt_len, groups), lambda i: (0, 0))],
        pl.BlockSpec((groups, filt_len), lambda i: (0, 0)),
        jax.ShapeDtypeStruct((groups, filt_len), F32),
        name="taps",
    )(role, filters[0])
    group_spec = lambda first: pl.BlockSpec((block_groups, filt_len), lambda i: (i + first, 0))

    grad_specs = [group_spec(0), pl.BlockSpec((1, block), lambda i: (0, i))]

    def grad_shapes(k):
        width = bounds[k][1] - bounds[k][0]
        return [
            jax.ShapeDtypeStruct((width // group_size, filt_len), F32),
            jax.ShapeDtypeStruct((1, width), F32),
        ]

    def upper_grad(k, after):
        first, last = bounds[k]
        own, halo, at = sources[k]
        here, there = spec(rows, block, first // block), spec(rows, block, at)
        return call(
            functools.partial(upper_grad_kernel, group_size),
            ((last - first) // block,),
            [SMEM, here, here, there, there, spec(rows, block)],
            grad_specs,
            grad_shapes(k),
            name="upper_grads",
            cycles=2000,
            after=tuple(after),
        )(role, mid_gate, layer_inputs, own, halo, outgoing[k], *after)

    def turned_filter(k, after):
        first, last = bounds[k]
        here = spec(rows, block, first // block)
        return call(
            functools.partial(turned_filter_kernel, group_size),
            ((last - first) // block,),
            [SMEM, here, here, group_spec(first // block)],
            spec(rows, block),
            jax.ShapeDtypeStruct((rows, last - first), F32),
            name="turned_filter",
            cycles=1000,
            after=tuple(after),
        )(role, mid_gate, mid_halo, taps, *after)

    incoming = [(cotangent, 0)] * len(bounds)
    early, uppers, filtered = [], [], []
    for hop in range(sections - 1):
        split = [channels * eighths // 8 for eighths in HALO_EDGES] if hop == 0 else edges
        starts, ends = split[:-1], split[1:]
        owns, halos = [], []

        def send_halo(after):
            first, last = starts[len(owns)], ends[len(owns)]
            array, offset = next(entry for entry, edge in zip(incoming, edges) if edge == first)
            if hop == 0 and first == 0:
                owns.append(first_weigh(last))
            else:
                owns.append(weigh(array, first, last, offset, after))
            halos.append(lax.ppermute(owns[-1], ("section", "seq"), behind))

        send_halo(())
        if hop == 0:
            mid_sent, inputs_sent, _ = lax.optimization_barrier((mid_gate, layer_inputs, owns[0]))
            mid_halo = lax.ppermute(mid_sent, ("section", "seq"), ahead)
            inputs_halo = lax.ppermute(inputs_sent, ("section", "seq"), ahead)
        send_halo((owns[0],))
        sources, outgoing, received = [], [], []
        for k, (first, last) in enumerate(bounds):
            part = max(i for i, start in enumerate(starts) if start <= first)
            while part >= len(owns):
                send_halo(tuple(received[:1]) + tuple(early))
            at = (first - starts[part]) // block
            array, offset = incoming[k]
            before = tuple(outgoing[-1:])
            if hop == sections - 2 and k == 2:
                uppers.append(upper_grad(1, owns[-1:]))
                before += tuple(uppers[-1][:1])
            out = call(
                functools.partial(filter_kernel, group_size),
                ((last - first) // block,),
                [SMEM, spec(rows, block, at), spec(rows, block, at), group_spec(first // block),
                 spec(rows, block, first // block), spec(rows, block, (first - offset) // block)],
                spec(rows, block),
                bf16(last - first),
                name="filter",
                cycles=1000,
                after=before,
            )(role, owns[part], halos[part], taps, mid_gate, array, *before)
            sources.append((owns[part], halos[part], at))
            outgoing.append(out)
            received.append(lax.ppermute(out, "section", down))
            if hop == sections - 2 and k == 1:
                uppers = [upper_grad(0, (out,))]
                filtered = [turned_filter(0, (out,))]
                filtered.append(turned_filter(1, filtered[-1:]))
                early = [uppers[0][0], filtered[-1]]
        top = my_section == sections - 1
        incoming = [
            (jnp.where(top, cotangent[:, first:last], arrived), first)
            for (first, last), arrived in zip(bounds, received)
        ]

    latest = outgoing[-1:]
    for k in range(len(filtered), len(bounds)):
        filtered.append(turned_filter(k, latest))
        latest = filtered[-1:]
    for k in range(len(uppers), len(bounds)):
        uppers.append(upper_grad(k, latest))
        latest = uppers[-1][:1]
    firsts = []
    for k, (first, last) in enumerate(bounds):
        here = spec(rows, block, first // block)
        firsts.append(call(
            functools.partial(first_grad_kernel, group_size),
            ((last - first) // block,),
            [SMEM, here, here, here, here, here, spec(rows, block), spec(rows, block)],
            grad_specs,
            grad_shapes(k),
            name="first_grads",
            cycles=2000,
            after=tuple(latest),
        )(role, in_gate, mid_gate, layer_inputs, mid_halo, inputs_halo, received[k], filtered[k], *latest))
        latest = firsts[-1][:1]
    partial_sums = [grads[i] for both in (firsts, uppers) for i in range(2) for grads in both]

    own_channels = channels // seqs
    lines = groups // seqs + pl.cdiv(own_channels, LANES)
    vmem = pl.BlockSpec(memory_space=pltpu.VMEM)
    seconds = (steer_second, filter_second[0].T)
    packed, *seconds = pl.pallas_call(
        functools.partial(pack_kernel, seqs),
        in_specs=[SMEM] + [vmem] * (2 + len(partial_sums)),
        out_specs=[vmem] * 3,
        out_shape=[jax.ShapeDtypeStruct((seqs, lines, LANES), BF16)]
        + [jax.ShapeDtypeStruct(second.shape, F32) for second in seconds],
        compiler_params=SMALL,
        name="pack",
    )(role, *seconds, *partial_sums)
    parts = lax.all_to_all(packed, "seq", 0, 0)
    steer_step, filter_step = pl.pallas_call(
        step_kernel,
        in_specs=[SMEM] + [vmem] * 3,
        out_shape=[
            jax.ShapeDtypeStruct((1, own_channels), F32),
            jax.ShapeDtypeStruct((groups // seqs, filt_len), F32),
        ],
        compiler_params=SMALL,
        name="step",
    )(role, parts, *seconds)
    return steer_step, filter_step.T[None]


def solution(mesh):
    in_specs = (
        P("seq", None),
        P("section", "seq", None),
        P("section", "seq", None),
        P("section", "seq", None),
        P("section", None, None),
        P("section", "seq"),
        P("section", None, "seq"),
    )
    out_specs = (P("section", "seq"), P("section", None, "seq"))
    return jax.shard_map(body, mesh=mesh, in_specs=in_specs, out_specs=out_specs, check_vma=False)
```

```python
import functools

import jax
import jax.numpy as jnp
from jax import lax
from jax.experimental import pallas as pl
from jax.experimental.pallas import tpu as pltpu
from jax.sharding import PartitionSpec as P

F32 = jnp.float32
BF16 = jnp.bfloat16
LANES = 128
SUB = 32
CHUNK_EDGES = (0, 3, 6, 7, 8)
HALO_EDGES = (0, 3, 6, 8)


def lane_of(shape):
    return lax.broadcasted_iota(jnp.int32, shape, 1)


def row_of(shape):
    return lax.broadcasted_iota(jnp.int32, shape, 0)


def first_section(role):
    return (role[0] & 1) > 0


def times(a, b):
    return (a.astype(F32) * b.astype(F32)).astype(BF16)


def turned(x):
    return pltpu.roll(x, LANES // 2, 1)


def spread(x, x_turned, parity, count):
    low = lane_of((count, LANES)) < LANES // 2
    natural, other = (x, x_turned) if parity == 0 else (x_turned, x)
    tiles = []
    for first in (0, 2 * SUB):
        tiles.append(jnp.where(low, natural[first : first + count], other[first + SUB : first + SUB + count]))
    return jnp.concatenate(tiles, 1)


def gathered(even, odd):
    low = lane_of((SUB, LANES)) < LANES // 2
    out = []
    for tile in range(2):
        a = even[:, tile * LANES : (tile + 1) * LANES]
        b = odd[:, tile * LANES : (tile + 1) * LANES]
        out.append(jnp.where(low, a, turned(b)))
        out.append(jnp.where(low, turned(a), b))
    return jnp.concatenate(out, 0)


def in_order(reverse, own, halo):
    return jnp.concatenate([jnp.where(reverse, halo, own), jnp.where(reverse, own, halo)], 0)


def diagonal_sums(blocks):
    tiles = []
    for block in blocks:
        tile = block[:8]
        for first in range(8, SUB, 8):
            tile = tile + pltpu.roll(block[first : first + 8], LANES - first, 1)
        tiles.append(tile)
    row = row_of((8, LANES))
    for fold in (4, 2, 1):
        upper = row % (2 * fold) < fold
        tiles = [
            jnp.where(upper, a, pltpu.roll(b, fold, 0))
            + pltpu.roll(jnp.where(upper, pltpu.roll(a, 8 - fold, 0), b), LANES - fold, 1)
            for a, b in zip(tiles[:fold], tiles[fold:])
        ]
    return tiles[0]


def near(reverse_int, shape):
    return lane_of(shape) - row_of(shape) >= reverse_int


def tap_matrix(reverse, taps_by_group):
    taps = taps_by_group.shape[0]
    source = row_of((taps, taps))
    target = lane_of((taps, taps))
    mirrored = jnp.where(source == 0, 0, taps - source)
    pick = jnp.where(target == jnp.where(reverse, mirrored, source), 1.0, 0.0)
    return pick, taps


def weigh_kernel(role, gate, incoming, out):
    @pl.when(jnp.logical_not(first_section(role)))
    def _():
        out[...] = times(gate[...], incoming[...])


def first_weigh_kernel(block, role, gate, incoming, out, gate_part, incoming_part, sems):
    @pl.when(jnp.logical_not(first_section(role)))
    def _():
        tiles = [pl.ds(at, block) for at in range(0, out.shape[1], block)]
        copies = [
            [
                pltpu.make_async_copy(source.at[:, t], part.at[:, t], sems.at[which, i])
                for which, (source, part) in enumerate(((gate, gate_part), (incoming, incoming_part)))
            ]
            for i, t in enumerate(tiles)
        ]
        for pair in copies:
            for copy in pair:
                copy.start()
        for t, pair in zip(tiles, copies):
            for copy in pair:
                copy.wait()
            out[:, t] = times(gate_part[:, t], incoming_part[:, t])


def taps_kernel(role, filters, steer_second, filter_second, taps_out, steer_out, filter_out):
    steer_out[...] = steer_second[...]
    filter_out[...] = filter_second[...]
    pick, _ = tap_matrix(first_section(role), filters[...])
    taps_out[...] = lax.dot_general(
        filters[...], pick.astype(BF16), (((0,), (0,)), ((), ())), preferred_element_type=F32
    )


def convolved(reverse, group_size, own, halo, taps, first_group):
    half = LANES // 2
    per_half = half // group_size
    mask = near(int(reverse), (SUB, LANES))
    zero = jnp.zeros((SUB, LANES), F32)
    lane_group = (lane_of((SUB, 2 * LANES)) % half) // group_size
    ext = jnp.concatenate([halo, own] if reverse else [own, halo], 0)
    ext_turned = turned(ext)
    results = []
    for parity in range(2):
        window = spread(ext, ext_turned, parity, own.shape[0] + SUB)
        bands = []
        for g in range(per_half):
            row = taps[pl.ds(first_group + parity * per_half + g, 1), :]
            circ = pltpu.roll(jnp.broadcast_to(row, (SUB, LANES)), 0, 1, stride=1, stride_axis=0)
            band = jnp.concatenate([jnp.where(mask, circ, zero), jnp.where(mask, zero, circ)[:, :SUB]], 1)
            bands.append(band.astype(BF16))
        product = jnp.dot(jnp.concatenate(bands, 0), window, preferred_element_type=F32)
        total = product[:SUB]
        for g in range(1, per_half):
            total = jnp.where(lane_group == g, product[g * SUB : (g + 1) * SUB], total)
        results.append(total)
    return gathered(*results)


def filter_kernel(group_size, role, own, halo, taps, mid, incoming, outgoing):
    @pl.when(jnp.logical_not(first_section(role)))
    def _():
        for first in range(0, own.shape[1], LANES):
            cols = pl.ds(first, LANES)
            conv = convolved(False, group_size, own[:, cols], halo[:, cols], taps, first // group_size)
            outgoing[:, cols] = (
                incoming[:, cols].astype(F32) + mid[:, cols].astype(F32) * conv
            ).astype(BF16)


def turned_filter_kernel(group_size, role, mid, mid_halo, taps, filtered):
    @pl.when(first_section(role))
    def _():
        for first in range(0, mid.shape[1], LANES):
            cols = pl.ds(first, LANES)
            filtered[:, cols] = convolved(True, group_size, mid[:, cols], mid_halo[:, cols], taps, first // group_size)


def tap_sums(reverse, group_size, left, own, halo):
    half = LANES // 2
    per_half = half // group_size
    mask = near(int(reverse), (SUB, LANES))
    lane_group = (lane_of((SUB, 2 * LANES)) % half) // group_size
    nothing = jnp.zeros((SUB, 2 * LANES), BF16)
    ext = jnp.concatenate([halo, own] if reverse else [own, halo], 0)
    ext_turned, left_turned = turned(ext), turned(left)
    blocks = []
    for parity in range(2):
        window = spread(ext, ext_turned, parity, own.shape[0] + SUB)
        short = spread(left, left_turned, parity, SUB)
        lhs = jnp.concatenate([jnp.where(lane_group == g, short, nothing) for g in range(per_half)], 0)
        product = lax.dot_general(lhs, window, (((1,), (1,)), ((), ())), preferred_element_type=F32)
        for g in range(per_half):
            block = product[g * SUB : (g + 1) * SUB]
            late = jnp.concatenate([block[:, LANES:], jnp.zeros((SUB, LANES - SUB), F32)], 1)
            blocks.append(jnp.where(mask, block[:, :LANES], late))
    return diagonal_sums(blocks)


def upper_grad_kernel(group_size, role, mid, inputs, own, halo, outgoing, tap_grad, steer_grad):
    @pl.when(role[0] == 0)
    def _():
        steer_grad[...] = jnp.sum(outgoing[...].astype(F32), 0, keepdims=True)
        for pair in range(own.shape[1] // LANES):
            cols = pl.ds(pair * LANES, LANES)
            values = times(mid[:, cols], inputs[:, cols])
            tap_grad[pl.ds(8 * pair, 8), :] = tap_sums(False, group_size, values, own[:, cols], halo[:, cols])


def first_grad_kernel(
    group_size, role, gate, mid, inputs, mid_halo, inputs_halo, received, filtered, tap_grad, steer_grad
):
    @pl.when(role[0] > 0)
    def _():
        for pair in range(gate.shape[1] // LANES):
            cols = pl.ds(pair * LANES, LANES)
            grad = received[:, cols]
            weighted = times(gate[:, cols], grad)
            grad_in = grad.astype(F32) + weighted.astype(F32) * filtered[:, cols]
            steer_grad[:, cols] = jnp.sum(grad_in, 0, keepdims=True)
            own, halo = times(mid[:, cols], inputs[:, cols]), times(mid_halo[:, cols], inputs_halo[:, cols])
            tap_grad[pl.ds(8 * pair, 8), :] = tap_sums(True, group_size, weighted, own, halo)


def pack_kernel(owners, role, *refs):
    refs, out = refs[:-1], refs[-1]
    count = len(refs) // 4

    def part(parts, axis, at, size):
        for ref in parts:
            if at < ref.shape[axis]:
                return ref[at : at + size, :] if axis == 0 else ref[:, at : at + size]
            at -= ref.shape[axis]

    def pack(taps, steers):
        groups = sum(ref.shape[0] for ref in taps) // owners
        channels = sum(ref.shape[1] for ref in steers) // owners
        for owner in range(owners):
            lines = [part(taps, 0, owner * groups, groups)]
            for at in range(0, channels, LANES):
                size = min(LANES, channels - at)
                steer = part(steers, 1, owner * channels + at, size)
                if size < LANES:
                    steer = jnp.concatenate([steer, jnp.zeros((1, LANES - size), F32)], 1)
                lines.append(steer)
            out[owner] = jnp.concatenate(lines, 0).astype(BF16)

    @pl.when(first_section(role))
    def _():
        pack(refs[:count], refs[count : 2 * count])

    @pl.when(jnp.logical_not(first_section(role)))
    def _():
        pack(refs[2 * count : 3 * count], refs[3 * count :])


def step_kernel(role, parts, steer_second, filter_second, steer_out, filter_out):
    total = jnp.sum(parts[...].astype(F32), 0)
    groups = filter_second.shape[0]
    tap_grad = total[:groups]
    lane = lane_of(tap_grad.shape)
    mirrored = jnp.where(lane == 0, 0, tap_grad.shape[1] - lane)
    tap_grad = jnp.take_along_axis(tap_grad, jnp.where(first_section(role), mirrored, lane), axis=1)
    filter_out[...] = tap_grad / jnp.sqrt(filter_second[...] + tap_grad * tap_grad)
    channels = steer_out.shape[1]
    for row in range(pl.cdiv(channels, LANES)):
        cols = min(LANES, channels - row * LANES)
        at = pl.ds(row * LANES, cols)
        grad = total[groups + row : groups + row + 1, :cols]
        steer_out[:, at] = grad / jnp.sqrt(steer_second[:, at] + grad * grad)


def spec(rows, width, first=0):
    return pl.BlockSpec((rows, width), lambda i: (0, i + first))


SMEM = pl.BlockSpec(memory_space=pltpu.SMEM)
ANY = pl.BlockSpec(memory_space=pl.ANY)
SMALL = pltpu.CompilerParams(vmem_limit_bytes=4 * 1024 * 1024)


def call(kernel, grid, in_specs, out_specs, out_shape, scratch=(), name=None, cycles=100, after=()):
    count = len(in_specs)

    def with_after(*refs):
        kernel(*refs[:count], *refs[count + len(after) :])

    return pl.pallas_call(
        with_after,
        grid=grid,
        in_specs=list(in_specs) + [ANY] * len(after),
        out_specs=out_specs,
        out_shape=out_shape,
        scratch_shapes=list(scratch),
        compiler_params=pltpu.CompilerParams(vmem_limit_bytes=16 * 1024 * 1024),
        cost_estimate=pl.CostEstimate(flops=cycles, bytes_accessed=0, transcendentals=0),
        name=name,
    )


def body(cotangent, in_gate, mid_gate, layer_inputs, filters, steer_second, filter_second):
    in_gate, mid_gate, layer_inputs = in_gate[0], mid_gate[0], layer_inputs[0]
    rows, channels = in_gate.shape
    filt_len, groups = filters.shape[1:]
    group_size = channels // groups
    sections, seqs = lax.axis_size("section"), lax.axis_size("seq")
    my_section = lax.axis_index("section")
    role = (my_section == 0).astype(jnp.int32).reshape(1)

    edges = [channels * eighths // 8 for eighths in CHUNK_EDGES]
    bounds = list(zip(edges[:-1], edges[1:]))
    block = channels // 8
    block_groups = block // group_size
    behind = [(seqs * s + i, seqs * s + i - 1) for s in range(1, sections) for i in range(1, seqs)]
    ahead = [(i, i + 1) for i in range(seqs - 1)]
    down = [(s, s - 1) for s in range(1, sections)]

    def bf16(width_of):
        return jax.ShapeDtypeStruct((rows, width_of), BF16)

    def weigh(incoming, first, last, offset, after):
        return call(
            weigh_kernel,
            ((last - first) // block,),
            [SMEM, spec(rows, block, first // block), spec(rows, block, (first - offset) // block)],
            spec(rows, block),
            bf16(last - first),
            name="weigh",
            after=after,
        )(role, in_gate, incoming, *after)

    def first_weigh(last):
        part = pltpu.VMEM((rows, last), BF16)
        return pl.pallas_call(
            functools.partial(first_weigh_kernel, block),
            in_specs=[SMEM] + [pl.BlockSpec(memory_space=pl.ANY)] * 2,
            out_specs=pl.BlockSpec(memory_space=pltpu.VMEM),
            out_shape=bf16(last),
            scratch_shapes=[part, part, pltpu.SemaphoreType.DMA((2, last // block))],
            compiler_params=SMALL,
            name="first_weigh",
        )(role, *[pltpu.with_memory_space_constraint(a, pltpu.HBM) for a in (in_gate, cotangent)])

    seconds = (steer_second, filter_second[0].T)
    vmem = pl.BlockSpec(memory_space=pltpu.VMEM)
    taps, *seconds = pl.pallas_call(
        taps_kernel,
        in_specs=[SMEM] + [vmem] * 3,
        out_specs=[vmem] * 3,
        out_shape=[jax.ShapeDtypeStruct((groups, filt_len), F32)]
        + [jax.ShapeDtypeStruct(second.shape, F32) for second in seconds],
        compiler_params=SMALL,
        name="taps",
    )(role, filters[0], *seconds)
    group_spec = lambda first: pl.BlockSpec((block_groups, filt_len), lambda i: (i + first, 0))

    grad_specs = [group_spec(0), pl.BlockSpec((1, block), lambda i: (0, i))]

    def grad_shapes(k):
        width = bounds[k][1] - bounds[k][0]
        return [
            jax.ShapeDtypeStruct((width // group_size, filt_len), F32),
            jax.ShapeDtypeStruct((1, width), F32),
        ]

    def upper_grad(k, after):
        first, last = bounds[k]
        own, halo, at = sources[k]
        here, there = spec(rows, block, first // block), spec(rows, block, at)
        return call(
            functools.partial(upper_grad_kernel, group_size),
            ((last - first) // block,),
            [SMEM, here, here, there, there, spec(rows, block)],
            grad_specs,
            grad_shapes(k),
            name="upper_grads",
            cycles=2000,
            after=tuple(after),
        )(role, mid_gate, layer_inputs, own, halo, outgoing[k], *after)

    def turned_filter(k, after):
        first, last = bounds[k]
        here = spec(rows, block, first // block)
        return call(
            functools.partial(turned_filter_kernel, group_size),
            ((last - first) // block,),
            [SMEM, here, here, group_spec(first // block)],
            spec(rows, block),
            jax.ShapeDtypeStruct((rows, last - first), F32),
            name="turned_filter",
            cycles=1000,
            after=tuple(after),
        )(role, mid_gate, mid_halo, taps, *after)

    incoming = [(cotangent, 0)] * len(bounds)
    early, uppers, filtered = [], [], []
    for hop in range(sections - 1):
        split = [channels * eighths // 8 for eighths in HALO_EDGES] if hop == 0 else edges
        starts, ends = split[:-1], split[1:]
        owns, halos = [], []

        def send_halo(after):
            first, last = starts[len(owns)], ends[len(owns)]
            array, offset = next(entry for entry, edge in zip(incoming, edges) if edge == first)
            if hop == 0 and first == 0:
                owns.append(first_weigh(last))
            else:
                owns.append(weigh(array, first, last, offset, after))
            halos.append(lax.ppermute(owns[-1], ("section", "seq"), behind))

        send_halo(())
        if hop == 0:
            mid_sent, inputs_sent, _ = lax.optimization_barrier((mid_gate, layer_inputs, owns[0]))
            mid_halo = lax.ppermute(mid_sent, ("section", "seq"), ahead)
            inputs_halo = lax.ppermute(inputs_sent, ("section", "seq"), ahead)
        send_halo((owns[0],))
        sources, outgoing, received = [], [], []
        for k, (first, last) in enumerate(bounds):
            part = max(i for i, start in enumerate(starts) if start <= first)
            while part >= len(owns):
                send_halo(tuple(received[:1]) + tuple(early))
            at = (first - starts[part]) // block
            array, offset = incoming[k]
            before = tuple(outgoing[-1:])
            if hop == sections - 2 and k == 2:
                uppers.append(upper_grad(1, owns[-1:]))
                filtered.append(turned_filter(0, owns[-1:]))
                filtered.append(turned_filter(1, filtered[-1:]))
                before += (uppers[-1][0], filtered[-1])
            out = call(
                functools.partial(filter_kernel, group_size),
                ((last - first) // block,),
                [SMEM, spec(rows, block, at), spec(rows, block, at), group_spec(first // block),
                 spec(rows, block, first // block), spec(rows, block, (first - offset) // block)],
                spec(rows, block),
                bf16(last - first),
                name="filter",
                cycles=1000,
                after=before,
            )(role, owns[part], halos[part], taps, mid_gate, array, *before)
            sources.append((owns[part], halos[part], at))
            outgoing.append(out)
            received.append(lax.ppermute(out, "section", down))
            if hop == sections - 2 and k == 1:
                uppers = [upper_grad(0, (out,))]
                early = [uppers[0][0]]
        top = my_section == sections - 1
        incoming = [
            (jnp.where(top, cotangent[:, first:last], arrived), first)
            for (first, last), arrived in zip(bounds, received)
        ]

    latest = outgoing[-1:]
    for k in range(len(filtered), len(bounds)):
        filtered.append(turned_filter(k, latest))
        latest = filtered[-1:]
    for k in range(len(uppers), len(bounds)):
        uppers.append(upper_grad(k, latest))
        latest = uppers[-1][:1]
    firsts = []
    for k, (first, last) in enumerate(bounds):
        here = spec(rows, block, first // block)
        firsts.append(call(
            functools.partial(first_grad_kernel, group_size),
            ((last - first) // block,),
            [SMEM, here, here, here, here, here, spec(rows, block), spec(rows, block)],
            grad_specs,
            grad_shapes(k),
            name="first_grads",
            cycles=2000,
            after=tuple(latest),
        )(role, in_gate, mid_gate, layer_inputs, mid_halo, inputs_halo, received[k], filtered[k], *latest))
        latest = firsts[-1][:1]
    partial_sums = [grads[i] for both in (firsts, uppers) for i in range(2) for grads in both]

    own_channels = channels // seqs
    lines = groups // seqs + pl.cdiv(own_channels, LANES)
    packed = pl.pallas_call(
        functools.partial(pack_kernel, seqs),
        in_specs=[SMEM] + [vmem] * len(partial_sums),
        out_specs=vmem,
        out_shape=jax.ShapeDtypeStruct((seqs, lines, LANES), BF16),
        compiler_params=SMALL,
        name="pack",
    )(role, *partial_sums)
    parts = lax.all_to_all(packed, "seq", 0, 0)
    steer_step, filter_step = pl.pallas_call(
        step_kernel,
        in_specs=[SMEM] + [vmem] * 3,
        out_shape=[
            jax.ShapeDtypeStruct((1, own_channels), F32),
            jax.ShapeDtypeStruct((groups // seqs, filt_len), F32),
        ],
        compiler_params=SMALL,
        name="step",
    )(role, parts, *seconds)
    return steer_step, filter_step.T[None]


def solution(mesh):
    in_specs = (
        P("seq", None),
        P("section", "seq", None),
        P("section", "seq", None),
        P("section", "seq", None),
        P("section", None, None),
        P("section", "seq"),
        P("section", None, "seq"),
    )
    out_specs = (P("section", "seq"), P("section", None, "seq"))
    return jax.shard_map(body, mesh=mesh, in_specs=in_specs, out_specs=out_specs, check_vma=False)
```

```python
import functools

import jax
import jax.numpy as jnp
from jax import lax
from jax.experimental import pallas as pl
from jax.experimental.pallas import tpu as pltpu
from jax.sharding import PartitionSpec as P

F32 = jnp.float32
BF16 = jnp.bfloat16
LANES = 128
SUB = 32
CHUNK_EDGES = (0, 3, 6, 7, 8)
HALO_EDGES = (0, 3, 6, 8)


def lane_of(shape):
    return lax.broadcasted_iota(jnp.int32, shape, 1)


def row_of(shape):
    return lax.broadcasted_iota(jnp.int32, shape, 0)


def first_section(role):
    return (role[0] & 1) > 0


def times(a, b):
    return (a.astype(F32) * b.astype(F32)).astype(BF16)


def turned(x):
    return pltpu.roll(x, LANES // 2, 1)


def spread(x, x_turned, parity, count):
    low = lane_of((count, LANES)) < LANES // 2
    natural, other = (x, x_turned) if parity == 0 else (x_turned, x)
    tiles = []
    for first in (0, 2 * SUB):
        tiles.append(jnp.where(low, natural[first : first + count], other[first + SUB : first + SUB + count]))
    return jnp.concatenate(tiles, 1)


def gathered(even, odd):
    low = lane_of((SUB, LANES)) < LANES // 2
    out = []
    for tile in range(2):
        a = even[:, tile * LANES : (tile + 1) * LANES]
        b = odd[:, tile * LANES : (tile + 1) * LANES]
        out.append(jnp.where(low, a, turned(b)))
        out.append(jnp.where(low, turned(a), b))
    return jnp.concatenate(out, 0)


def in_order(reverse, own, halo):
    return jnp.concatenate([jnp.where(reverse, halo, own), jnp.where(reverse, own, halo)], 0)


def diagonal_sums(blocks):
    tiles = []
    for block in blocks:
        tile = block[:8]
        for first in range(8, SUB, 8):
            tile = tile + pltpu.roll(block[first : first + 8], LANES - first, 1)
        tiles.append(tile)
    row = row_of((8, LANES))
    for fold in (4, 2, 1):
        upper = row % (2 * fold) < fold
        tiles = [
            jnp.where(upper, a, pltpu.roll(b, fold, 0))
            + pltpu.roll(jnp.where(upper, pltpu.roll(a, 8 - fold, 0), b), LANES - fold, 1)
            for a, b in zip(tiles[:fold], tiles[fold:])
        ]
    return tiles[0]


def near(reverse_int, shape):
    return lane_of(shape) - row_of(shape) >= reverse_int


def tap_matrix(reverse, taps_by_group):
    taps = taps_by_group.shape[0]
    source = row_of((taps, taps))
    target = lane_of((taps, taps))
    mirrored = jnp.where(source == 0, 0, taps - source)
    pick = jnp.where(target == jnp.where(reverse, mirrored, source), 1.0, 0.0)
    return pick, taps


def weigh_kernel(role, gate, incoming, out):
    @pl.when(jnp.logical_not(first_section(role)))
    def _():
        out[...] = times(gate[...], incoming[...])


def direct_weigh_kernel(first, block, role, gate, incoming, out, gate_part, incoming_part, sems):
    @pl.when(jnp.logical_not(first_section(role)))
    def _():
        tiles = [pl.ds(at, block) for at in range(0, out.shape[1], block)]
        copies = [
            [
                pltpu.make_async_copy(source.at[:, pl.ds(first + i * block, block)], part.at[:, t], sems.at[which, i])
                for which, (source, part) in enumerate(((gate, gate_part), (incoming, incoming_part)))
            ]
            for i, t in enumerate(tiles)
        ]
        for pair in copies:
            for copy in pair:
                copy.start()
        for t, pair in zip(tiles, copies):
            for copy in pair:
                copy.wait()
            out[:, t] = times(gate_part[:, t], incoming_part[:, t])


def moments_kernel(role, steer_second, filter_second, *refs):
    steer_out, filter_out = refs[-2:]
    steer_out[...] = steer_second[...]
    filter_out[...] = filter_second[...]


def taps_kernel(role, filters, taps_out):
    pick, _ = tap_matrix(first_section(role), filters[...])
    taps_out[...] = lax.dot_general(
        filters[...], pick.astype(BF16), (((0,), (0,)), ((), ())), preferred_element_type=F32
    )


def convolved(reverse, group_size, own, halo, taps, first_group):
    half = LANES // 2
    per_half = half // group_size
    mask = near(int(reverse), (SUB, LANES))
    zero = jnp.zeros((SUB, LANES), F32)
    lane_group = (lane_of((SUB, 2 * LANES)) % half) // group_size
    ext = jnp.concatenate([halo, own] if reverse else [own, halo], 0)
    ext_turned = turned(ext)
    results = []
    for parity in range(2):
        window = spread(ext, ext_turned, parity, own.shape[0] + SUB)
        bands = []
        for g in range(per_half):
            row = taps[pl.ds(first_group + parity * per_half + g, 1), :]
            circ = pltpu.roll(jnp.broadcast_to(row, (SUB, LANES)), 0, 1, stride=1, stride_axis=0)
            band = jnp.concatenate([jnp.where(mask, circ, zero), jnp.where(mask, zero, circ)[:, :SUB]], 1)
            bands.append(band.astype(BF16))
        product = jnp.dot(jnp.concatenate(bands, 0), window, preferred_element_type=F32)
        total = product[:SUB]
        for g in range(1, per_half):
            total = jnp.where(lane_group == g, product[g * SUB : (g + 1) * SUB], total)
        results.append(total)
    return gathered(*results)


def filter_kernel(group_size, role, own, halo, taps, mid, incoming, outgoing):
    @pl.when(jnp.logical_not(first_section(role)))
    def _():
        for first in range(0, own.shape[1], LANES):
            cols = pl.ds(first, LANES)
            conv = convolved(False, group_size, own[:, cols], halo[:, cols], taps, first // group_size)
            outgoing[:, cols] = (
                incoming[:, cols].astype(F32) + mid[:, cols].astype(F32) * conv
            ).astype(BF16)


def turned_filter_kernel(group_size, role, mid, mid_halo, taps, filtered):
    @pl.when(first_section(role))
    def _():
        for first in range(0, mid.shape[1], LANES):
            cols = pl.ds(first, LANES)
            filtered[:, cols] = convolved(True, group_size, mid[:, cols], mid_halo[:, cols], taps, first // group_size)


def tap_sums(reverse, group_size, left, own, halo):
    half = LANES // 2
    per_half = half // group_size
    mask = near(int(reverse), (SUB, LANES))
    lane_group = (lane_of((SUB, 2 * LANES)) % half) // group_size
    nothing = jnp.zeros((SUB, 2 * LANES), BF16)
    ext = jnp.concatenate([halo, own] if reverse else [own, halo], 0)
    ext_turned, left_turned = turned(ext), turned(left)
    blocks = []
    for parity in range(2):
        window = spread(ext, ext_turned, parity, own.shape[0] + SUB)
        short = spread(left, left_turned, parity, SUB)
        lhs = jnp.concatenate([jnp.where(lane_group == g, short, nothing) for g in range(per_half)], 0)
        product = lax.dot_general(lhs, window, (((1,), (1,)), ((), ())), preferred_element_type=F32)
        for g in range(per_half):
            block = product[g * SUB : (g + 1) * SUB]
            late = jnp.concatenate([block[:, LANES:], jnp.zeros((SUB, LANES - SUB), F32)], 1)
            blocks.append(jnp.where(mask, block[:, :LANES], late))
    return diagonal_sums(blocks)


def upper_grad_kernel(group_size, role, mid, inputs, own, halo, outgoing, tap_grad, steer_grad):
    @pl.when(role[0] == 0)
    def _():
        steer_grad[...] = jnp.sum(outgoing[...].astype(F32), 0, keepdims=True)
        for pair in range(own.shape[1] // LANES):
            cols = pl.ds(pair * LANES, LANES)
            values = times(mid[:, cols], inputs[:, cols])
            tap_grad[pl.ds(8 * pair, 8), :] = tap_sums(False, group_size, values, own[:, cols], halo[:, cols])


def first_grad_kernel(
    group_size, role, gate, mid, inputs, mid_halo, inputs_halo, received, filtered, tap_grad, steer_grad
):
    @pl.when(role[0] > 0)
    def _():
        for pair in range(gate.shape[1] // LANES):
            cols = pl.ds(pair * LANES, LANES)
            grad = received[:, cols]
            weighted = times(gate[:, cols], grad)
            grad_in = grad.astype(F32) + weighted.astype(F32) * filtered[:, cols]
            steer_grad[:, cols] = jnp.sum(grad_in, 0, keepdims=True)
            own, halo = times(mid[:, cols], inputs[:, cols]), times(mid_halo[:, cols], inputs_halo[:, cols])
            tap_grad[pl.ds(8 * pair, 8), :] = tap_sums(True, group_size, weighted, own, halo)


def pack_kernel(owners, role, *refs):
    refs, out = refs[:-1], refs[-1]
    count = len(refs) // 4

    def part(parts, axis, at, size):
        for ref in parts:
            if at < ref.shape[axis]:
                return ref[at : at + size, :] if axis == 0 else ref[:, at : at + size]
            at -= ref.shape[axis]

    def pack(taps, steers):
        groups = sum(ref.shape[0] for ref in taps) // owners
        channels = sum(ref.shape[1] for ref in steers) // owners
        for owner in range(owners):
            lines = [part(taps, 0, owner * groups, groups)]
            for at in range(0, channels, LANES):
                size = min(LANES, channels - at)
                steer = part(steers, 1, owner * channels + at, size)
                if size < LANES:
                    steer = jnp.concatenate([steer, jnp.zeros((1, LANES - size), F32)], 1)
                lines.append(steer)
            out[owner] = jnp.concatenate(lines, 0).astype(BF16)

    @pl.when(first_section(role))
    def _():
        pack(refs[:count], refs[count : 2 * count])

    @pl.when(jnp.logical_not(first_section(role)))
    def _():
        pack(refs[2 * count : 3 * count], refs[3 * count :])


def step_kernel(role, parts, steer_second, filter_second, steer_out, filter_out):
    total = jnp.sum(parts[...].astype(F32), 0)
    groups = filter_second.shape[0]
    tap_grad = total[:groups]
    lane = lane_of(tap_grad.shape)
    mirrored = jnp.where(lane == 0, 0, tap_grad.shape[1] - lane)
    tap_grad = jnp.take_along_axis(tap_grad, jnp.where(first_section(role), mirrored, lane), axis=1)
    filter_out[...] = tap_grad / jnp.sqrt(filter_second[...] + tap_grad * tap_grad)
    channels = steer_out.shape[1]
    for row in range(pl.cdiv(channels, LANES)):
        cols = min(LANES, channels - row * LANES)
        at = pl.ds(row * LANES, cols)
        grad = total[groups + row : groups + row + 1, :cols]
        steer_out[:, at] = grad / jnp.sqrt(steer_second[:, at] + grad * grad)


def spec(rows, width, first=0):
    return pl.BlockSpec((rows, width), lambda i: (0, i + first))


SMEM = pl.BlockSpec(memory_space=pltpu.SMEM)
ANY = pl.BlockSpec(memory_space=pl.ANY)
SMALL = pltpu.CompilerParams(vmem_limit_bytes=4 * 1024 * 1024)


def call(kernel, grid, in_specs, out_specs, out_shape, scratch=(), name=None, cycles=100, after=()):
    count = len(in_specs)

    def with_after(*refs):
        kernel(*refs[:count], *refs[count + len(after) :])

    return pl.pallas_call(
        with_after,
        grid=grid,
        in_specs=list(in_specs) + [ANY] * len(after),
        out_specs=out_specs,
        out_shape=out_shape,
        scratch_shapes=list(scratch),
        compiler_params=pltpu.CompilerParams(vmem_limit_bytes=16 * 1024 * 1024),
        cost_estimate=pl.CostEstimate(flops=cycles, bytes_accessed=0, transcendentals=0),
        name=name,
    )


def body(cotangent, in_gate, mid_gate, layer_inputs, filters, steer_second, filter_second):
    in_gate, mid_gate, layer_inputs = in_gate[0], mid_gate[0], layer_inputs[0]
    rows, channels = in_gate.shape
    filt_len, groups = filters.shape[1:]
    group_size = channels // groups
    sections, seqs = lax.axis_size("section"), lax.axis_size("seq")
    my_section = lax.axis_index("section")
    role = (my_section == 0).astype(jnp.int32).reshape(1)

    edges = [channels * eighths // 8 for eighths in CHUNK_EDGES]
    bounds = list(zip(edges[:-1], edges[1:]))
    block = channels // 8
    block_groups = block // group_size
    behind = [(seqs * s + i, seqs * s + i - 1) for s in range(1, sections) for i in range(1, seqs)]
    ahead = [(i, i + 1) for i in range(seqs - 1)]
    down = [(s, s - 1) for s in range(1, sections)]

    def bf16(width_of):
        return jax.ShapeDtypeStruct((rows, width_of), BF16)

    def weigh(incoming, first, last, offset, after):
        return call(
            weigh_kernel,
            ((last - first) // block,),
            [SMEM, spec(rows, block, first // block), spec(rows, block, (first - offset) // block)],
            spec(rows, block),
            bf16(last - first),
            name="weigh",
            after=after,
        )(role, in_gate, incoming, *after)

    def direct_weigh(first, last, after):
        width = last - first
        part = pltpu.VMEM((rows, width), BF16)

        def kernel(*refs):
            direct_weigh_kernel(first, block, *refs[:3], *refs[3 + len(after) :])

        return pl.pallas_call(
            kernel,
            in_specs=[SMEM] + [ANY] * (2 + len(after)),
            out_specs=pl.BlockSpec(memory_space=pltpu.VMEM),
            out_shape=bf16(width),
            scratch_shapes=[part, part, pltpu.SemaphoreType.DMA((2, width // block))],
            compiler_params=SMALL,
            name="direct_weigh",
        )(role, *[pltpu.with_memory_space_constraint(a, pltpu.HBM) for a in (in_gate, cotangent)], *after)

    vmem = pl.BlockSpec(memory_space=pltpu.VMEM)
    taps = pl.pallas_call(
        taps_kernel,
        in_specs=[SMEM, vmem],
        out_specs=vmem,
        out_shape=jax.ShapeDtypeStruct((groups, filt_len), F32),
        compiler_params=SMALL,
        name="taps",
    )(role, filters[0])

    def moments(after):
        seconds = (steer_second, filter_second[0].T)
        return pl.pallas_call(
            moments_kernel,
            in_specs=[SMEM] + [vmem] * 2 + [ANY] * len(after),
            out_specs=[vmem] * 2,
            out_shape=[jax.ShapeDtypeStruct(second.shape, F32) for second in seconds],
            compiler_params=SMALL,
            name="moments",
        )(role, *seconds, *after)

    group_spec = lambda first: pl.BlockSpec((block_groups, filt_len), lambda i: (i + first, 0))

    grad_specs = [group_spec(0), pl.BlockSpec((1, block), lambda i: (0, i))]

    def grad_shapes(k):
        width = bounds[k][1] - bounds[k][0]
        return [
            jax.ShapeDtypeStruct((width // group_size, filt_len), F32),
            jax.ShapeDtypeStruct((1, width), F32),
        ]

    def upper_grad(k, after):
        first, last = bounds[k]
        own, halo, at = sources[k]
        here, there = spec(rows, block, first // block), spec(rows, block, at)
        return call(
            functools.partial(upper_grad_kernel, group_size),
            ((last - first) // block,),
            [SMEM, here, here, there, there, spec(rows, block)],
            grad_specs,
            grad_shapes(k),
            name="upper_grads",
            cycles=2000,
            after=tuple(after),
        )(role, mid_gate, layer_inputs, own, halo, outgoing[k], *after)

    def turned_filter(k, after):
        first, last = bounds[k]
        here = spec(rows, block, first // block)
        return call(
            functools.partial(turned_filter_kernel, group_size),
            ((last - first) // block,),
            [SMEM, here, here, group_spec(first // block)],
            spec(rows, block),
            jax.ShapeDtypeStruct((rows, last - first), F32),
            name="turned_filter",
            cycles=1000,
            after=tuple(after),
        )(role, mid_gate, mid_halo, taps, *after)

    incoming = [(cotangent, 0)] * len(bounds)
    early, uppers, filtered = [], [], []
    for hop in range(sections - 1):
        split = [channels * eighths // 8 for eighths in HALO_EDGES] if hop == 0 else edges
        starts, ends = split[:-1], split[1:]
        owns, halos = [], []

        def send_halo(after):
            first, last = starts[len(owns)], ends[len(owns)]
            array, offset = next(entry for entry, edge in zip(incoming, edges) if edge == first)
            if hop == 0 and not early:
                owns.append(direct_weigh(first, last, after))
            else:
                owns.append(weigh(array, first, last, offset, after))
            halos.append(lax.ppermute(owns[-1], ("section", "seq"), behind))

        send_halo(())
        if hop == 0:
            mid_sent, inputs_sent, _ = lax.optimization_barrier((mid_gate, layer_inputs, owns[0]))
            mid_halo = lax.ppermute(mid_sent, ("section", "seq"), ahead)
            inputs_halo = lax.ppermute(inputs_sent, ("section", "seq"), ahead)
        send_halo((owns[0],))
        sources, outgoing, received = [], [], []
        for k, (first, last) in enumerate(bounds):
            part = max(i for i, start in enumerate(starts) if start <= first)
            while part >= len(owns):
                send_halo(tuple(received[:1]) + tuple(early))
            at = (first - starts[part]) // block
            array, offset = incoming[k]
            before = tuple(outgoing[-1:])
            if hop == sections - 2 and k == 2:
                uppers.append(upper_grad(1, owns[-1:]))
                filtered.append(turned_filter(0, owns[-1:]))
                filtered.append(turned_filter(1, filtered[-1:]))
                before += (uppers[-1][0], filtered[-1])
            out = call(
                functools.partial(filter_kernel, group_size),
                ((last - first) // block,),
                [SMEM, spec(rows, block, at), spec(rows, block, at), group_spec(first // block),
                 spec(rows, block, first // block), spec(rows, block, (first - offset) // block)],
                spec(rows, block),
                bf16(last - first),
                name="filter",
                cycles=1000,
                after=before,
            )(role, owns[part], halos[part], taps, mid_gate, array, *before)
            sources.append((owns[part], halos[part], at))
            outgoing.append(out)
            received.append(lax.ppermute(out, "section", down))
            if hop == sections - 2 and k == 1:
                uppers = [upper_grad(0, (out,))]
                seconds = moments((out,))
                early = [uppers[0][0], seconds[0]]
        top = my_section == sections - 1
        incoming = [
            (jnp.where(top, cotangent[:, first:last], arrived), first)
            for (first, last), arrived in zip(bounds, received)
        ]

    latest = outgoing[-1:]
    for k in range(len(filtered), len(bounds)):
        filtered.append(turned_filter(k, latest))
        latest = filtered[-1:]
    for k in range(len(uppers), len(bounds)):
        uppers.append(upper_grad(k, latest))
        latest = uppers[-1][:1]
    firsts = []
    for k, (first, last) in enumerate(bounds):
        here = spec(rows, block, first // block)
        firsts.append(call(
            functools.partial(first_grad_kernel, group_size),
            ((last - first) // block,),
            [SMEM, here, here, here, here, here, spec(rows, block), spec(rows, block)],
            grad_specs,
            grad_shapes(k),
            name="first_grads",
            cycles=2000,
            after=tuple(latest),
        )(role, in_gate, mid_gate, layer_inputs, mid_halo, inputs_halo, received[k], filtered[k], *latest))
        latest = firsts[-1][:1]
    partial_sums = [grads[i] for both in (firsts, uppers) for i in range(2) for grads in both]

    own_channels = channels // seqs
    lines = groups // seqs + pl.cdiv(own_channels, LANES)
    packed = pl.pallas_call(
        functools.partial(pack_kernel, seqs),
        in_specs=[SMEM] + [vmem] * len(partial_sums),
        out_specs=vmem,
        out_shape=jax.ShapeDtypeStruct((seqs, lines, LANES), BF16),
        compiler_params=SMALL,
        name="pack",
    )(role, *partial_sums)
    parts = lax.all_to_all(packed, "seq", 0, 0)
    steer_step, filter_step = pl.pallas_call(
        step_kernel,
        in_specs=[SMEM] + [vmem] * 3,
        out_shape=[
            jax.ShapeDtypeStruct((1, own_channels), F32),
            jax.ShapeDtypeStruct((groups // seqs, filt_len), F32),
        ],
        compiler_params=SMALL,
        name="step",
    )(role, parts, *seconds)
    return steer_step, filter_step.T[None]


def solution(mesh):
    in_specs = (
        P("seq", None),
        P("section", "seq", None),
        P("section", "seq", None),
        P("section", "seq", None),
        P("section", None, None),
        P("section", "seq"),
        P("section", None, "seq"),
    )
    out_specs = (P("section", "seq"), P("section", None, "seq"))
    return jax.shard_map(body, mesh=mesh, in_specs=in_specs, out_specs=out_specs, check_vma=False)
```

```python
import functools

import jax
import jax.numpy as jnp
from jax import lax
from jax.experimental import pallas as pl
from jax.experimental.pallas import tpu as pltpu
from jax.sharding import PartitionSpec as P

F32 = jnp.float32
BF16 = jnp.bfloat16
LANES = 128
SUB = 32
CHUNK_EDGES = (0, 3, 6, 7, 8)
HALO_EDGES = (0, 3, 6, 8)


def lane_of(shape):
    return lax.broadcasted_iota(jnp.int32, shape, 1)


def row_of(shape):
    return lax.broadcasted_iota(jnp.int32, shape, 0)


def first_section(role):
    return (role[0] & 1) > 0


def times(a, b):
    return (a.astype(F32) * b.astype(F32)).astype(BF16)


def turned(x):
    return pltpu.roll(x, LANES // 2, 1)


def spread(x, x_turned, parity, count):
    low = lane_of((count, LANES)) < LANES // 2
    natural, other = (x, x_turned) if parity == 0 else (x_turned, x)
    tiles = []
    for first in (0, 2 * SUB):
        tiles.append(jnp.where(low, natural[first : first + count], other[first + SUB : first + SUB + count]))
    return jnp.concatenate(tiles, 1)


def gathered(even, odd):
    low = lane_of((SUB, LANES)) < LANES // 2
    out = []
    for tile in range(2):
        a = even[:, tile * LANES : (tile + 1) * LANES]
        b = odd[:, tile * LANES : (tile + 1) * LANES]
        out.append(jnp.where(low, a, turned(b)))
        out.append(jnp.where(low, turned(a), b))
    return jnp.concatenate(out, 0)


def in_order(reverse, own, halo):
    return jnp.concatenate([jnp.where(reverse, halo, own), jnp.where(reverse, own, halo)], 0)


def diagonal_sums(blocks):
    tiles = []
    for block in blocks:
        tile = block[:8]
        for first in range(8, SUB, 8):
            tile = tile + pltpu.roll(block[first : first + 8], LANES - first, 1)
        tiles.append(tile)
    row = row_of((8, LANES))
    for fold in (4, 2, 1):
        upper = row % (2 * fold) < fold
        tiles = [
            jnp.where(upper, a, pltpu.roll(b, fold, 0))
            + pltpu.roll(jnp.where(upper, pltpu.roll(a, 8 - fold, 0), b), LANES - fold, 1)
            for a, b in zip(tiles[:fold], tiles[fold:])
        ]
    return tiles[0]


def near(reverse_int, shape):
    return lane_of(shape) - row_of(shape) >= reverse_int


def tap_matrix(reverse, taps_by_group):
    taps = taps_by_group.shape[0]
    source = row_of((taps, taps))
    target = lane_of((taps, taps))
    mirrored = jnp.where(source == 0, 0, taps - source)
    pick = jnp.where(target == jnp.where(reverse, mirrored, source), 1.0, 0.0)
    return pick, taps


def weigh_kernel(role, gate, incoming, out):
    @pl.when(jnp.logical_not(first_section(role)))
    def _():
        out[...] = times(gate[...], incoming[...])


def direct_weigh_kernel(first, block, role, gate, incoming, out, gate_part, incoming_part, sems):
    @pl.when(jnp.logical_not(first_section(role)))
    def _():
        tiles = [pl.ds(at, block) for at in range(0, out.shape[1], block)]
        copies = [
            [
                pltpu.make_async_copy(source.at[:, pl.ds(first + i * block, block)], part.at[:, t], sems.at[which, i])
                for which, (source, part) in enumerate(((gate, gate_part), (incoming, incoming_part)))
            ]
            for i, t in enumerate(tiles)
        ]
        for pair in copies:
            for copy in pair:
                copy.start()
        for t, pair in zip(tiles, copies):
            for copy in pair:
                copy.wait()
            out[:, t] = times(gate_part[:, t], incoming_part[:, t])


def moments_kernel(role, steer_second, filter_second, *refs):
    steer_out, filter_out = refs[-2:]
    steer_out[...] = steer_second[...]
    filter_out[...] = filter_second[...]


def taps_kernel(role, filters, taps_out):
    pick, _ = tap_matrix(first_section(role), filters[...])
    taps_out[...] = lax.dot_general(
        filters[...], pick.astype(BF16), (((0,), (0,)), ((), ())), preferred_element_type=F32
    )


def convolved(reverse, group_size, own, halo, taps, first_group):
    half = LANES // 2
    per_half = half // group_size
    mask = near(int(reverse), (SUB, LANES))
    zero = jnp.zeros((SUB, LANES), F32)
    lane_group = (lane_of((SUB, 2 * LANES)) % half) // group_size
    ext = jnp.concatenate([halo, own] if reverse else [own, halo], 0)
    ext_turned = turned(ext)
    results = []
    for parity in range(2):
        window = spread(ext, ext_turned, parity, own.shape[0] + SUB)
        bands = []
        for g in range(per_half):
            row = taps[pl.ds(first_group + parity * per_half + g, 1), :]
            circ = pltpu.roll(jnp.broadcast_to(row, (SUB, LANES)), 0, 1, stride=1, stride_axis=0)
            band = jnp.concatenate([jnp.where(mask, circ, zero), jnp.where(mask, zero, circ)[:, :SUB]], 1)
            bands.append(band.astype(BF16))
        product = jnp.dot(jnp.concatenate(bands, 0), window, preferred_element_type=F32)
        total = product[:SUB]
        for g in range(1, per_half):
            total = jnp.where(lane_group == g, product[g * SUB : (g + 1) * SUB], total)
        results.append(total)
    return gathered(*results)


def filter_kernel(group_size, role, own, halo, taps, mid, incoming, outgoing):
    @pl.when(jnp.logical_not(first_section(role)))
    def _():
        for first in range(0, own.shape[1], LANES):
            cols = pl.ds(first, LANES)
            conv = convolved(False, group_size, own[:, cols], halo[:, cols], taps, first // group_size)
            outgoing[:, cols] = (
                incoming[:, cols].astype(F32) + mid[:, cols].astype(F32) * conv
            ).astype(BF16)


def turned_filter_kernel(group_size, role, mid, mid_halo, taps, filtered):
    @pl.when(first_section(role))
    def _():
        for first in range(0, mid.shape[1], LANES):
            cols = pl.ds(first, LANES)
            filtered[:, cols] = convolved(True, group_size, mid[:, cols], mid_halo[:, cols], taps, first // group_size)


def tap_sums(reverse, group_size, left, own, halo):
    half = LANES // 2
    per_half = half // group_size
    mask = near(int(reverse), (SUB, LANES))
    lane_group = (lane_of((SUB, 2 * LANES)) % half) // group_size
    nothing = jnp.zeros((SUB, 2 * LANES), BF16)
    ext = jnp.concatenate([halo, own] if reverse else [own, halo], 0)
    ext_turned, left_turned = turned(ext), turned(left)
    blocks = []
    for parity in range(2):
        window = spread(ext, ext_turned, parity, own.shape[0] + SUB)
        short = spread(left, left_turned, parity, SUB)
        lhs = jnp.concatenate([jnp.where(lane_group == g, short, nothing) for g in range(per_half)], 0)
        product = lax.dot_general(lhs, window, (((1,), (1,)), ((), ())), preferred_element_type=F32)
        for g in range(per_half):
            block = product[g * SUB : (g + 1) * SUB]
            late = jnp.concatenate([block[:, LANES:], jnp.zeros((SUB, LANES - SUB), F32)], 1)
            blocks.append(jnp.where(mask, block[:, :LANES], late))
    return diagonal_sums(blocks)


def upper_grad_kernel(group_size, role, mid, inputs, own, halo, outgoing, tap_grad, steer_grad):
    @pl.when(role[0] == 0)
    def _():
        steer_grad[...] = jnp.sum(outgoing[...].astype(F32), 0, keepdims=True)
        for pair in range(own.shape[1] // LANES):
            cols = pl.ds(pair * LANES, LANES)
            values = times(mid[:, cols], inputs[:, cols])
            tap_grad[pl.ds(8 * pair, 8), :] = tap_sums(False, group_size, values, own[:, cols], halo[:, cols])


def first_grad_kernel(
    group_size, role, gate, mid, inputs, mid_halo, inputs_halo, received, filtered, tap_grad, steer_grad
):
    @pl.when(role[0] > 0)
    def _():
        for pair in range(gate.shape[1] // LANES):
            cols = pl.ds(pair * LANES, LANES)
            grad = received[:, cols]
            weighted = times(gate[:, cols], grad)
            grad_in = grad.astype(F32) + weighted.astype(F32) * filtered[:, cols]
            steer_grad[:, cols] = jnp.sum(grad_in, 0, keepdims=True)
            own, halo = times(mid[:, cols], inputs[:, cols]), times(mid_halo[:, cols], inputs_halo[:, cols])
            tap_grad[pl.ds(8 * pair, 8), :] = tap_sums(True, group_size, weighted, own, halo)


def pack_kernel(owners, role, *refs):
    refs, out = refs[:-1], refs[-1]
    count = len(refs) // 4

    def part(parts, axis, at, size):
        for ref in parts:
            if at < ref.shape[axis]:
                return ref[at : at + size, :] if axis == 0 else ref[:, at : at + size]
            at -= ref.shape[axis]

    def pack(taps, steers):
        groups = sum(ref.shape[0] for ref in taps) // owners
        channels = sum(ref.shape[1] for ref in steers) // owners
        for owner in range(owners):
            lines = [part(taps, 0, owner * groups, groups)]
            for at in range(0, channels, LANES):
                size = min(LANES, channels - at)
                steer = part(steers, 1, owner * channels + at, size)
                if size < LANES:
                    steer = jnp.concatenate([steer, jnp.zeros((1, LANES - size), F32)], 1)
                lines.append(steer)
            out[owner] = jnp.concatenate(lines, 0).astype(BF16)

    @pl.when(first_section(role))
    def _():
        pack(refs[:count], refs[count : 2 * count])

    @pl.when(jnp.logical_not(first_section(role)))
    def _():
        pack(refs[2 * count : 3 * count], refs[3 * count :])


def step_kernel(role, parts, steer_second, filter_second, steer_out, filter_out):
    total = jnp.sum(parts[...].astype(F32), 0)
    groups = filter_second.shape[0]
    tap_grad = total[:groups]
    lane = lane_of(tap_grad.shape)
    mirrored = jnp.where(lane == 0, 0, tap_grad.shape[1] - lane)
    tap_grad = jnp.take_along_axis(tap_grad, jnp.where(first_section(role), mirrored, lane), axis=1)
    filter_out[...] = tap_grad / jnp.sqrt(filter_second[...] + tap_grad * tap_grad)
    channels = steer_out.shape[1]
    for row in range(pl.cdiv(channels, LANES)):
        cols = min(LANES, channels - row * LANES)
        at = pl.ds(row * LANES, cols)
        grad = total[groups + row : groups + row + 1, :cols]
        steer_out[:, at] = grad / jnp.sqrt(steer_second[:, at] + grad * grad)


def spec(rows, width, first=0):
    return pl.BlockSpec((rows, width), lambda i: (0, i + first))


SMEM = pl.BlockSpec(memory_space=pltpu.SMEM)
ANY = pl.BlockSpec(memory_space=pl.ANY)
SMALL = pltpu.CompilerParams(vmem_limit_bytes=4 * 1024 * 1024)


def call(kernel, grid, in_specs, out_specs, out_shape, scratch=(), name=None, cycles=100, after=()):
    count = len(in_specs)

    def with_after(*refs):
        kernel(*refs[:count], *refs[count + len(after) :])

    return pl.pallas_call(
        with_after,
        grid=grid,
        in_specs=list(in_specs) + [ANY] * len(after),
        out_specs=out_specs,
        out_shape=out_shape,
        scratch_shapes=list(scratch),
        compiler_params=pltpu.CompilerParams(vmem_limit_bytes=16 * 1024 * 1024),
        cost_estimate=pl.CostEstimate(flops=cycles, bytes_accessed=0, transcendentals=0),
        name=name,
    )


def body(cotangent, in_gate, mid_gate, layer_inputs, filters, steer_second, filter_second):
    in_gate, mid_gate, layer_inputs = in_gate[0], mid_gate[0], layer_inputs[0]
    rows, channels = in_gate.shape
    filt_len, groups = filters.shape[1:]
    group_size = channels // groups
    sections, seqs = lax.axis_size("section"), lax.axis_size("seq")
    my_section = lax.axis_index("section")
    role = (my_section == 0).astype(jnp.int32).reshape(1)

    edges = [channels * eighths // 8 for eighths in CHUNK_EDGES]
    bounds = list(zip(edges[:-1], edges[1:]))
    block = channels // 8
    block_groups = block // group_size
    behind = [(seqs * s + i, seqs * s + i - 1) for s in range(1, sections) for i in range(1, seqs)]
    ahead = [(i, i + 1) for i in range(seqs - 1)]
    down = [(s, s - 1) for s in range(1, sections)]

    def bf16(width_of):
        return jax.ShapeDtypeStruct((rows, width_of), BF16)

    def weigh(incoming, first, last, offset, after):
        return call(
            weigh_kernel,
            ((last - first) // block,),
            [SMEM, spec(rows, block, first // block), spec(rows, block, (first - offset) // block)],
            spec(rows, block),
            bf16(last - first),
            name="weigh",
            after=after,
        )(role, in_gate, incoming, *after)

    def direct_weigh(first, last, after):
        width = last - first
        part = pltpu.VMEM((rows, width), BF16)

        def kernel(*refs):
            direct_weigh_kernel(first, block, *refs[:3], *refs[3 + len(after) :])

        return pl.pallas_call(
            kernel,
            in_specs=[SMEM] + [ANY] * (2 + len(after)),
            out_specs=pl.BlockSpec(memory_space=pltpu.VMEM),
            out_shape=bf16(width),
            scratch_shapes=[part, part, pltpu.SemaphoreType.DMA((2, width // block))],
            compiler_params=SMALL,
            name="direct_weigh",
        )(role, *[pltpu.with_memory_space_constraint(a, pltpu.HBM) for a in (in_gate, cotangent)], *after)

    vmem = pl.BlockSpec(memory_space=pltpu.VMEM)
    taps = pl.pallas_call(
        taps_kernel,
        in_specs=[SMEM, vmem],
        out_specs=vmem,
        out_shape=jax.ShapeDtypeStruct((groups, filt_len), F32),
        compiler_params=SMALL,
        name="taps",
    )(role, filters[0])

    def moments(after):
        seconds = (steer_second, filter_second[0].T)
        return pl.pallas_call(
            moments_kernel,
            in_specs=[SMEM] + [vmem] * 2 + [ANY] * len(after),
            out_specs=[vmem] * 2,
            out_shape=[jax.ShapeDtypeStruct(second.shape, F32) for second in seconds],
            compiler_params=SMALL,
            name="moments",
        )(role, *seconds, *after)

    group_spec = lambda first: pl.BlockSpec((block_groups, filt_len), lambda i: (i + first, 0))

    grad_specs = [group_spec(0), pl.BlockSpec((1, block), lambda i: (0, i))]

    def grad_shapes(k):
        width = bounds[k][1] - bounds[k][0]
        return [
            jax.ShapeDtypeStruct((width // group_size, filt_len), F32),
            jax.ShapeDtypeStruct((1, width), F32),
        ]

    def upper_grad(k, after):
        first, last = bounds[k]
        own, halo, at = sources[k]
        here, there = spec(rows, block, first // block), spec(rows, block, at)
        return call(
            functools.partial(upper_grad_kernel, group_size),
            ((last - first) // block,),
            [SMEM, here, here, there, there, spec(rows, block)],
            grad_specs,
            grad_shapes(k),
            name="upper_grads",
            cycles=6 * 10**9 if k == 0 else 2000,
            after=tuple(after),
        )(role, mid_gate, layer_inputs, own, halo, outgoing[k], *after)

    def turned_filter(k, after):
        first, last = bounds[k]
        here = spec(rows, block, first // block)
        return call(
            functools.partial(turned_filter_kernel, group_size),
            ((last - first) // block,),
            [SMEM, here, here, group_spec(first // block)],
            spec(rows, block),
            jax.ShapeDtypeStruct((rows, last - first), F32),
            name="turned_filter",
            cycles=1000,
            after=tuple(after),
        )(role, mid_gate, mid_halo, taps, *after)

    incoming = [(cotangent, 0)] * len(bounds)
    early, uppers, filtered = [], [], []
    for hop in range(sections - 1):
        split = [channels * eighths // 8 for eighths in HALO_EDGES] if hop == 0 else edges
        starts, ends = split[:-1], split[1:]
        owns, halos = [], []

        def send_halo(after):
            first, last = starts[len(owns)], ends[len(owns)]
            array, offset = next(entry for entry, edge in zip(incoming, edges) if edge == first)
            if hop == 0 and not early:
                owns.append(direct_weigh(first, last, after))
            else:
                owns.append(weigh(array, first, last, offset, after))
            halos.append(lax.ppermute(owns[-1], ("section", "seq"), behind))

        send_halo(())
        if hop == 0:
            mid_sent, inputs_sent, _ = lax.optimization_barrier((mid_gate, layer_inputs, owns[0]))
            mid_halo = lax.ppermute(mid_sent, ("section", "seq"), ahead)
            inputs_halo = lax.ppermute(inputs_sent, ("section", "seq"), ahead)
        send_halo((owns[0],))
        sources, outgoing, received = [], [], []
        for k, (first, last) in enumerate(bounds):
            part = max(i for i, start in enumerate(starts) if start <= first)
            while part >= len(owns):
                send_halo(tuple(early))
            at = (first - starts[part]) // block
            array, offset = incoming[k]
            before = tuple(outgoing[-1:])
            if hop == sections - 2 and k == 2:
                uppers.append(upper_grad(1, owns[-1:]))
                filtered.append(turned_filter(0, owns[-1:] + received[:1]))
                filtered.append(turned_filter(1, filtered[-1:]))
                before += (uppers[-1][0], filtered[-1])
            out = call(
                functools.partial(filter_kernel, group_size),
                ((last - first) // block,),
                [SMEM, spec(rows, block, at), spec(rows, block, at), group_spec(first // block),
                 spec(rows, block, first // block), spec(rows, block, (first - offset) // block)],
                spec(rows, block),
                bf16(last - first),
                name="filter",
                cycles=1000,
                after=before,
            )(role, owns[part], halos[part], taps, mid_gate, array, *before)
            sources.append((owns[part], halos[part], at))
            outgoing.append(out)
            received.append(lax.ppermute(out, "section", down))
            if hop == sections - 2 and k == 1:
                uppers = [upper_grad(0, (out,))]
                seconds = moments((out,))
                early = [uppers[0][0], seconds[0]]
        top = my_section == sections - 1
        incoming = [
            (jnp.where(top, cotangent[:, first:last], arrived), first)
            for (first, last), arrived in zip(bounds, received)
        ]

    latest = outgoing[-1:]
    for k in range(len(filtered), len(bounds)):
        filtered.append(turned_filter(k, latest))
        latest = filtered[-1:]
    for k in range(len(uppers), len(bounds)):
        uppers.append(upper_grad(k, latest))
        latest = uppers[-1][:1]
    firsts = []
    for k, (first, last) in enumerate(bounds):
        here = spec(rows, block, first // block)
        firsts.append(call(
            functools.partial(first_grad_kernel, group_size),
            ((last - first) // block,),
            [SMEM, here, here, here, here, here, spec(rows, block), spec(rows, block)],
            grad_specs,
            grad_shapes(k),
            name="first_grads",
            cycles=2000,
            after=tuple(latest),
        )(role, in_gate, mid_gate, layer_inputs, mid_halo, inputs_halo, received[k], filtered[k], *latest))
        latest = firsts[-1][:1]
    partial_sums = [grads[i] for both in (firsts, uppers) for i in range(2) for grads in both]

    own_channels = channels // seqs
    lines = groups // seqs + pl.cdiv(own_channels, LANES)
    packed = pl.pallas_call(
        functools.partial(pack_kernel, seqs),
        in_specs=[SMEM] + [vmem] * len(partial_sums),
        out_specs=vmem,
        out_shape=jax.ShapeDtypeStruct((seqs, lines, LANES), BF16),
        compiler_params=SMALL,
        name="pack",
    )(role, *partial_sums)
    parts = lax.all_to_all(packed, "seq", 0, 0)
    steer_step, filter_step = pl.pallas_call(
        step_kernel,
        in_specs=[SMEM] + [vmem] * 3,
        out_shape=[
            jax.ShapeDtypeStruct((1, own_channels), F32),
            jax.ShapeDtypeStruct((groups // seqs, filt_len), F32),
        ],
        compiler_params=SMALL,
        name="step",
    )(role, parts, *seconds)
    return steer_step, filter_step.T[None]


def solution(mesh):
    in_specs = (
        P("seq", None),
        P("section", "seq", None),
        P("section", "seq", None),
        P("section", "seq", None),
        P("section", None, None),
        P("section", "seq"),
        P("section", None, "seq"),
    )
    out_specs = (P("section", "seq"), P("section", None, "seq"))
    return jax.shard_map(body, mesh=mesh, in_specs=in_specs, out_specs=out_specs, check_vma=False)
```

```python
import functools

import jax
import jax.numpy as jnp
from jax import lax
from jax.experimental import pallas as pl
from jax.experimental.pallas import tpu as pltpu
from jax.sharding import PartitionSpec as P

F32 = jnp.float32
BF16 = jnp.bfloat16
LANES = 128
SUB = 32
CHUNK_EDGES = (0, 2, 3, 6, 7, 8)
HALO_EDGES = (0, 3, 6, 8)


def lane_of(shape):
    return lax.broadcasted_iota(jnp.int32, shape, 1)


def row_of(shape):
    return lax.broadcasted_iota(jnp.int32, shape, 0)


def first_section(role):
    return (role[0] & 1) > 0


def times(a, b):
    return (a.astype(F32) * b.astype(F32)).astype(BF16)


def turned(x):
    return pltpu.roll(x, LANES // 2, 1)


def spread(x, x_turned, parity, count):
    low = lane_of((count, LANES)) < LANES // 2
    natural, other = (x, x_turned) if parity == 0 else (x_turned, x)
    tiles = []
    for first in (0, 2 * SUB):
        tiles.append(jnp.where(low, natural[first : first + count], other[first + SUB : first + SUB + count]))
    return jnp.concatenate(tiles, 1)


def gathered(even, odd):
    low = lane_of((SUB, LANES)) < LANES // 2
    out = []
    for tile in range(2):
        a = even[:, tile * LANES : (tile + 1) * LANES]
        b = odd[:, tile * LANES : (tile + 1) * LANES]
        out.append(jnp.where(low, a, turned(b)))
        out.append(jnp.where(low, turned(a), b))
    return jnp.concatenate(out, 0)


def in_order(reverse, own, halo):
    return jnp.concatenate([jnp.where(reverse, halo, own), jnp.where(reverse, own, halo)], 0)


def diagonal_sums(blocks):
    tiles = []
    for block in blocks:
        tile = block[:8]
        for first in range(8, SUB, 8):
            tile = tile + pltpu.roll(block[first : first + 8], LANES - first, 1)
        tiles.append(tile)
    row = row_of((8, LANES))
    for fold in (4, 2, 1):
        upper = row % (2 * fold) < fold
        tiles = [
            jnp.where(upper, a, pltpu.roll(b, fold, 0))
            + pltpu.roll(jnp.where(upper, pltpu.roll(a, 8 - fold, 0), b), LANES - fold, 1)
            for a, b in zip(tiles[:fold], tiles[fold:])
        ]
    return tiles[0]


def near(reverse_int, shape):
    return lane_of(shape) - row_of(shape) >= reverse_int


def tap_matrix(reverse, taps_by_group):
    taps = taps_by_group.shape[0]
    source = row_of((taps, taps))
    target = lane_of((taps, taps))
    mirrored = jnp.where(source == 0, 0, taps - source)
    pick = jnp.where(target == jnp.where(reverse, mirrored, source), 1.0, 0.0)
    return pick, taps


def weigh_kernel(role, gate, incoming, out):
    @pl.when(jnp.logical_not(first_section(role)))
    def _():
        out[...] = times(gate[...], incoming[...])


def direct_weigh_kernel(first, block, role, gate, incoming, out, gate_part, incoming_part, sems):
    @pl.when(jnp.logical_not(first_section(role)))
    def _():
        tiles = [pl.ds(at, block) for at in range(0, out.shape[1], block)]
        copies = [
            [
                pltpu.make_async_copy(source.at[:, pl.ds(first + i * block, block)], part.at[:, t], sems.at[which, i])
                for which, (source, part) in enumerate(((gate, gate_part), (incoming, incoming_part)))
            ]
            for i, t in enumerate(tiles)
        ]
        for pair in copies:
            for copy in pair:
                copy.start()
        for t, pair in zip(tiles, copies):
            for copy in pair:
                copy.wait()
            out[:, t] = times(gate_part[:, t], incoming_part[:, t])


def moments_kernel(role, steer_second, filter_second, *refs):
    steer_out, filter_out = refs[-2:]
    steer_out[...] = steer_second[...]
    filter_out[...] = filter_second[...]


def taps_kernel(role, filters, taps_out):
    pick, _ = tap_matrix(first_section(role), filters[...])
    taps_out[...] = lax.dot_general(
        filters[...], pick.astype(BF16), (((0,), (0,)), ((), ())), preferred_element_type=F32
    )


def convolved(reverse, group_size, own, halo, taps, first_group):
    half = LANES // 2
    per_half = half // group_size
    mask = near(int(reverse), (SUB, LANES))
    zero = jnp.zeros((SUB, LANES), F32)
    lane_group = (lane_of((SUB, 2 * LANES)) % half) // group_size
    ext = jnp.concatenate([halo, own] if reverse else [own, halo], 0)
    ext_turned = turned(ext)
    results = []
    for parity in range(2):
        window = spread(ext, ext_turned, parity, own.shape[0] + SUB)
        bands = []
        for g in range(per_half):
            row = taps[pl.ds(first_group + parity * per_half + g, 1), :]
            circ = pltpu.roll(jnp.broadcast_to(row, (SUB, LANES)), 0, 1, stride=1, stride_axis=0)
            band = jnp.concatenate([jnp.where(mask, circ, zero), jnp.where(mask, zero, circ)[:, :SUB]], 1)
            bands.append(band.astype(BF16))
        product = jnp.dot(jnp.concatenate(bands, 0), window, preferred_element_type=F32)
        total = product[:SUB]
        for g in range(1, per_half):
            total = jnp.where(lane_group == g, product[g * SUB : (g + 1) * SUB], total)
        results.append(total)
    return gathered(*results)


def filter_kernel(group_size, role, own, halo, taps, mid, incoming, outgoing):
    @pl.when(jnp.logical_not(first_section(role)))
    def _():
        for first in range(0, own.shape[1], LANES):
            cols = pl.ds(first, LANES)
            conv = convolved(False, group_size, own[:, cols], halo[:, cols], taps, first // group_size)
            outgoing[:, cols] = (
                incoming[:, cols].astype(F32) + mid[:, cols].astype(F32) * conv
            ).astype(BF16)


def turned_filter_kernel(group_size, role, mid, mid_halo, taps, filtered):
    @pl.when(first_section(role))
    def _():
        for first in range(0, mid.shape[1], LANES):
            cols = pl.ds(first, LANES)
            filtered[:, cols] = convolved(True, group_size, mid[:, cols], mid_halo[:, cols], taps, first // group_size)


def tap_sums(reverse, group_size, left, own, halo):
    half = LANES // 2
    per_half = half // group_size
    mask = near(int(reverse), (SUB, LANES))
    lane_group = (lane_of((SUB, 2 * LANES)) % half) // group_size
    nothing = jnp.zeros((SUB, 2 * LANES), BF16)
    ext = jnp.concatenate([halo, own] if reverse else [own, halo], 0)
    ext_turned, left_turned = turned(ext), turned(left)
    blocks = []
    for parity in range(2):
        window = spread(ext, ext_turned, parity, own.shape[0] + SUB)
        short = spread(left, left_turned, parity, SUB)
        lhs = jnp.concatenate([jnp.where(lane_group == g, short, nothing) for g in range(per_half)], 0)
        product = lax.dot_general(lhs, window, (((1,), (1,)), ((), ())), preferred_element_type=F32)
        for g in range(per_half):
            block = product[g * SUB : (g + 1) * SUB]
            late = jnp.concatenate([block[:, LANES:], jnp.zeros((SUB, LANES - SUB), F32)], 1)
            blocks.append(jnp.where(mask, block[:, :LANES], late))
    return diagonal_sums(blocks)


def upper_grad_kernel(group_size, role, mid, inputs, own, halo, outgoing, tap_grad, steer_grad):
    @pl.when(role[0] == 0)
    def _():
        steer_grad[...] = jnp.sum(outgoing[...].astype(F32), 0, keepdims=True)
        for pair in range(own.shape[1] // LANES):
            cols = pl.ds(pair * LANES, LANES)
            values = times(mid[:, cols], inputs[:, cols])
            tap_grad[pl.ds(8 * pair, 8), :] = tap_sums(False, group_size, values, own[:, cols], halo[:, cols])


def first_grad_kernel(
    group_size, role, gate, mid, inputs, mid_halo, inputs_halo, received, filtered, tap_grad, steer_grad
):
    @pl.when(role[0] > 0)
    def _():
        for pair in range(gate.shape[1] // LANES):
            cols = pl.ds(pair * LANES, LANES)
            grad = received[:, cols]
            weighted = times(gate[:, cols], grad)
            grad_in = grad.astype(F32) + weighted.astype(F32) * filtered[:, cols]
            steer_grad[:, cols] = jnp.sum(grad_in, 0, keepdims=True)
            own, halo = times(mid[:, cols], inputs[:, cols]), times(mid_halo[:, cols], inputs_halo[:, cols])
            tap_grad[pl.ds(8 * pair, 8), :] = tap_sums(True, group_size, weighted, own, halo)


def pack_kernel(owners, role, *refs):
    refs, out = refs[:-1], refs[-1]
    count = len(refs) // 4

    def part(parts, axis, at, size):
        for ref in parts:
            if at < ref.shape[axis]:
                return ref[at : at + size, :] if axis == 0 else ref[:, at : at + size]
            at -= ref.shape[axis]

    def pack(taps, steers):
        groups = sum(ref.shape[0] for ref in taps) // owners
        channels = sum(ref.shape[1] for ref in steers) // owners
        for owner in range(owners):
            lines = [part(taps, 0, owner * groups, groups)]
            for at in range(0, channels, LANES):
                size = min(LANES, channels - at)
                steer = part(steers, 1, owner * channels + at, size)
                if size < LANES:
                    steer = jnp.concatenate([steer, jnp.zeros((1, LANES - size), F32)], 1)
                lines.append(steer)
            out[owner] = jnp.concatenate(lines, 0).astype(BF16)

    @pl.when(first_section(role))
    def _():
        pack(refs[:count], refs[count : 2 * count])

    @pl.when(jnp.logical_not(first_section(role)))
    def _():
        pack(refs[2 * count : 3 * count], refs[3 * count :])


def step_kernel(role, parts, steer_second, filter_second, steer_out, filter_out):
    total = jnp.sum(parts[...].astype(F32), 0)
    groups = filter_second.shape[0]
    tap_grad = total[:groups]
    lane = lane_of(tap_grad.shape)
    mirrored = jnp.where(lane == 0, 0, tap_grad.shape[1] - lane)
    tap_grad = jnp.take_along_axis(tap_grad, jnp.where(first_section(role), mirrored, lane), axis=1)
    filter_out[...] = tap_grad / jnp.sqrt(filter_second[...] + tap_grad * tap_grad)
    channels = steer_out.shape[1]
    for row in range(pl.cdiv(channels, LANES)):
        cols = min(LANES, channels - row * LANES)
        at = pl.ds(row * LANES, cols)
        grad = total[groups + row : groups + row + 1, :cols]
        steer_out[:, at] = grad / jnp.sqrt(steer_second[:, at] + grad * grad)


def spec(rows, width, first=0):
    return pl.BlockSpec((rows, width), lambda i: (0, i + first))


SMEM = pl.BlockSpec(memory_space=pltpu.SMEM)
ANY = pl.BlockSpec(memory_space=pl.ANY)
SMALL = pltpu.CompilerParams(vmem_limit_bytes=4 * 1024 * 1024)


def call(kernel, grid, in_specs, out_specs, out_shape, scratch=(), name=None, cycles=100, after=()):
    count = len(in_specs)

    def with_after(*refs):
        kernel(*refs[:count], *refs[count + len(after) :])

    return pl.pallas_call(
        with_after,
        grid=grid,
        in_specs=list(in_specs) + [ANY] * len(after),
        out_specs=out_specs,
        out_shape=out_shape,
        scratch_shapes=list(scratch),
        compiler_params=pltpu.CompilerParams(vmem_limit_bytes=16 * 1024 * 1024),
        cost_estimate=pl.CostEstimate(flops=cycles, bytes_accessed=0, transcendentals=0),
        name=name,
    )


def body(cotangent, in_gate, mid_gate, layer_inputs, filters, steer_second, filter_second):
    in_gate, mid_gate, layer_inputs = in_gate[0], mid_gate[0], layer_inputs[0]
    rows, channels = in_gate.shape
    filt_len, groups = filters.shape[1:]
    group_size = channels // groups
    sections, seqs = lax.axis_size("section"), lax.axis_size("seq")
    my_section = lax.axis_index("section")
    role = (my_section == 0).astype(jnp.int32).reshape(1)

    edges = [channels * eighths // 8 for eighths in CHUNK_EDGES]
    bounds = list(zip(edges[:-1], edges[1:]))
    block = channels // 8
    block_groups = block // group_size
    behind = [(seqs * s + i, seqs * s + i - 1) for s in range(1, sections) for i in range(1, seqs)]
    ahead = [(i, i + 1) for i in range(seqs - 1)]
    down = [(s, s - 1) for s in range(1, sections)]

    def bf16(width_of):
        return jax.ShapeDtypeStruct((rows, width_of), BF16)

    def weigh(incoming, first, last, offset, after):
        return call(
            weigh_kernel,
            ((last - first) // block,),
            [SMEM, spec(rows, block, first // block), spec(rows, block, (first - offset) // block)],
            spec(rows, block),
            bf16(last - first),
            name="weigh",
            after=after,
        )(role, in_gate, incoming, *after)

    def direct_weigh(first, last, after):
        width = last - first
        part = pltpu.VMEM((rows, width), BF16)

        def kernel(*refs):
            direct_weigh_kernel(first, block, *refs[:3], *refs[3 + len(after) :])

        return pl.pallas_call(
            kernel,
            in_specs=[SMEM] + [ANY] * (2 + len(after)),
            out_specs=pl.BlockSpec(memory_space=pltpu.VMEM),
            out_shape=bf16(width),
            scratch_shapes=[part, part, pltpu.SemaphoreType.DMA((2, width // block))],
            compiler_params=SMALL,
            name="direct_weigh",
        )(role, *[pltpu.with_memory_space_constraint(a, pltpu.HBM) for a in (in_gate, cotangent)], *after)

    vmem = pl.BlockSpec(memory_space=pltpu.VMEM)
    taps = pl.pallas_call(
        taps_kernel,
        in_specs=[SMEM, vmem],
        out_specs=vmem,
        out_shape=jax.ShapeDtypeStruct((groups, filt_len), F32),
        compiler_params=SMALL,
        name="taps",
    )(role, filters[0])

    def moments(after):
        seconds = (steer_second, filter_second[0].T)
        return pl.pallas_call(
            moments_kernel,
            in_specs=[SMEM] + [vmem] * 2 + [ANY] * len(after),
            out_specs=[vmem] * 2,
            out_shape=[jax.ShapeDtypeStruct(second.shape, F32) for second in seconds],
            compiler_params=SMALL,
            name="moments",
        )(role, *seconds, *after)

    group_spec = lambda first: pl.BlockSpec((block_groups, filt_len), lambda i: (i + first, 0))

    grad_specs = [group_spec(0), pl.BlockSpec((1, block), lambda i: (0, i))]

    def grad_shapes(k):
        width = bounds[k][1] - bounds[k][0]
        return [
            jax.ShapeDtypeStruct((width // group_size, filt_len), F32),
            jax.ShapeDtypeStruct((1, width), F32),
        ]

    def upper_grad(k, after):
        first, last = bounds[k]
        own, halo, at = sources[k]
        here, there = spec(rows, block, first // block), spec(rows, block, at)
        return call(
            functools.partial(upper_grad_kernel, group_size),
            ((last - first) // block,),
            [SMEM, here, here, there, there, spec(rows, block)],
            grad_specs,
            grad_shapes(k),
            name="upper_grads",
            cycles=6 * 10**9 if k == 0 else 2000,
            after=tuple(after),
        )(role, mid_gate, layer_inputs, own, halo, outgoing[k], *after)

    def turned_filter(k, after):
        first, last = bounds[k]
        here = spec(rows, block, first // block)
        return call(
            functools.partial(turned_filter_kernel, group_size),
            ((last - first) // block,),
            [SMEM, here, here, group_spec(first // block)],
            spec(rows, block),
            jax.ShapeDtypeStruct((rows, last - first), F32),
            name="turned_filter",
            cycles=1000,
            after=tuple(after),
        )(role, mid_gate, mid_halo, taps, *after)

    incoming = [(cotangent, 0)] * len(bounds)
    early, uppers, filtered = [], [], []
    ready = CHUNK_EDGES.index(HALO_EDGES[-2])
    for hop in range(sections - 1):
        split = [channels * eighths // 8 for eighths in HALO_EDGES] if hop == 0 else edges
        starts, ends = split[:-1], split[1:]
        owns, halos = [], []

        def send_halo(after):
            first, last = starts[len(owns)], ends[len(owns)]
            array, offset = next(entry for entry, edge in zip(incoming, edges) if edge == first)
            if hop == 0 and not early:
                owns.append(direct_weigh(first, last, after))
            else:
                owns.append(weigh(array, first, last, offset, after))
            halos.append(lax.ppermute(owns[-1], ("section", "seq"), behind))

        send_halo(())
        if hop == 0:
            mid_sent, inputs_sent, _ = lax.optimization_barrier((mid_gate, layer_inputs, owns[0]))
            mid_halo = lax.ppermute(mid_sent, ("section", "seq"), ahead)
            inputs_halo = lax.ppermute(inputs_sent, ("section", "seq"), ahead)
        send_halo((owns[0],))
        sources, outgoing, received = [], [], []
        for k, (first, last) in enumerate(bounds):
            part = max(i for i, start in enumerate(starts) if start <= first)
            while part >= len(owns):
                send_halo(tuple(early))
            at = (first - starts[part]) // block
            array, offset = incoming[k]
            before = tuple(outgoing[-1:])
            if hop == sections - 2 and k == ready:
                uppers.append(upper_grad(k - 1, owns[-1:]))
                filtered.append(turned_filter(0, owns[-1:] + received[:1]))
                for early_chunk in range(1, k):
                    filtered.append(turned_filter(early_chunk, filtered[-1:]))
                before += (uppers[-1][0], filtered[-1])
            out = call(
                functools.partial(filter_kernel, group_size),
                ((last - first) // block,),
                [SMEM, spec(rows, block, at), spec(rows, block, at), group_spec(first // block),
                 spec(rows, block, first // block), spec(rows, block, (first - offset) // block)],
                spec(rows, block),
                bf16(last - first),
                name="filter",
                cycles=1000,
                after=before,
            )(role, owns[part], halos[part], taps, mid_gate, array, *before)
            sources.append((owns[part], halos[part], at))
            outgoing.append(out)
            received.append(lax.ppermute(out, "section", down))
            if hop == sections - 2 and k == ready - 1:
                latest = (out,)
                for early_chunk in range(k):
                    uppers.append(upper_grad(early_chunk, latest))
                    latest = uppers[-1][:1]
                seconds = moments((out,))
                early = [uppers[-1][0], seconds[0]]
        top = my_section == sections - 1
        incoming = [
            (jnp.where(top, cotangent[:, first:last], arrived), first)
            for (first, last), arrived in zip(bounds, received)
        ]

    latest = outgoing[-1:]
    for k in range(len(filtered), len(bounds)):
        filtered.append(turned_filter(k, latest))
        latest = filtered[-1:]
    for k in range(len(uppers), len(bounds)):
        uppers.append(upper_grad(k, latest))
        latest = uppers[-1][:1]
    firsts = []
    for k, (first, last) in enumerate(bounds):
        here = spec(rows, block, first // block)
        firsts.append(call(
            functools.partial(first_grad_kernel, group_size),
            ((last - first) // block,),
            [SMEM, here, here, here, here, here, spec(rows, block), spec(rows, block)],
            grad_specs,
            grad_shapes(k),
            name="first_grads",
            cycles=2000,
            after=tuple(latest),
        )(role, in_gate, mid_gate, layer_inputs, mid_halo, inputs_halo, received[k], filtered[k], *latest))
        latest = firsts[-1][:1]
    partial_sums = [grads[i] for both in (firsts, uppers) for i in range(2) for grads in both]

    own_channels = channels // seqs
    lines = groups // seqs + pl.cdiv(own_channels, LANES)
    packed = pl.pallas_call(
        functools.partial(pack_kernel, seqs),
        in_specs=[SMEM] + [vmem] * len(partial_sums),
        out_specs=vmem,
        out_shape=jax.ShapeDtypeStruct((seqs, lines, LANES), BF16),
        compiler_params=SMALL,
        name="pack",
    )(role, *partial_sums)
    parts = lax.all_to_all(packed, "seq", 0, 0)
    steer_step, filter_step = pl.pallas_call(
        step_kernel,
        in_specs=[SMEM] + [vmem] * 3,
        out_shape=[
            jax.ShapeDtypeStruct((1, own_channels), F32),
            jax.ShapeDtypeStruct((groups // seqs, filt_len), F32),
        ],
        compiler_params=SMALL,
        name="step",
    )(role, parts, *seconds)
    return steer_step, filter_step.T[None]


def solution(mesh):
    in_specs = (
        P("seq", None),
        P("section", "seq", None),
        P("section", "seq", None),
        P("section", "seq", None),
        P("section", None, None),
        P("section", "seq"),
        P("section", None, "seq"),
    )
    out_specs = (P("section", "seq"), P("section", None, "seq"))
    return jax.shard_map(body, mesh=mesh, in_specs=in_specs, out_specs=out_specs, check_vma=False)
```

```python
import functools

import jax
import jax.numpy as jnp
from jax import lax
from jax.experimental import pallas as pl
from jax.experimental.pallas import tpu as pltpu
from jax.sharding import PartitionSpec as P

F32 = jnp.float32
BF16 = jnp.bfloat16
LANES = 128
SUB = 32
CHUNK_EDGES = (0, 3, 6, 7, 8)
HALO_EDGES = (0, 3, 6, 8)


def lane_of(shape):
    return lax.broadcasted_iota(jnp.int32, shape, 1)


def row_of(shape):
    return lax.broadcasted_iota(jnp.int32, shape, 0)


def first_section(role):
    return (role[0] & 1) > 0


def times(a, b):
    return (a.astype(F32) * b.astype(F32)).astype(BF16)


def turned(x):
    return pltpu.roll(x, LANES // 2, 1)


def spread(x, x_turned, parity, count):
    low = lane_of((count, LANES)) < LANES // 2
    natural, other = (x, x_turned) if parity == 0 else (x_turned, x)
    tiles = []
    for first in (0, 2 * SUB):
        tiles.append(jnp.where(low, natural[first : first + count], other[first + SUB : first + SUB + count]))
    return jnp.concatenate(tiles, 1)


def gathered(even, odd):
    low = lane_of((SUB, LANES)) < LANES // 2
    out = []
    for tile in range(2):
        a = even[:, tile * LANES : (tile + 1) * LANES]
        b = odd[:, tile * LANES : (tile + 1) * LANES]
        out.append(jnp.where(low, a, turned(b)))
        out.append(jnp.where(low, turned(a), b))
    return jnp.concatenate(out, 0)


def in_order(reverse, own, halo):
    return jnp.concatenate([jnp.where(reverse, halo, own), jnp.where(reverse, own, halo)], 0)


def diagonal_sums(blocks):
    tiles = []
    for block in blocks:
        tile = block[:8]
        for first in range(8, SUB, 8):
            tile = tile + pltpu.roll(block[first : first + 8], LANES - first, 1)
        tiles.append(tile)
    row = row_of((8, LANES))
    for fold in (4, 2, 1):
        upper = row % (2 * fold) < fold
        tiles = [
            jnp.where(upper, a, pltpu.roll(b, fold, 0))
            + pltpu.roll(jnp.where(upper, pltpu.roll(a, 8 - fold, 0), b), LANES - fold, 1)
            for a, b in zip(tiles[:fold], tiles[fold:])
        ]
    return tiles[0]


def near(reverse_int, shape):
    return lane_of(shape) - row_of(shape) >= reverse_int


def tap_matrix(reverse, taps_by_group):
    taps = taps_by_group.shape[0]
    source = row_of((taps, taps))
    target = lane_of((taps, taps))
    mirrored = jnp.where(source == 0, 0, taps - source)
    pick = jnp.where(target == jnp.where(reverse, mirrored, source), 1.0, 0.0)
    return pick, taps


def weigh_kernel(role, gate, incoming, out):
    @pl.when(jnp.logical_not(first_section(role)))
    def _():
        out[...] = times(gate[...], incoming[...])


def direct_weigh_kernel(first, role, gate, incoming, out, gate_part, incoming_part, sems):
    @pl.when(role[0] == 0)
    def _():
        cols = pl.ds(first, out.shape[1])
        pieces = [pl.ds(at, SUB) for at in range(0, out.shape[0], SUB)]
        copies = [
            [
                pltpu.make_async_copy(source.at[piece, cols], part.at[piece, :], sems.at[which, i])
                for which, (source, part) in enumerate(((gate, gate_part), (incoming, incoming_part)))
            ]
            for i, piece in enumerate(pieces)
        ]
        for pair in copies:
            for copy in pair:
                copy.start()
        for piece, pair in zip(pieces, copies):
            for copy in pair:
                copy.wait()
            out[piece, :] = times(gate_part[piece, :], incoming_part[piece, :])


def moments_kernel(role, steer_second, filter_second, *refs):
    steer_out, filter_out = refs[-2:]
    steer_out[...] = steer_second[...]
    filter_out[...] = filter_second[...]


def taps_kernel(role, filters, taps_out):
    pick, _ = tap_matrix(first_section(role), filters[...])
    taps_out[...] = lax.dot_general(
        filters[...], pick.astype(BF16), (((0,), (0,)), ((), ())), preferred_element_type=F32
    )


def convolved(reverse, group_size, own, halo, taps, first_group):
    half = LANES // 2
    per_half = half // group_size
    mask = near(int(reverse), (SUB, LANES))
    zero = jnp.zeros((SUB, LANES), F32)
    lane_group = (lane_of((SUB, 2 * LANES)) % half) // group_size
    ext = jnp.concatenate([halo, own] if reverse else [own, halo], 0)
    ext_turned = turned(ext)
    results = []
    for parity in range(2):
        window = spread(ext, ext_turned, parity, own.shape[0] + SUB)
        bands = []
        for g in range(per_half):
            row = taps[pl.ds(first_group + parity * per_half + g, 1), :]
            circ = pltpu.roll(jnp.broadcast_to(row, (SUB, LANES)), 0, 1, stride=1, stride_axis=0)
            band = jnp.concatenate([jnp.where(mask, circ, zero), jnp.where(mask, zero, circ)[:, :SUB]], 1)
            bands.append(band.astype(BF16))
        product = jnp.dot(jnp.concatenate(bands, 0), window, preferred_element_type=F32)
        total = product[:SUB]
        for g in range(1, per_half):
            total = jnp.where(lane_group == g, product[g * SUB : (g + 1) * SUB], total)
        results.append(total)
    return gathered(*results)


def filter_kernel(group_size, role, own, halo, taps, mid, incoming, outgoing):
    @pl.when(jnp.logical_not(first_section(role)))
    def _():
        for first in range(0, own.shape[1], LANES):
            cols = pl.ds(first, LANES)
            conv = convolved(False, group_size, own[:, cols], halo[:, cols], taps, first // group_size)
            outgoing[:, cols] = (
                incoming[:, cols].astype(F32) + mid[:, cols].astype(F32) * conv
            ).astype(BF16)


def turned_filter_kernel(group_size, role, mid, mid_halo, taps, filtered):
    @pl.when(first_section(role))
    def _():
        for first in range(0, mid.shape[1], LANES):
            cols = pl.ds(first, LANES)
            filtered[:, cols] = convolved(True, group_size, mid[:, cols], mid_halo[:, cols], taps, first // group_size)


def tap_sums(reverse, group_size, left, own, halo):
    half = LANES // 2
    per_half = half // group_size
    mask = near(int(reverse), (SUB, LANES))
    lane_group = (lane_of((SUB, 2 * LANES)) % half) // group_size
    nothing = jnp.zeros((SUB, 2 * LANES), BF16)
    ext = jnp.concatenate([halo, own] if reverse else [own, halo], 0)
    ext_turned, left_turned = turned(ext), turned(left)
    blocks = []
    for parity in range(2):
        window = spread(ext, ext_turned, parity, own.shape[0] + SUB)
        short = spread(left, left_turned, parity, SUB)
        lhs = jnp.concatenate([jnp.where(lane_group == g, short, nothing) for g in range(per_half)], 0)
        product = lax.dot_general(lhs, window, (((1,), (1,)), ((), ())), preferred_element_type=F32)
        for g in range(per_half):
            block = product[g * SUB : (g + 1) * SUB]
            late = jnp.concatenate([block[:, LANES:], jnp.zeros((SUB, LANES - SUB), F32)], 1)
            blocks.append(jnp.where(mask, block[:, :LANES], late))
    return diagonal_sums(blocks)


def upper_grad_kernel(group_size, role, mid, inputs, own, halo, outgoing, tap_grad, steer_grad):
    @pl.when(role[0] == 0)
    def _():
        steer_grad[...] = jnp.sum(outgoing[...].astype(F32), 0, keepdims=True)
        for pair in range(own.shape[1] // LANES):
            cols = pl.ds(pair * LANES, LANES)
            values = times(mid[:, cols], inputs[:, cols])
            tap_grad[pl.ds(8 * pair, 8), :] = tap_sums(False, group_size, values, own[:, cols], halo[:, cols])


def first_grad_kernel(
    group_size, role, gate, mid, inputs, mid_halo, inputs_halo, received, filtered, tap_grad, steer_grad
):
    @pl.when(role[0] > 0)
    def _():
        for pair in range(gate.shape[1] // LANES):
            cols = pl.ds(pair * LANES, LANES)
            grad = received[:, cols]
            weighted = times(gate[:, cols], grad)
            grad_in = grad.astype(F32) + weighted.astype(F32) * filtered[:, cols]
            steer_grad[:, cols] = jnp.sum(grad_in, 0, keepdims=True)
            own, halo = times(mid[:, cols], inputs[:, cols]), times(mid_halo[:, cols], inputs_halo[:, cols])
            tap_grad[pl.ds(8 * pair, 8), :] = tap_sums(True, group_size, weighted, own, halo)


def pack_kernel(owners, role, *refs):
    refs, out = refs[:-1], refs[-1]
    count = len(refs) // 4

    def part(parts, axis, at, size):
        for ref in parts:
            if at < ref.shape[axis]:
                return ref[at : at + size, :] if axis == 0 else ref[:, at : at + size]
            at -= ref.shape[axis]

    def pack(taps, steers):
        groups = sum(ref.shape[0] for ref in taps) // owners
        channels = sum(ref.shape[1] for ref in steers) // owners
        for owner in range(owners):
            lines = [part(taps, 0, owner * groups, groups)]
            for at in range(0, channels, LANES):
                size = min(LANES, channels - at)
                steer = part(steers, 1, owner * channels + at, size)
                if size < LANES:
                    steer = jnp.concatenate([steer, jnp.zeros((1, LANES - size), F32)], 1)
                lines.append(steer)
            out[owner] = jnp.concatenate(lines, 0).astype(BF16)

    @pl.when(first_section(role))
    def _():
        pack(refs[:count], refs[count : 2 * count])

    @pl.when(jnp.logical_not(first_section(role)))
    def _():
        pack(refs[2 * count : 3 * count], refs[3 * count :])


def step_kernel(role, parts, steer_second, filter_second, steer_out, filter_out):
    total = jnp.sum(parts[...].astype(F32), 0)
    groups = filter_second.shape[0]
    tap_grad = total[:groups]
    lane = lane_of(tap_grad.shape)
    mirrored = jnp.where(lane == 0, 0, tap_grad.shape[1] - lane)
    tap_grad = jnp.take_along_axis(tap_grad, jnp.where(first_section(role), mirrored, lane), axis=1)
    filter_out[...] = tap_grad / jnp.sqrt(filter_second[...] + tap_grad * tap_grad)
    channels = steer_out.shape[1]
    for row in range(pl.cdiv(channels, LANES)):
        cols = min(LANES, channels - row * LANES)
        at = pl.ds(row * LANES, cols)
        grad = total[groups + row : groups + row + 1, :cols]
        steer_out[:, at] = grad / jnp.sqrt(steer_second[:, at] + grad * grad)


def spec(rows, width, first=0):
    return pl.BlockSpec((rows, width), lambda i: (0, i + first))


SMEM = pl.BlockSpec(memory_space=pltpu.SMEM)
ANY = pl.BlockSpec(memory_space=pl.ANY)
SMALL = pltpu.CompilerParams(vmem_limit_bytes=4 * 1024 * 1024)


def call(kernel, grid, in_specs, out_specs, out_shape, scratch=(), name=None, cycles=100, after=()):
    count = len(in_specs)

    def with_after(*refs):
        kernel(*refs[:count], *refs[count + len(after) :])

    return pl.pallas_call(
        with_after,
        grid=grid,
        in_specs=list(in_specs) + [ANY] * len(after),
        out_specs=out_specs,
        out_shape=out_shape,
        scratch_shapes=list(scratch),
        compiler_params=pltpu.CompilerParams(vmem_limit_bytes=16 * 1024 * 1024),
        cost_estimate=pl.CostEstimate(flops=cycles, bytes_accessed=0, transcendentals=0),
        name=name,
    )


def body(cotangent, in_gate, mid_gate, layer_inputs, filters, steer_second, filter_second):
    in_gate, mid_gate, layer_inputs = in_gate[0], mid_gate[0], layer_inputs[0]
    rows, channels = in_gate.shape
    filt_len, groups = filters.shape[1:]
    group_size = channels // groups
    sections, seqs = lax.axis_size("section"), lax.axis_size("seq")
    my_section = lax.axis_index("section")
    role = (my_section == 0).astype(jnp.int32).reshape(1)

    edges = [channels * eighths // 8 for eighths in CHUNK_EDGES]
    bounds = list(zip(edges[:-1], edges[1:]))
    block = channels // 8
    block_groups = block // group_size
    behind = [(seqs * s + i, seqs * s + i - 1) for s in range(1, sections) for i in range(1, seqs)]
    ahead = [(i, i + 1) for i in range(seqs - 1)]
    down = [(s, s - 1) for s in range(1, sections)]

    def bf16(width_of):
        return jax.ShapeDtypeStruct((rows, width_of), BF16)

    def weigh(incoming, first, last, offset, after):
        return call(
            weigh_kernel,
            ((last - first) // block,),
            [SMEM, spec(rows, block, first // block), spec(rows, block, (first - offset) // block)],
            spec(rows, block),
            bf16(last - first),
            name="weigh",
            after=after,
        )(role, in_gate, incoming, *after)

    def direct_weigh(first, last, after):
        width = last - first
        part = pltpu.VMEM((rows, width), BF16)

        def kernel(*refs):
            direct_weigh_kernel(first, *refs[:3], *refs[3 + len(after) :])

        return pl.pallas_call(
            kernel,
            in_specs=[SMEM] + [ANY] * (2 + len(after)),
            out_specs=pl.BlockSpec(memory_space=pltpu.VMEM),
            out_shape=bf16(width),
            scratch_shapes=[part, part, pltpu.SemaphoreType.DMA((2, rows // SUB))],
            compiler_params=SMALL,
            name="direct_weigh",
        )(role, *[pltpu.with_memory_space_constraint(a, pltpu.HBM) for a in (in_gate, cotangent)], *after)

    vmem = pl.BlockSpec(memory_space=pltpu.VMEM)
    taps = pl.pallas_call(
        taps_kernel,
        in_specs=[SMEM, vmem],
        out_specs=vmem,
        out_shape=jax.ShapeDtypeStruct((groups, filt_len), F32),
        compiler_params=SMALL,
        name="taps",
    )(role, filters[0])

    def moments(after):
        seconds = (steer_second, filter_second[0].T)
        return pl.pallas_call(
            moments_kernel,
            in_specs=[SMEM] + [vmem] * 2 + [ANY] * len(after),
            out_specs=[vmem] * 2,
            out_shape=[jax.ShapeDtypeStruct(second.shape, F32) for second in seconds],
            compiler_params=SMALL,
            name="moments",
        )(role, *seconds, *after)

    group_spec = lambda first: pl.BlockSpec((block_groups, filt_len), lambda i: (i + first, 0))

    grad_specs = [group_spec(0), pl.BlockSpec((1, block), lambda i: (0, i))]

    def grad_shapes(k):
        width = bounds[k][1] - bounds[k][0]
        return [
            jax.ShapeDtypeStruct((width // group_size, filt_len), F32),
            jax.ShapeDtypeStruct((1, width), F32),
        ]

    def upper_grad(k, after):
        first, last = bounds[k]
        own, halo, at = sources[k]
        here, there = spec(rows, block, first // block), spec(rows, block, at)
        return call(
            functools.partial(upper_grad_kernel, group_size),
            ((last - first) // block,),
            [SMEM, here, here, there, there, spec(rows, block)],
            grad_specs,
            grad_shapes(k),
            name="upper_grads",
            cycles=6 * 10**9 if k == 0 else 2000,
            after=tuple(after),
        )(role, mid_gate, layer_inputs, own, halo, outgoing[k], *after)

    def turned_filter(k, after):
        first, last = bounds[k]
        here = spec(rows, block, first // block)
        return call(
            functools.partial(turned_filter_kernel, group_size),
            ((last - first) // block,),
            [SMEM, here, here, group_spec(first // block)],
            spec(rows, block),
            jax.ShapeDtypeStruct((rows, last - first), F32),
            name="turned_filter",
            cycles=1000,
            after=tuple(after),
        )(role, mid_gate, mid_halo, taps, *after)

    incoming = [(cotangent, 0)] * len(bounds)
    early, uppers, filtered = [], [], []
    for hop in range(sections - 1):
        split = [channels * eighths // 8 for eighths in HALO_EDGES] if hop == 0 else edges
        starts, ends = split[:-1], split[1:]
        owns, halos = [], []

        def send_halo(after):
            first, last = starts[len(owns)], ends[len(owns)]
            array, offset = next(entry for entry, edge in zip(incoming, edges) if edge == first)
            if hop == 0 and not early:
                owns.append(direct_weigh(first, last, after))
            else:
                owns.append(weigh(array, first, last, offset, after))
            halos.append(lax.ppermute(owns[-1], ("section", "seq"), behind))

        send_halo(())
        if hop == 0:
            mid_sent, inputs_sent, _ = lax.optimization_barrier((mid_gate, layer_inputs, owns[0]))
            mid_halo = lax.ppermute(mid_sent, ("section", "seq"), ahead)
            inputs_halo = lax.ppermute(inputs_sent, ("section", "seq"), ahead)
        send_halo((owns[0],))
        sources, outgoing, received = [], [], []
        for k, (first, last) in enumerate(bounds):
            part = max(i for i, start in enumerate(starts) if start <= first)
            while part >= len(owns):
                send_halo(tuple(early))
            at = (first - starts[part]) // block
            array, offset = incoming[k]
            before = tuple(outgoing[-1:])
            if hop == sections - 2 and k == 2:
                uppers.append(upper_grad(1, owns[-1:]))
                filtered.append(turned_filter(0, owns[-1:] + received[:1]))
                filtered.append(turned_filter(1, filtered[-1:]))
                before += (uppers[-1][0], filtered[-1])
            out = call(
                functools.partial(filter_kernel, group_size),
                ((last - first) // block,),
                [SMEM, spec(rows, block, at), spec(rows, block, at), group_spec(first // block),
                 spec(rows, block, first // block), spec(rows, block, (first - offset) // block)],
                spec(rows, block),
                bf16(last - first),
                name="filter",
                cycles=1000,
                after=before,
            )(role, owns[part], halos[part], taps, mid_gate, array, *before)
            sources.append((owns[part], halos[part], at))
            outgoing.append(out)
            received.append(lax.ppermute(out, "section", down))
            if hop == sections - 2 and k == 1:
                uppers = [upper_grad(0, (out,))]
                seconds = moments((out,))
                early = [uppers[0][0], seconds[0]]
        top = my_section == sections - 1
        incoming = [
            (jnp.where(top, cotangent[:, first:last], arrived), first)
            for (first, last), arrived in zip(bounds, received)
        ]

    latest = outgoing[-1:]
    for k in range(len(filtered), len(bounds)):
        filtered.append(turned_filter(k, latest))
        latest = filtered[-1:]
    for k in range(len(uppers), len(bounds)):
        uppers.append(upper_grad(k, latest))
        latest = uppers[-1][:1]
    firsts = []
    for k, (first, last) in enumerate(bounds):
        here = spec(rows, block, first // block)
        firsts.append(call(
            functools.partial(first_grad_kernel, group_size),
            ((last - first) // block,),
            [SMEM, here, here, here, here, here, spec(rows, block), spec(rows, block)],
            grad_specs,
            grad_shapes(k),
            name="first_grads",
            cycles=2000,
            after=tuple(latest),
        )(role, in_gate, mid_gate, layer_inputs, mid_halo, inputs_halo, received[k], filtered[k], *latest))
        latest = firsts[-1][:1]
    partial_sums = [grads[i] for both in (firsts, uppers) for i in range(2) for grads in both]

    own_channels = channels // seqs
    lines = groups // seqs + pl.cdiv(own_channels, LANES)
    packed = pl.pallas_call(
        functools.partial(pack_kernel, seqs),
        in_specs=[SMEM] + [vmem] * len(partial_sums),
        out_specs=vmem,
        out_shape=jax.ShapeDtypeStruct((seqs, lines, LANES), BF16),
        compiler_params=SMALL,
        name="pack",
    )(role, *partial_sums)
    parts = lax.all_to_all(packed, "seq", 0, 0)
    steer_step, filter_step = pl.pallas_call(
        step_kernel,
        in_specs=[SMEM] + [vmem] * 3,
        out_shape=[
            jax.ShapeDtypeStruct((1, own_channels), F32),
            jax.ShapeDtypeStruct((groups // seqs, filt_len), F32),
        ],
        compiler_params=SMALL,
        name="step",
    )(role, parts, *seconds)
    return steer_step, filter_step.T[None]


def solution(mesh):
    in_specs = (
        P("seq", None),
        P("section", "seq", None),
        P("section", "seq", None),
        P("section", "seq", None),
        P("section", None, None),
        P("section", "seq"),
        P("section", None, "seq"),
    )
    out_specs = (P("section", "seq"), P("section", None, "seq"))
    return jax.shard_map(body, mesh=mesh, in_specs=in_specs, out_specs=out_specs, check_vma=False)
```

```python
import functools

import jax
import jax.numpy as jnp
from jax import lax
from jax.experimental import pallas as pl
from jax.experimental.pallas import tpu as pltpu
from jax.sharding import PartitionSpec as P

F32 = jnp.float32
BF16 = jnp.bfloat16
LANES = 128
SUB = 32
CHUNK_EDGES = (0, 3, 6, 7, 8)
HALO_EDGES = (0, 3, 6, 8)


def lane_of(shape):
    return lax.broadcasted_iota(jnp.int32, shape, 1)


def row_of(shape):
    return lax.broadcasted_iota(jnp.int32, shape, 0)


def first_section(role):
    return (role[0] & 1) > 0


def times(a, b):
    return (a.astype(F32) * b.astype(F32)).astype(BF16)


def turned(x):
    return pltpu.roll(x, LANES // 2, 1)


def spread(x, x_turned, parity, count):
    low = lane_of((count, LANES)) < LANES // 2
    natural, other = (x, x_turned) if parity == 0 else (x_turned, x)
    tiles = []
    for first in (0, 2 * SUB):
        tiles.append(jnp.where(low, natural[first : first + count], other[first + SUB : first + SUB + count]))
    return jnp.concatenate(tiles, 1)


def gathered(even, odd):
    low = lane_of((SUB, LANES)) < LANES // 2
    out = []
    for tile in range(2):
        a = even[:, tile * LANES : (tile + 1) * LANES]
        b = odd[:, tile * LANES : (tile + 1) * LANES]
        out.append(jnp.where(low, a, turned(b)))
        out.append(jnp.where(low, turned(a), b))
    return jnp.concatenate(out, 0)


def in_order(reverse, own, halo):
    return jnp.concatenate([jnp.where(reverse, halo, own), jnp.where(reverse, own, halo)], 0)


def diagonal_sums(blocks):
    tiles = []
    for block in blocks:
        tile = block[:8]
        for first in range(8, SUB, 8):
            tile = tile + pltpu.roll(block[first : first + 8], LANES - first, 1)
        tiles.append(tile)
    row = row_of((8, LANES))
    for fold in (4, 2, 1):
        upper = row % (2 * fold) < fold
        tiles = [
            jnp.where(upper, a, pltpu.roll(b, fold, 0))
            + pltpu.roll(jnp.where(upper, pltpu.roll(a, 8 - fold, 0), b), LANES - fold, 1)
            for a, b in zip(tiles[:fold], tiles[fold:])
        ]
    return tiles[0]


def near(reverse_int, shape):
    return lane_of(shape) - row_of(shape) >= reverse_int


def tap_matrix(reverse, taps_by_group):
    taps = taps_by_group.shape[0]
    source = row_of((taps, taps))
    target = lane_of((taps, taps))
    mirrored = jnp.where(source == 0, 0, taps - source)
    pick = jnp.where(target == jnp.where(reverse, mirrored, source), 1.0, 0.0)
    return pick, taps


def weigh_kernel(role, gate, incoming, out):
    @pl.when(jnp.logical_not(first_section(role)))
    def _():
        out[...] = times(gate[...], incoming[...])


def direct_weigh_kernel(first, block, role, gate, incoming, out, gate_part, incoming_part, sems):
    @pl.when(jnp.logical_not(first_section(role)))
    def _():
        tiles = [pl.ds(at, block) for at in range(0, out.shape[1], block)]
        copies = [
            [
                pltpu.make_async_copy(source.at[:, pl.ds(first + i * block, block)], part.at[:, t], sems.at[which, i])
                for which, (source, part) in enumerate(((gate, gate_part), (incoming, incoming_part)))
            ]
            for i, t in enumerate(tiles)
        ]
        for pair in copies:
            for copy in pair:
                copy.start()
        for t, pair in zip(tiles, copies):
            for copy in pair:
                copy.wait()
            out[:, t] = times(gate_part[:, t], incoming_part[:, t])


def moments_kernel(role, steer_second, filter_second, *refs):
    steer_out, filter_out = refs[-2:]
    steer_out[...] = steer_second[...]
    filter_out[...] = filter_second[...]


def taps_kernel(role, filters, taps_out):
    pick, _ = tap_matrix(first_section(role), filters[...])
    taps_out[...] = lax.dot_general(
        filters[...], pick.astype(BF16), (((0,), (0,)), ((), ())), preferred_element_type=F32
    )


def convolved(reverse, group_size, own, halo, taps, first_group):
    half = LANES // 2
    per_half = half // group_size
    mask = near(int(reverse), (SUB, LANES))
    zero = jnp.zeros((SUB, LANES), F32)
    lane_group = (lane_of((SUB, 2 * LANES)) % half) // group_size
    ext = jnp.concatenate([halo, own] if reverse else [own, halo], 0)
    ext_turned = turned(ext)
    results = []
    for parity in range(2):
        window = spread(ext, ext_turned, parity, own.shape[0] + SUB)
        bands = []
        for g in range(per_half):
            row = taps[pl.ds(first_group + parity * per_half + g, 1), :]
            circ = pltpu.roll(jnp.broadcast_to(row, (SUB, LANES)), 0, 1, stride=1, stride_axis=0)
            band = jnp.concatenate([jnp.where(mask, circ, zero), jnp.where(mask, zero, circ)[:, :SUB]], 1)
            bands.append(band.astype(BF16))
        product = jnp.dot(jnp.concatenate(bands, 0), window, preferred_element_type=F32)
        total = product[:SUB]
        for g in range(1, per_half):
            total = jnp.where(lane_group == g, product[g * SUB : (g + 1) * SUB], total)
        results.append(total)
    return gathered(*results)


def filter_kernel(group_size, role, own, halo, taps, mid, incoming, outgoing):
    @pl.when(jnp.logical_not(first_section(role)))
    def _():
        for first in range(0, own.shape[1], LANES):
            cols = pl.ds(first, LANES)
            conv = convolved(False, group_size, own[:, cols], halo[:, cols], taps, first // group_size)
            outgoing[:, cols] = (
                incoming[:, cols].astype(F32) + mid[:, cols].astype(F32) * conv
            ).astype(BF16)


def turned_filter_kernel(group_size, role, mid, mid_halo, taps, filtered):
    @pl.when(first_section(role))
    def _():
        for first in range(0, mid.shape[1], LANES):
            cols = pl.ds(first, LANES)
            filtered[:, cols] = convolved(True, group_size, mid[:, cols], mid_halo[:, cols], taps, first // group_size)


def tap_sums(reverse, group_size, left, own, halo):
    half = LANES // 2
    per_half = half // group_size
    mask = near(int(reverse), (SUB, LANES))
    lane_group = (lane_of((SUB, 2 * LANES)) % half) // group_size
    nothing = jnp.zeros((SUB, 2 * LANES), BF16)
    ext = jnp.concatenate([halo, own] if reverse else [own, halo], 0)
    ext_turned, left_turned = turned(ext), turned(left)
    blocks = []
    for parity in range(2):
        window = spread(ext, ext_turned, parity, own.shape[0] + SUB)
        short = spread(left, left_turned, parity, SUB)
        lhs = jnp.concatenate([jnp.where(lane_group == g, short, nothing) for g in range(per_half)], 0)
        product = lax.dot_general(lhs, window, (((1,), (1,)), ((), ())), preferred_element_type=F32)
        for g in range(per_half):
            block = product[g * SUB : (g + 1) * SUB]
            late = jnp.concatenate([block[:, LANES:], jnp.zeros((SUB, LANES - SUB), F32)], 1)
            blocks.append(jnp.where(mask, block[:, :LANES], late))
    return diagonal_sums(blocks)


def upper_grad_kernel(group_size, role, mid, inputs, own, halo, outgoing, tap_grad, steer_grad):
    @pl.when(role[0] == 0)
    def _():
        steer_grad[...] = jnp.sum(outgoing[...].astype(F32), 0, keepdims=True)
        for pair in range(own.shape[1] // LANES):
            cols = pl.ds(pair * LANES, LANES)
            values = times(mid[:, cols], inputs[:, cols])
            tap_grad[pl.ds(8 * pair, 8), :] = tap_sums(False, group_size, values, own[:, cols], halo[:, cols])


def first_grad_kernel(
    group_size, role, gate, mid, inputs, mid_halo, inputs_halo, received, filtered, tap_grad, steer_grad
):
    @pl.when(role[0] > 0)
    def _():
        for pair in range(gate.shape[1] // LANES):
            cols = pl.ds(pair * LANES, LANES)
            grad = received[:, cols]
            weighted = times(gate[:, cols], grad)
            grad_in = grad.astype(F32) + weighted.astype(F32) * filtered[:, cols]
            steer_grad[:, cols] = jnp.sum(grad_in, 0, keepdims=True)
            own, halo = times(mid[:, cols], inputs[:, cols]), times(mid_halo[:, cols], inputs_halo[:, cols])
            tap_grad[pl.ds(8 * pair, 8), :] = tap_sums(True, group_size, weighted, own, halo)


def pack_kernel(owners, role, *refs):
    refs, out = refs[:-1], refs[-1]
    count = len(refs) // 4

    def part(parts, axis, at, size):
        for ref in parts:
            if at < ref.shape[axis]:
                return ref[at : at + size, :] if axis == 0 else ref[:, at : at + size]
            at -= ref.shape[axis]

    def pack(taps, steers):
        groups = sum(ref.shape[0] for ref in taps) // owners
        channels = sum(ref.shape[1] for ref in steers) // owners
        for owner in range(owners):
            lines = [part(taps, 0, owner * groups, groups)]
            for at in range(0, channels, LANES):
                size = min(LANES, channels - at)
                steer = part(steers, 1, owner * channels + at, size)
                if size < LANES:
                    steer = jnp.concatenate([steer, jnp.zeros((1, LANES - size), F32)], 1)
                lines.append(steer)
            out[owner] = jnp.concatenate(lines, 0).astype(BF16)

    @pl.when(first_section(role))
    def _():
        pack(refs[:count], refs[count : 2 * count])

    @pl.when(jnp.logical_not(first_section(role)))
    def _():
        pack(refs[2 * count : 3 * count], refs[3 * count :])


def step_kernel(role, parts, steer_second, filter_second, steer_out, filter_out):
    total = jnp.sum(parts[...].astype(F32), 0)
    groups = filter_second.shape[0]
    tap_grad = total[:groups]
    lane = lane_of(tap_grad.shape)
    mirrored = jnp.where(lane == 0, 0, tap_grad.shape[1] - lane)
    tap_grad = jnp.take_along_axis(tap_grad, jnp.where(first_section(role), mirrored, lane), axis=1)
    filter_out[...] = tap_grad / jnp.sqrt(filter_second[...] + tap_grad * tap_grad)
    channels = steer_out.shape[1]
    for row in range(pl.cdiv(channels, LANES)):
        cols = min(LANES, channels - row * LANES)
        at = pl.ds(row * LANES, cols)
        grad = total[groups + row : groups + row + 1, :cols]
        steer_out[:, at] = grad / jnp.sqrt(steer_second[:, at] + grad * grad)


def spec(rows, width, first=0):
    return pl.BlockSpec((rows, width), lambda i: (0, i + first))


SMEM = pl.BlockSpec(memory_space=pltpu.SMEM)
ANY = pl.BlockSpec(memory_space=pl.ANY)
SMALL = pltpu.CompilerParams(vmem_limit_bytes=4 * 1024 * 1024)


def call(kernel, grid, in_specs, out_specs, out_shape, scratch=(), name=None, cycles=100, after=()):
    count = len(in_specs)

    def with_after(*refs):
        kernel(*refs[:count], *refs[count + len(after) :])

    return pl.pallas_call(
        with_after,
        grid=grid,
        in_specs=list(in_specs) + [ANY] * len(after),
        out_specs=out_specs,
        out_shape=out_shape,
        scratch_shapes=list(scratch),
        compiler_params=pltpu.CompilerParams(vmem_limit_bytes=16 * 1024 * 1024),
        cost_estimate=pl.CostEstimate(flops=cycles, bytes_accessed=0, transcendentals=0),
        name=name,
    )


def body(cotangent, in_gate, mid_gate, layer_inputs, filters, steer_second, filter_second):
    in_gate, mid_gate, layer_inputs = in_gate[0], mid_gate[0], layer_inputs[0]
    rows, channels = in_gate.shape
    filt_len, groups = filters.shape[1:]
    group_size = channels // groups
    sections, seqs = lax.axis_size("section"), lax.axis_size("seq")
    my_section = lax.axis_index("section")
    role = (my_section == 0).astype(jnp.int32).reshape(1)

    edges = [channels * eighths // 8 for eighths in CHUNK_EDGES]
    bounds = list(zip(edges[:-1], edges[1:]))
    block = channels // 8
    block_groups = block // group_size
    behind = [(seqs * s + i, seqs * s + i - 1) for s in range(1, sections) for i in range(1, seqs)]
    ahead = [(i, i + 1) for i in range(seqs - 1)]
    down = [(s, s - 1) for s in range(1, sections)]

    def bf16(width_of):
        return jax.ShapeDtypeStruct((rows, width_of), BF16)

    def weigh(incoming, first, last, offset, after):
        return call(
            weigh_kernel,
            ((last - first) // block,),
            [SMEM, spec(rows, block, first // block), spec(rows, block, (first - offset) // block)],
            spec(rows, block),
            bf16(last - first),
            name="weigh",
            after=after,
        )(role, in_gate, incoming, *after)

    def direct_weigh(first, last, after):
        width = last - first
        part = pltpu.VMEM((rows, width), BF16)

        def kernel(*refs):
            direct_weigh_kernel(first, block, *refs[:3], *refs[3 + len(after) :])

        return pl.pallas_call(
            kernel,
            in_specs=[SMEM] + [ANY] * (2 + len(after)),
            out_specs=pl.BlockSpec(memory_space=pltpu.VMEM),
            out_shape=bf16(width),
            scratch_shapes=[part, part, pltpu.SemaphoreType.DMA((2, width // block))],
            compiler_params=SMALL,
            name="direct_weigh",
        )(role, *[pltpu.with_memory_space_constraint(a, pltpu.HBM) for a in (in_gate, cotangent)], *after)

    vmem = pl.BlockSpec(memory_space=pltpu.VMEM)
    taps = pl.pallas_call(
        taps_kernel,
        in_specs=[SMEM, vmem],
        out_specs=vmem,
        out_shape=jax.ShapeDtypeStruct((groups, filt_len), F32),
        compiler_params=SMALL,
        name="taps",
    )(role, filters[0])

    def moments(after):
        seconds = (steer_second, filter_second[0].T)
        return pl.pallas_call(
            moments_kernel,
            in_specs=[SMEM] + [vmem] * 2 + [ANY] * len(after),
            out_specs=[vmem] * 2,
            out_shape=[jax.ShapeDtypeStruct(second.shape, F32) for second in seconds],
            compiler_params=SMALL,
            name="moments",
        )(role, *seconds, *after)

    group_spec = lambda first: pl.BlockSpec((block_groups, filt_len), lambda i: (i + first, 0))

    grad_specs = [group_spec(0), pl.BlockSpec((1, block), lambda i: (0, i))]

    def grad_shapes(k):
        width = bounds[k][1] - bounds[k][0]
        return [
            jax.ShapeDtypeStruct((width // group_size, filt_len), F32),
            jax.ShapeDtypeStruct((1, width), F32),
        ]

    def upper_grad(k, after):
        first, last = bounds[k]
        own, halo, at = sources[k]
        here, there = spec(rows, block, first // block), spec(rows, block, at)
        return call(
            functools.partial(upper_grad_kernel, group_size),
            ((last - first) // block,),
            [SMEM, here, here, there, there, spec(rows, block)],
            grad_specs,
            grad_shapes(k),
            name="upper_grads",
            cycles=6 * 10**9 if k == 0 else 2000,
            after=tuple(after),
        )(role, mid_gate, layer_inputs, own, halo, outgoing[k], *after)

    def turned_filter(k, after):
        first, last = bounds[k]
        here = spec(rows, block, first // block)
        return call(
            functools.partial(turned_filter_kernel, group_size),
            ((last - first) // block,),
            [SMEM, here, here, group_spec(first // block)],
            spec(rows, block),
            jax.ShapeDtypeStruct((rows, last - first), F32),
            name="turned_filter",
            cycles=1000,
            after=tuple(after),
        )(role, mid_gate, mid_halo, taps, *after)

    incoming = [(cotangent, 0)] * len(bounds)
    early, uppers, filtered = [], [], []
    for hop in range(sections - 1):
        split = [channels * eighths // 8 for eighths in HALO_EDGES] if hop == 0 else edges
        starts, ends = split[:-1], split[1:]
        owns, halos = [], []

        def send_halo(after):
            first, last = starts[len(owns)], ends[len(owns)]
            array, offset = next(entry for entry, edge in zip(incoming, edges) if edge == first)
            if hop == 0 and not early:
                owns.append(direct_weigh(first, last, after))
            else:
                owns.append(weigh(array, first, last, offset, after))
            halos.append(lax.ppermute(owns[-1], ("section", "seq"), behind))

        send_halo(())
        if hop == 0:
            mid_sent, inputs_sent, _ = lax.optimization_barrier((mid_gate, layer_inputs, owns[0]))
            mid_halo = lax.ppermute(mid_sent, ("section", "seq"), ahead)
            inputs_halo = lax.ppermute(inputs_sent, ("section", "seq"), ahead)
        send_halo((owns[0],))
        sources, outgoing, received = [], [], []
        for k, (first, last) in enumerate(bounds):
            part = max(i for i, start in enumerate(starts) if start <= first)
            while part >= len(owns):
                send_halo(tuple(early))
            at = (first - starts[part]) // block
            array, offset = incoming[k]
            before = tuple(outgoing[-1:])
            if hop == sections - 2 and k == 2:
                uppers.append(upper_grad(1, owns[-1:]))
                filtered.append(turned_filter(0, owns[-1:] + received[:1]))
                filtered.append(turned_filter(1, filtered[-1:]))
                seconds = moments(owns[-1:])
                before += (uppers[-1][0], filtered[-1], seconds[0])
            out = call(
                functools.partial(filter_kernel, group_size),
                ((last - first) // block,),
                [SMEM, spec(rows, block, at), spec(rows, block, at), group_spec(first // block),
                 spec(rows, block, first // block), spec(rows, block, (first - offset) // block)],
                spec(rows, block),
                bf16(last - first),
                name="filter",
                cycles=1000,
                after=before,
            )(role, owns[part], halos[part], taps, mid_gate, array, *before)
            sources.append((owns[part], halos[part], at))
            outgoing.append(out)
            received.append(lax.ppermute(out, "section", down))
            if hop == sections - 2 and k == 1:
                uppers = [upper_grad(0, (out,))]
                early = [uppers[0][0]]
        top = my_section == sections - 1
        incoming = [
            (jnp.where(top, cotangent[:, first:last], arrived), first)
            for (first, last), arrived in zip(bounds, received)
        ]

    latest = outgoing[-1:]
    for k in range(len(filtered), len(bounds)):
        filtered.append(turned_filter(k, latest))
        latest = filtered[-1:]
    for k in range(len(uppers), len(bounds)):
        uppers.append(upper_grad(k, latest))
        latest = uppers[-1][:1]
    firsts = []
    for k, (first, last) in enumerate(bounds):
        here = spec(rows, block, first // block)
        firsts.append(call(
            functools.partial(first_grad_kernel, group_size),
            ((last - first) // block,),
            [SMEM, here, here, here, here, here, spec(rows, block), spec(rows, block)],
            grad_specs,
            grad_shapes(k),
            name="first_grads",
            cycles=2000,
            after=tuple(latest),
        )(role, in_gate, mid_gate, layer_inputs, mid_halo, inputs_halo, received[k], filtered[k], *latest))
        latest = firsts[-1][:1]
    partial_sums = [grads[i] for both in (firsts, uppers) for i in range(2) for grads in both]

    own_channels = channels // seqs
    lines = groups // seqs + pl.cdiv(own_channels, LANES)
    packed = pl.pallas_call(
        functools.partial(pack_kernel, seqs),
        in_specs=[SMEM] + [vmem] * len(partial_sums),
        out_specs=vmem,
        out_shape=jax.ShapeDtypeStruct((seqs, lines, LANES), BF16),
        compiler_params=SMALL,
        name="pack",
    )(role, *partial_sums)
    parts = lax.all_to_all(packed, "seq", 0, 0)
    steer_step, filter_step = pl.pallas_call(
        step_kernel,
        in_specs=[SMEM] + [vmem] * 3,
        out_shape=[
            jax.ShapeDtypeStruct((1, own_channels), F32),
            jax.ShapeDtypeStruct((groups // seqs, filt_len), F32),
        ],
        compiler_params=SMALL,
        name="step",
    )(role, parts, *seconds)
    return steer_step, filter_step.T[None]


def solution(mesh):
    in_specs = (
        P("seq", None),
        P("section", "seq", None),
        P("section", "seq", None),
        P("section", "seq", None),
        P("section", None, None),
        P("section", "seq"),
        P("section", None, "seq"),
    )
    out_specs = (P("section", "seq"), P("section", None, "seq"))
    return jax.shard_map(body, mesh=mesh, in_specs=in_specs, out_specs=out_specs, check_vma=False)
```

```python
import functools

import jax
import jax.numpy as jnp
from jax import lax
from jax.experimental import pallas as pl
from jax.experimental.pallas import tpu as pltpu
from jax.sharding import PartitionSpec as P

F32 = jnp.float32
BF16 = jnp.bfloat16
LANES = 128
SUB = 32
CHUNK_EDGES = (0, 3, 6, 8)
HALO_EDGES = (0, 3, 6, 8)


def lane_of(shape):
    return lax.broadcasted_iota(jnp.int32, shape, 1)


def row_of(shape):
    return lax.broadcasted_iota(jnp.int32, shape, 0)


def first_section(role):
    return (role[0] & 1) > 0


def times(a, b):
    return (a.astype(F32) * b.astype(F32)).astype(BF16)


def turned(x):
    return pltpu.roll(x, LANES // 2, 1)


def spread(x, x_turned, parity, count):
    low = lane_of((count, LANES)) < LANES // 2
    natural, other = (x, x_turned) if parity == 0 else (x_turned, x)
    tiles = []
    for first in (0, 2 * SUB):
        tiles.append(jnp.where(low, natural[first : first + count], other[first + SUB : first + SUB + count]))
    return jnp.concatenate(tiles, 1)


def gathered(even, odd):
    low = lane_of((SUB, LANES)) < LANES // 2
    out = []
    for tile in range(2):
        a = even[:, tile * LANES : (tile + 1) * LANES]
        b = odd[:, tile * LANES : (tile + 1) * LANES]
        out.append(jnp.where(low, a, turned(b)))
        out.append(jnp.where(low, turned(a), b))
    return jnp.concatenate(out, 0)


def in_order(reverse, own, halo):
    return jnp.concatenate([jnp.where(reverse, halo, own), jnp.where(reverse, own, halo)], 0)


def diagonal_sums(blocks):
    tiles = []
    for block in blocks:
        tile = block[:8]
        for first in range(8, SUB, 8):
            tile = tile + pltpu.roll(block[first : first + 8], LANES - first, 1)
        tiles.append(tile)
    row = row_of((8, LANES))
    for fold in (4, 2, 1):
        upper = row % (2 * fold) < fold
        tiles = [
            jnp.where(upper, a, pltpu.roll(b, fold, 0))
            + pltpu.roll(jnp.where(upper, pltpu.roll(a, 8 - fold, 0), b), LANES - fold, 1)
            for a, b in zip(tiles[:fold], tiles[fold:])
        ]
    return tiles[0]


def near(reverse_int, shape):
    return lane_of(shape) - row_of(shape) >= reverse_int


def tap_matrix(reverse, taps_by_group):
    taps = taps_by_group.shape[0]
    source = row_of((taps, taps))
    target = lane_of((taps, taps))
    mirrored = jnp.where(source == 0, 0, taps - source)
    pick = jnp.where(target == jnp.where(reverse, mirrored, source), 1.0, 0.0)
    return pick, taps


def weigh_kernel(role, gate, incoming, out):
    @pl.when(jnp.logical_not(first_section(role)))
    def _():
        out[...] = times(gate[...], incoming[...])


def direct_weigh_kernel(first, block, role, gate, incoming, out, gate_part, incoming_part, sems):
    @pl.when(jnp.logical_not(first_section(role)))
    def _():
        tiles = [pl.ds(at, block) for at in range(0, out.shape[1], block)]
        copies = [
            [
                pltpu.make_async_copy(source.at[:, pl.ds(first + i * block, block)], part.at[:, t], sems.at[which, i])
                for which, (source, part) in enumerate(((gate, gate_part), (incoming, incoming_part)))
            ]
            for i, t in enumerate(tiles)
        ]
        for pair in copies:
            for copy in pair:
                copy.start()
        for t, pair in zip(tiles, copies):
            for copy in pair:
                copy.wait()
            out[:, t] = times(gate_part[:, t], incoming_part[:, t])


def moments_kernel(role, steer_second, filter_second, *refs):
    steer_out, filter_out = refs[-2:]
    steer_out[...] = steer_second[...]
    filter_out[...] = filter_second[...]


def taps_kernel(role, filters, taps_out):
    pick, _ = tap_matrix(first_section(role), filters[...])
    taps_out[...] = lax.dot_general(
        filters[...], pick.astype(BF16), (((0,), (0,)), ((), ())), preferred_element_type=F32
    )


def convolved(reverse, group_size, own, halo, taps, first_group):
    half = LANES // 2
    per_half = half // group_size
    mask = near(int(reverse), (SUB, LANES))
    zero = jnp.zeros((SUB, LANES), F32)
    lane_group = (lane_of((SUB, 2 * LANES)) % half) // group_size
    ext = jnp.concatenate([halo, own] if reverse else [own, halo], 0)
    ext_turned = turned(ext)
    results = []
    for parity in range(2):
        window = spread(ext, ext_turned, parity, own.shape[0] + SUB)
        bands = []
        for g in range(per_half):
            row = taps[pl.ds(first_group + parity * per_half + g, 1), :]
            circ = pltpu.roll(jnp.broadcast_to(row, (SUB, LANES)), 0, 1, stride=1, stride_axis=0)
            band = jnp.concatenate([jnp.where(mask, circ, zero), jnp.where(mask, zero, circ)[:, :SUB]], 1)
            bands.append(band.astype(BF16))
        product = jnp.dot(jnp.concatenate(bands, 0), window, preferred_element_type=F32)
        total = product[:SUB]
        for g in range(1, per_half):
            total = jnp.where(lane_group == g, product[g * SUB : (g + 1) * SUB], total)
        results.append(total)
    return gathered(*results)


def filter_kernel(group_size, role, own, halo, taps, mid, incoming, outgoing):
    @pl.when(jnp.logical_not(first_section(role)))
    def _():
        for first in range(0, own.shape[1], LANES):
            cols = pl.ds(first, LANES)
            conv = convolved(False, group_size, own[:, cols], halo[:, cols], taps, first // group_size)
            outgoing[:, cols] = (
                incoming[:, cols].astype(F32) + mid[:, cols].astype(F32) * conv
            ).astype(BF16)


def turned_filter_kernel(group_size, role, mid, mid_halo, taps, filtered):
    @pl.when(first_section(role))
    def _():
        for first in range(0, mid.shape[1], LANES):
            cols = pl.ds(first, LANES)
            filtered[:, cols] = convolved(True, group_size, mid[:, cols], mid_halo[:, cols], taps, first // group_size)


def tap_sums(reverse, group_size, left, own, halo):
    half = LANES // 2
    per_half = half // group_size
    mask = near(int(reverse), (SUB, LANES))
    lane_group = (lane_of((SUB, 2 * LANES)) % half) // group_size
    nothing = jnp.zeros((SUB, 2 * LANES), BF16)
    ext = jnp.concatenate([halo, own] if reverse else [own, halo], 0)
    ext_turned, left_turned = turned(ext), turned(left)
    blocks = []
    for parity in range(2):
        window = spread(ext, ext_turned, parity, own.shape[0] + SUB)
        short = spread(left, left_turned, parity, SUB)
        lhs = jnp.concatenate([jnp.where(lane_group == g, short, nothing) for g in range(per_half)], 0)
        product = lax.dot_general(lhs, window, (((1,), (1,)), ((), ())), preferred_element_type=F32)
        for g in range(per_half):
            block = product[g * SUB : (g + 1) * SUB]
            late = jnp.concatenate([block[:, LANES:], jnp.zeros((SUB, LANES - SUB), F32)], 1)
            blocks.append(jnp.where(mask, block[:, :LANES], late))
    return diagonal_sums(blocks)


def upper_grad_kernel(group_size, role, mid, inputs, own, halo, outgoing, tap_grad, steer_grad):
    @pl.when(role[0] == 0)
    def _():
        steer_grad[...] = jnp.sum(outgoing[...].astype(F32), 0, keepdims=True)
        for pair in range(own.shape[1] // LANES):
            cols = pl.ds(pair * LANES, LANES)
            values = times(mid[:, cols], inputs[:, cols])
            tap_grad[pl.ds(8 * pair, 8), :] = tap_sums(False, group_size, values, own[:, cols], halo[:, cols])


def first_grad_kernel(
    group_size, role, gate, mid, inputs, mid_halo, inputs_halo, received, filtered, tap_grad, steer_grad
):
    @pl.when(role[0] > 0)
    def _():
        for pair in range(gate.shape[1] // LANES):
            cols = pl.ds(pair * LANES, LANES)
            grad = received[:, cols]
            weighted = times(gate[:, cols], grad)
            grad_in = grad.astype(F32) + weighted.astype(F32) * filtered[:, cols]
            steer_grad[:, cols] = jnp.sum(grad_in, 0, keepdims=True)
            own, halo = times(mid[:, cols], inputs[:, cols]), times(mid_halo[:, cols], inputs_halo[:, cols])
            tap_grad[pl.ds(8 * pair, 8), :] = tap_sums(True, group_size, weighted, own, halo)


def pack_kernel(owners, role, *refs):
    refs, out = refs[:-1], refs[-1]
    count = len(refs) // 4

    def part(parts, axis, at, size):
        for ref in parts:
            if at < ref.shape[axis]:
                return ref[at : at + size, :] if axis == 0 else ref[:, at : at + size]
            at -= ref.shape[axis]

    def pack(taps, steers):
        groups = sum(ref.shape[0] for ref in taps) // owners
        channels = sum(ref.shape[1] for ref in steers) // owners
        for owner in range(owners):
            lines = [part(taps, 0, owner * groups, groups)]
            for at in range(0, channels, LANES):
                size = min(LANES, channels - at)
                steer = part(steers, 1, owner * channels + at, size)
                if size < LANES:
                    steer = jnp.concatenate([steer, jnp.zeros((1, LANES - size), F32)], 1)
                lines.append(steer)
            out[owner] = jnp.concatenate(lines, 0).astype(BF16)

    @pl.when(first_section(role))
    def _():
        pack(refs[:count], refs[count : 2 * count])

    @pl.when(jnp.logical_not(first_section(role)))
    def _():
        pack(refs[2 * count : 3 * count], refs[3 * count :])


def step_kernel(role, parts, steer_second, filter_second, steer_out, filter_out):
    total = jnp.sum(parts[...].astype(F32), 0)
    groups = filter_second.shape[0]
    tap_grad = total[:groups]
    lane = lane_of(tap_grad.shape)
    mirrored = jnp.where(lane == 0, 0, tap_grad.shape[1] - lane)
    tap_grad = jnp.take_along_axis(tap_grad, jnp.where(first_section(role), mirrored, lane), axis=1)
    filter_out[...] = tap_grad / jnp.sqrt(filter_second[...] + tap_grad * tap_grad)
    channels = steer_out.shape[1]
    for row in range(pl.cdiv(channels, LANES)):
        cols = min(LANES, channels - row * LANES)
        at = pl.ds(row * LANES, cols)
        grad = total[groups + row : groups + row + 1, :cols]
        steer_out[:, at] = grad / jnp.sqrt(steer_second[:, at] + grad * grad)


def spec(rows, width, first=0):
    return pl.BlockSpec((rows, width), lambda i: (0, i + first))


SMEM = pl.BlockSpec(memory_space=pltpu.SMEM)
ANY = pl.BlockSpec(memory_space=pl.ANY)
SMALL = pltpu.CompilerParams(vmem_limit_bytes=4 * 1024 * 1024)


def call(kernel, grid, in_specs, out_specs, out_shape, scratch=(), name=None, cycles=100, after=()):
    count = len(in_specs)

    def with_after(*refs):
        kernel(*refs[:count], *refs[count + len(after) :])

    return pl.pallas_call(
        with_after,
        grid=grid,
        in_specs=list(in_specs) + [ANY] * len(after),
        out_specs=out_specs,
        out_shape=out_shape,
        scratch_shapes=list(scratch),
        compiler_params=pltpu.CompilerParams(vmem_limit_bytes=16 * 1024 * 1024),
        cost_estimate=pl.CostEstimate(flops=cycles, bytes_accessed=0, transcendentals=0),
        name=name,
    )


def body(cotangent, in_gate, mid_gate, layer_inputs, filters, steer_second, filter_second):
    in_gate, mid_gate, layer_inputs = in_gate[0], mid_gate[0], layer_inputs[0]
    rows, channels = in_gate.shape
    filt_len, groups = filters.shape[1:]
    group_size = channels // groups
    sections, seqs = lax.axis_size("section"), lax.axis_size("seq")
    my_section = lax.axis_index("section")
    role = (my_section == 0).astype(jnp.int32).reshape(1)

    edges = [channels * eighths // 8 for eighths in CHUNK_EDGES]
    bounds = list(zip(edges[:-1], edges[1:]))
    block = channels // 8
    block_groups = block // group_size
    behind = [(seqs * s + i, seqs * s + i - 1) for s in range(1, sections) for i in range(1, seqs)]
    ahead = [(i, i + 1) for i in range(seqs - 1)]
    down = [(s, s - 1) for s in range(1, sections)]

    def bf16(width_of):
        return jax.ShapeDtypeStruct((rows, width_of), BF16)

    def weigh(incoming, first, last, offset, after):
        return call(
            weigh_kernel,
            ((last - first) // block,),
            [SMEM, spec(rows, block, first // block), spec(rows, block, (first - offset) // block)],
            spec(rows, block),
            bf16(last - first),
            name="weigh",
            after=after,
        )(role, in_gate, incoming, *after)

    def direct_weigh(first, last, after):
        width = last - first
        part = pltpu.VMEM((rows, width), BF16)

        def kernel(*refs):
            direct_weigh_kernel(first, block, *refs[:3], *refs[3 + len(after) :])

        return pl.pallas_call(
            kernel,
            in_specs=[SMEM] + [ANY] * (2 + len(after)),
            out_specs=pl.BlockSpec(memory_space=pltpu.VMEM),
            out_shape=bf16(width),
            scratch_shapes=[part, part, pltpu.SemaphoreType.DMA((2, width // block))],
            compiler_params=SMALL,
            name="direct_weigh",
        )(role, *[pltpu.with_memory_space_constraint(a, pltpu.HBM) for a in (in_gate, cotangent)], *after)

    vmem = pl.BlockSpec(memory_space=pltpu.VMEM)
    taps = pl.pallas_call(
        taps_kernel,
        in_specs=[SMEM, vmem],
        out_specs=vmem,
        out_shape=jax.ShapeDtypeStruct((groups, filt_len), F32),
        compiler_params=SMALL,
        name="taps",
    )(role, filters[0])

    def moments(after):
        seconds = (steer_second, filter_second[0].T)
        return pl.pallas_call(
            moments_kernel,
            in_specs=[SMEM] + [vmem] * 2 + [ANY] * len(after),
            out_specs=[vmem] * 2,
            out_shape=[jax.ShapeDtypeStruct(second.shape, F32) for second in seconds],
            compiler_params=SMALL,
            name="moments",
        )(role, *seconds, *after)

    group_spec = lambda first: pl.BlockSpec((block_groups, filt_len), lambda i: (i + first, 0))

    grad_specs = [group_spec(0), pl.BlockSpec((1, block), lambda i: (0, i))]

    def grad_shapes(k):
        width = bounds[k][1] - bounds[k][0]
        return [
            jax.ShapeDtypeStruct((width // group_size, filt_len), F32),
            jax.ShapeDtypeStruct((1, width), F32),
        ]

    def upper_grad(k, after):
        first, last = bounds[k]
        own, halo, at = sources[k]
        here, there = spec(rows, block, first // block), spec(rows, block, at)
        return call(
            functools.partial(upper_grad_kernel, group_size),
            ((last - first) // block,),
            [SMEM, here, here, there, there, spec(rows, block)],
            grad_specs,
            grad_shapes(k),
            name="upper_grads",
            cycles=6 * 10**9 if k == 0 else 2000,
            after=tuple(after),
        )(role, mid_gate, layer_inputs, own, halo, outgoing[k], *after)

    def turned_filter(k, after):
        first, last = bounds[k]
        here = spec(rows, block, first // block)
        return call(
            functools.partial(turned_filter_kernel, group_size),
            ((last - first) // block,),
            [SMEM, here, here, group_spec(first // block)],
            spec(rows, block),
            jax.ShapeDtypeStruct((rows, last - first), F32),
            name="turned_filter",
            cycles=1000,
            after=tuple(after),
        )(role, mid_gate, mid_halo, taps, *after)

    incoming = [(cotangent, 0)] * len(bounds)
    early, uppers, filtered = [], [], []
    for hop in range(sections - 1):
        split = [channels * eighths // 8 for eighths in HALO_EDGES] if hop == 0 else edges
        starts, ends = split[:-1], split[1:]
        owns, halos = [], []

        def send_halo(after):
            first, last = starts[len(owns)], ends[len(owns)]
            array, offset = next(entry for entry, edge in zip(incoming, edges) if edge == first)
            if hop == 0 and not early:
                owns.append(direct_weigh(first, last, after))
            else:
                owns.append(weigh(array, first, last, offset, after))
            halos.append(lax.ppermute(owns[-1], ("section", "seq"), behind))

        send_halo(())
        if hop == 0:
            mid_sent, inputs_sent, _ = lax.optimization_barrier((mid_gate, layer_inputs, owns[0]))
            mid_halo = lax.ppermute(mid_sent, ("section", "seq"), ahead)
            inputs_halo = lax.ppermute(inputs_sent, ("section", "seq"), ahead)
        send_halo((owns[0],))
        sources, outgoing, received = [], [], []
        for k, (first, last) in enumerate(bounds):
            part = max(i for i, start in enumerate(starts) if start <= first)
            while part >= len(owns):
                send_halo(tuple(early))
            at = (first - starts[part]) // block
            array, offset = incoming[k]
            before = tuple(outgoing[-1:])
            if hop == sections - 2 and k == 2:
                uppers.append(upper_grad(1, owns[-1:]))
                filtered.append(turned_filter(0, owns[-1:] + received[:1]))
                filtered.append(turned_filter(1, filtered[-1:]))
                before += (uppers[-1][0], filtered[-1])
            out = call(
                functools.partial(filter_kernel, group_size),
                ((last - first) // block,),
                [SMEM, spec(rows, block, at), spec(rows, block, at), group_spec(first // block),
                 spec(rows, block, first // block), spec(rows, block, (first - offset) // block)],
                spec(rows, block),
                bf16(last - first),
                name="filter",
                cycles=1000,
                after=before,
            )(role, owns[part], halos[part], taps, mid_gate, array, *before)
            sources.append((owns[part], halos[part], at))
            outgoing.append(out)
            received.append(lax.ppermute(out, "section", down))
            if hop == sections - 2 and k == 1:
                uppers = [upper_grad(0, (out,))]
                seconds = moments((out,))
                early = [uppers[0][0], seconds[0]]
        top = my_section == sections - 1
        incoming = [
            (jnp.where(top, cotangent[:, first:last], arrived), first)
            for (first, last), arrived in zip(bounds, received)
        ]

    latest = outgoing[-1:]
    for k in range(len(filtered), len(bounds)):
        filtered.append(turned_filter(k, latest))
        latest = filtered[-1:]
    for k in range(len(uppers), len(bounds)):
        uppers.append(upper_grad(k, latest))
        latest = uppers[-1][:1]
    firsts = []
    for k, (first, last) in enumerate(bounds):
        here = spec(rows, block, first // block)
        firsts.append(call(
            functools.partial(first_grad_kernel, group_size),
            ((last - first) // block,),
            [SMEM, here, here, here, here, here, spec(rows, block), spec(rows, block)],
            grad_specs,
            grad_shapes(k),
            name="first_grads",
            cycles=2000,
            after=tuple(latest),
        )(role, in_gate, mid_gate, layer_inputs, mid_halo, inputs_halo, received[k], filtered[k], *latest))
        latest = firsts[-1][:1]
    partial_sums = [grads[i] for both in (firsts, uppers) for i in range(2) for grads in both]

    own_channels = channels // seqs
    lines = groups // seqs + pl.cdiv(own_channels, LANES)
    packed = pl.pallas_call(
        functools.partial(pack_kernel, seqs),
        in_specs=[SMEM] + [vmem] * len(partial_sums),
        out_specs=vmem,
        out_shape=jax.ShapeDtypeStruct((seqs, lines, LANES), BF16),
        compiler_params=SMALL,
        name="pack",
    )(role, *partial_sums)
    parts = lax.all_to_all(packed, "seq", 0, 0)
    steer_step, filter_step = pl.pallas_call(
        step_kernel,
        in_specs=[SMEM] + [vmem] * 3,
        out_shape=[
            jax.ShapeDtypeStruct((1, own_channels), F32),
            jax.ShapeDtypeStruct((groups // seqs, filt_len), F32),
        ],
        compiler_params=SMALL,
        name="step",
    )(role, parts, *seconds)
    return steer_step, filter_step.T[None]


def solution(mesh):
    in_specs = (
        P("seq", None),
        P("section", "seq", None),
        P("section", "seq", None),
        P("section", "seq", None),
        P("section", None, None),
        P("section", "seq"),
        P("section", None, "seq"),
    )
    out_specs = (P("section", "seq"), P("section", None, "seq"))
    return jax.shard_map(body, mesh=mesh, in_specs=in_specs, out_specs=out_specs, check_vma=False)
```
